32 devices in a mesh: section: 2 (over core), dp: 8 (over z, x), tensor: 2 (over y).
Axes of the slice: x: 2, y: 2, z: 4, core: 2. Of those that a mesh axis runs over, the one named last changes fastest.
Arguments:
- hidden: bfloat16 [2, 8, 128, 2048], P(None, 'dp', 'tensor'), may hold values from -6 to 6
- layer_inputs: bfloat16 [2, 2, 8, 128, 256], P('section', None, 'dp', 'tensor'), may hold values from -6 to 6
- span_starts: int32 [2, 8], P(None, 'dp'), may hold values from 0 to 64, as said below
- cotangent: bfloat16 [2, 8, 128, 2048], P(None, 'dp', 'tensor'), may hold values from -6 to 6
- input_gain: bfloat16 [2, 2048], P('section', 'dp'), may hold values from 0.5 to 1.5
- query_weight: bfloat16 [2, 2048, 2048], P('section', 'dp', 'tensor'), may hold values from -0.125 to 0.125
- key_projection: bfloat16 [2, 2048, 512], P('section', 'dp', 'tensor'), may hold values from -0.125 to 0.125
- value_projection: bfloat16 [2, 2048, 512], P('section', 'dp', 'tensor'), may hold values from -0.125 to 0.125
- query_gain: bfloat16 [2, 256], P('section', 'dp'), may hold values from 0.5 to 1.5
- key_norm_gain: bfloat16 [2, 256], P('section', 'dp'), may hold values from 0.5 to 1.5
- output_weight: bfloat16 [2, 2048, 2048], P('section', 'tensor', 'dp'), may hold values from -0.125 to 0.125
- attention_gain: bfloat16 [2, 2048], P('section', 'dp'), may hold values from 0.5 to 1.5
- laurel_left: bfloat16 [2, 2048, 64], P('section', 'dp'), may hold values from -0.125 to 0.125
- laurel_right: bfloat16 [2, 64, 2048], P('section', None, 'dp'), may hold values from -0.75 to 0.75
- laurel_gain: bfloat16 [2, 2048], P('section', 'dp'), may hold values from 0.5 to 1.5
- prefeed_gain: bfloat16 [2, 2048], P('section', 'dp'), may hold values from 0.5 to 1.5
- gate_weight: bfloat16 [2, 2048, 8192], P('section', 'dp', 'tensor'), may hold values from -0.125 to 0.125
- up_weight: bfloat16 [2, 2048, 8192], P('section', 'dp', 'tensor'), may hold values from -0.125 to 0.125
- down_weight: bfloat16 [2, 8192, 2048], P('section', 'tensor', 'dp'), may hold values from -0.0625 to 0.0625
- postfeed_gain: bfloat16 [2, 2048], P('section', 'dp'), may hold values from 0.5 to 1.5
- layer_gate: bfloat16 [2, 2048, 256], P('section', 'dp'), may hold values from -0.125 to 0.125
- layer_project: bfloat16 [2, 256, 2048], P('section', None, 'dp'), may hold values from -0.375 to 0.375
- layer_gain: bfloat16 [2, 2048], P('section', 'dp'), may hold values from 0.5 to 1.5
Outputs:
- activation: bfloat16 [2, 2, 8, 128, 2048], P('section', None, 'dp', 'tensor')
- input_grad: float32 [2, 2, 8, 128, 2048], P('section', None, 'dp', 'tensor')
- layer_input_grad: float32 [2, 2, 8, 128, 256], P('section', None, 'dp', 'tensor')
- grad_input_gain: float32 [2, 2048], P('section', 'dp')
- grad_query_weight: float32 [2, 2048, 2048], P('section', 'dp', 'tensor')
- grad_key_weight: float32 [2, 2048, 512], P('section', 'dp', 'tensor')
- grad_value_weight: float32 [2, 2048, 512], P('section', 'dp', 'tensor')
- grad_query_gain: float32 [2, 256], P('section', 'dp')
- grad_key_gain: float32 [2, 256], P('section', 'dp')
- grad_output_weight: float32 [2, 2048, 2048], P('section', 'tensor', 'dp')
- grad_attention_gain: float32 [2, 2048], P('section', 'dp')
- grad_laurel_left: float32 [2, 2048, 64], P('section', 'dp')
- grad_laurel_right: float32 [2, 64, 2048], P('section', None, 'dp')
- grad_laurel_gain: float32 [2, 2048], P('section', 'dp')
- grad_prefeed_gain: float32 [2, 2048], P('section', 'dp')
- grad_gate_weight: float32 [2, 2048, 8192], P('section', 'dp', 'tensor')
- grad_up_weight: float32 [2, 2048, 8192], P('section', 'dp', 'tensor')
- grad_down_weight: float32 [2, 8192, 2048], P('section', 'tensor', 'dp')
- grad_postfeed_gain: float32 [2, 2048], P('section', 'dp')
- grad_layer_gate: float32 [2, 2048, 256], P('section', 'dp')
- grad_layer_project: float32 [2, 256, 2048], P('section', None, 'dp')
- grad_layer_gain: float32 [2, 2048], P('section', 'dp')
The draws below stay inside these ranges and needn't reach their ends.
Inputs may be any that keep to these rules, and one draw needn't show every extreme that they name: `span_starts`: each sequence has one image span of 64 positions starting here.
All inputs are finite; a program needn't handle non-finite values.
Results may differ from the reference program's by a relative error of at most 0.033.
Values may be sent and summed in bfloat16 or wider, within the bound.
A program may use at most 320 MiB of HBM per device.

```python
import math
import jax
import jax.numpy as jnp
from jax import lax

MODEL_WIDTH = 2048
QUERY_HEADS = 8
KEY_VALUE_HEADS = 2
HEAD_SIZE = 256
FF = 8192
RANK = 64
PER_LAYER = 256
MICRO = 2
SEQ = 128
IMG = 64
SEQS = 8
N_SECTION = 2


def draw_span_starts(key, part):
    key = jax.random.fold_in(key, 7)
    first_key, second_key, third_key = jax.random.split(key, 3)
    total_count = MICRO * SEQS
    drawn = jax.random.randint(first_key, (total_count,), 0, SEQ - IMG + 1, dtype=jnp.int32)
    high_slot = jax.random.randint(second_key, (), 0, total_count, dtype=jnp.int32)
    low_slot = (high_slot + 1 + jax.random.randint(third_key, (), 0, total_count - 1, dtype=jnp.int32)) % total_count
    slots = jnp.arange(total_count, dtype=jnp.int32)
    drawn = jnp.where(slots == high_slot, SEQ - IMG, drawn)
    drawn = jnp.where(slots == low_slot, 0, drawn)
    return drawn.reshape(MICRO, SEQS)


def shard_levels(key, extent, shards, low, top_value):
    def one(axis_at, blocks):
        steps = jax.random.uniform(jax.random.fold_in(jax.random.fold_in(key, 6), axis_at), (blocks,), jnp.float32, low / len(shards), top_value / len(shards))
        return jnp.repeat(jnp.exp(steps), extent[axis_at] // blocks).reshape((-1,) + (1,) * (len(extent) - axis_at - 1))

    loudness = one(*shards[0])
    for cut in shards[1:]:
        loudness = loudness * one(*cut)
    return loudness


def noise(key, shape, scale, bound, cuts=(), held_as=jnp.bfloat16):
    factor_of = shard_levels(key, shape, cuts, -0.22, 0.18) if cuts else 1.0
    values = jax.random.normal(key, shape, jnp.float32) * scale * factor_of
    return jnp.minimum(jnp.maximum(values, -bound), bound).astype(held_as)


def setup_inputs(seed: int = 0) -> dict:
    splits = jax.random.split(jax.random.key(seed), 24)
    return {
        "hidden": noise(splits[0], (MICRO, SEQS, SEQ, MODEL_WIDTH), 1.0, 6.0, ((1, 8), (2, 2))),
        "layer_inputs": noise(splits[1], (N_SECTION, MICRO, SEQS, SEQ, PER_LAYER), 1.0, 6.0, ((0, 2), (2, 8), (3, 2))),
        "span_starts": draw_span_starts(jax.random.fold_in(splits[23], 71), 0),
        "cotangent": noise(splits[3], (MICRO, SEQS, SEQ, MODEL_WIDTH), 1.0, 6.0, ((1, 8), (2, 2))),
        "input_gain": jnp.clip(1.0 + 0.1 * jax.random.normal(splits[4], (N_SECTION, MODEL_WIDTH), jnp.float32), 0.5, 1.5).astype(jnp.bfloat16),
        "query_weight": noise(splits[5], (N_SECTION, MODEL_WIDTH, QUERY_HEADS * HEAD_SIZE), MODEL_WIDTH ** -0.5, 0.125, ((0, 2), (1, 8), (2, 2))),
        "key_projection": noise(splits[6], (N_SECTION, MODEL_WIDTH, KEY_VALUE_HEADS * HEAD_SIZE), MODEL_WIDTH ** -0.5, 0.125, ((0, 2), (1, 8), (2, 2))),
        "value_projection": noise(splits[7], (N_SECTION, MODEL_WIDTH, KEY_VALUE_HEADS * HEAD_SIZE), MODEL_WIDTH ** -0.5, 0.125, ((0, 2), (1, 8), (2, 2))),
        "query_gain": jnp.clip(1.0 + 0.1 * jax.random.normal(splits[8], (N_SECTION, HEAD_SIZE), jnp.float32), 0.5, 1.5).astype(jnp.bfloat16),
        "key_norm_gain": jnp.clip(1.0 + 0.1 * jax.random.normal(splits[9], (N_SECTION, HEAD_SIZE), jnp.float32), 0.5, 1.5).astype(jnp.bfloat16),
        "output_weight": noise(splits[10], (N_SECTION, QUERY_HEADS * HEAD_SIZE, MODEL_WIDTH), (QUERY_HEADS * HEAD_SIZE) ** -0.5, 0.125, ((0, 2), (1, 2), (2, 8))),
        "attention_gain": jnp.clip(1.0 + 0.1 * jax.random.normal(splits[11], (N_SECTION, MODEL_WIDTH), jnp.float32), 0.5, 1.5).astype(jnp.bfloat16),
        "laurel_left": noise(splits[12], (N_SECTION, MODEL_WIDTH, RANK), MODEL_WIDTH ** -0.5, 0.125, ((0, 2), (1, 8))),
        "laurel_right": noise(splits[13], (N_SECTION, RANK, MODEL_WIDTH), RANK ** -0.5, 0.75, ((0, 2), (2, 8))),
        "laurel_gain": jnp.clip(1.0 + 0.1 * jax.random.normal(splits[14], (N_SECTION, MODEL_WIDTH), jnp.float32), 0.5, 1.5).astype(jnp.bfloat16),
        "prefeed_gain": jnp.clip(1.0 + 0.1 * jax.random.normal(splits[15], (N_SECTION, MODEL_WIDTH), jnp.float32), 0.5, 1.5).astype(jnp.bfloat16),
        "gate_weight": noise(splits[16], (N_SECTION, MODEL_WIDTH, FF), MODEL_WIDTH ** -0.5, 0.125, ((0, 2), (1, 8), (2, 2))),
        "up_weight": noise(splits[17], (N_SECTION, MODEL_WIDTH, FF), MODEL_WIDTH ** -0.5, 0.125, ((0, 2), (1, 8), (2, 2))),
        "down_weight": noise(splits[18], (N_SECTION, FF, MODEL_WIDTH), FF ** -0.5, 0.0625, ((0, 2), (1, 2), (2, 8))),
        "postfeed_gain": jnp.clip(1.0 + 0.1 * jax.random.normal(splits[19], (N_SECTION, MODEL_WIDTH), jnp.float32), 0.5, 1.5).astype(jnp.bfloat16),
        "layer_gate": noise(splits[20], (N_SECTION, MODEL_WIDTH, PER_LAYER), MODEL_WIDTH ** -0.5, 0.125, ((0, 2), (1, 8))),
        "layer_project": noise(splits[21], (N_SECTION, PER_LAYER, MODEL_WIDTH), PER_LAYER ** -0.5, 0.375, ((0, 2), (2, 8))),
        "layer_gain": jnp.clip(1.0 + 0.1 * jax.random.normal(splits[22], (N_SECTION, MODEL_WIDTH), jnp.float32), 0.5, 1.5).astype(jnp.bfloat16),
    }


@jax.custom_vjp
def low(v):
    return lax.optimization_barrier(v.astype(jnp.bfloat16)).astype(jnp.float32)

@jax.custom_vjp
def low_back(v):
    return v

def low_keep(v):
    return (low(v), None)

def low_pass(kept, grad):
    return (grad,)

def back_keep(v):
    return (v, None)

def back_low(kept, grad):
    return (low(grad),)
low.defvjp(low_keep, low_pass)
low_back.defvjp(back_keep, back_low)
EPSILON = 1e-06
ROOT_HALF = 0.5 ** 0.5
NEG_FILL = -1e+30
WEIGHT_KEYS = ('input_gain', 'query_weight', 'key_weight', 'value_weight', 'query_gain', 'key_gain', 'output_weight', 'attention_gain', 'laurel_left', 'laurel_right', 'laurel_gain', 'prefeed_gain', 'gate_weight', 'up_weight', 'down_weight', 'postfeed_gain', 'layer_gate', 'layer_project', 'layer_gain')

def scaled_norm(values, scales):
    return values * lax.rsqrt(lax.optimization_barrier(jnp.mean(values * values, axis=-1, keepdims=True)) + EPSILON) * scales

def plain_norm(values):
    return values * lax.rsqrt(lax.optimization_barrier(jnp.mean(values * values, axis=-1, keepdims=True)) + EPSILON)

def gelu_tanh(values):
    return jax.nn.gelu(values, approximate=True)

def rope_tables(span_length, columns):
    half_width = columns // 2
    frequency = jnp.exp(jnp.arange(half_width, dtype=jnp.float32) * (-2.0 * math.log(10000.0) / columns))
    angles = jnp.arange(span_length, dtype=jnp.float32)[:, None] * frequency[None, :]
    return (jnp.cos(angles), jnp.sin(angles))

def apply_rotation(values, cosine_table, sine_values):
    half_width = values.shape[-1] // 2
    front_half = values[..., :half_width]
    back_half = values[..., half_width:]
    cosine_wide = cosine_table[:, None, :]
    sine_wide = sine_values[:, None, :]
    return jnp.concatenate([front_half * cosine_wide - back_half * sine_wide, back_half * cosine_wide + front_half * sine_wide], axis=-1)

def span_mask(span_start, span_length, span_width):
    position = jnp.arange(span_length, dtype=jnp.int32)
    inside = (position >= span_start) & (position < span_start + span_width)
    return (position[None, :] <= position[:, None]) | inside[:, None] & inside[None, :]

def matmul(operand, other):
    return jnp.einsum('...i,ij->...j', operand, other, precision=lax.Precision.HIGHEST)

def attend_one(packed):
    query_rows, key_row_block, value_row_block, span_start = packed
    span_length = query_rows.shape[0]
    grouped_heads = query_rows.reshape(span_length, KEY_VALUE_HEADS, QUERY_HEADS // KEY_VALUE_HEADS, HEAD_SIZE)
    raw_scores = low_back(jnp.einsum('sgjd,tgd->gjst', grouped_heads, key_row_block, precision=lax.Precision.HIGHEST) * HEAD_SIZE ** (-0.5))
    allowed = span_mask(span_start, span_length, IMG)
    masked = jnp.where(allowed, raw_scores, NEG_FILL)
    row_max = lax.optimization_barrier(jnp.max(masked, axis=-1, keepdims=True))
    shifted = jnp.exp(masked - row_max)
    probability = shifted / lax.optimization_barrier(jnp.sum(shifted, axis=-1, keepdims=True))
    mixture = jnp.einsum('gjst,tgd->sgjd', low(probability), value_row_block, precision=lax.Precision.HIGHEST)
    return mixture.reshape(span_length, QUERY_HEADS * HEAD_SIZE)

def layer_apply(hidden_rows, layer_values, starts, layer_weights):
    sequence_count, span_length, columns = hidden_rows.shape
    cosine_table, sine_values = rope_tables(span_length, HEAD_SIZE)
    normed = scaled_norm(hidden_rows, layer_weights['input_gain'])
    normed_low = low(normed)
    query_raw = low_back(matmul(normed_low, layer_weights['query_weight']))
    key_unnormed = low_back(matmul(normed_low, layer_weights['key_weight']))
    value_unnormed = low_back(matmul(normed_low, layer_weights['value_weight']))
    query_rows = apply_rotation(scaled_norm(query_raw.reshape(sequence_count, span_length, QUERY_HEADS, HEAD_SIZE), layer_weights['query_gain']), cosine_table, sine_values)
    key_row_block = apply_rotation(scaled_norm(key_unnormed.reshape(sequence_count, span_length, KEY_VALUE_HEADS, HEAD_SIZE), layer_weights['key_gain']), cosine_table, sine_values)
    value_row_block = plain_norm(value_unnormed.reshape(sequence_count, span_length, KEY_VALUE_HEADS, HEAD_SIZE))
    heads_out = lax.map(jax.checkpoint(attend_one), (low(query_rows), low(key_row_block), low(value_row_block), starts))
    heads_low = low_back(low(heads_out))
    attended = low_back(matmul(heads_low, layer_weights['output_weight']))
    laurel_mid = low_back(low(matmul(normed_low, layer_weights['laurel_left'])))
    laurel_raw = low_back(matmul(laurel_mid, layer_weights['laurel_right']))
    combined = (hidden_rows + scaled_norm(attended, layer_weights['attention_gain']) + normed + scaled_norm(laurel_raw, layer_weights['laurel_gain'])) * ROOT_HALF
    prefeed_low = low(scaled_norm(combined, layer_weights['prefeed_gain']))
    gate_proj = low_back(matmul(prefeed_low, layer_weights['gate_weight']))
    up_proj = low_back(matmul(prefeed_low, layer_weights['up_weight']))
    geglu_low = low(gelu_tanh(gate_proj) * up_proj)
    down_out = low_back(matmul(geglu_low, layer_weights['down_weight']))
    residual = combined + scaled_norm(down_out, layer_weights['postfeed_gain'])
    gate_raw = low_back(matmul(low(residual), layer_weights['layer_gate']))
    layer_low = low(gelu_tanh(gate_raw) * layer_values)
    projected = low_back(matmul(layer_low, layer_weights['layer_project']))
    return residual + scaled_norm(projected, layer_weights['layer_gain'])

def reference(hidden, layer_inputs, span_starts, cotangent, input_gain, query_weight, key_projection, value_projection, query_gain, key_norm_gain, output_weight, attention_gain, laurel_left, laurel_right, laurel_gain, prefeed_gain, gate_weight, up_weight, down_weight, postfeed_gain, layer_gate, layer_project, layer_gain):
    arrays = (input_gain, query_weight, key_projection, value_projection, query_gain, key_norm_gain, output_weight, attention_gain, laurel_left, laurel_right, laurel_gain, prefeed_gain, gate_weight, up_weight, down_weight, postfeed_gain, layer_gate, layer_project, layer_gain)
    layer_weights = {key_name: tensor.astype(jnp.float32) for key_name, tensor in zip(WEIGHT_KEYS, arrays)}
    hidden_rows = hidden.astype(jnp.float32).reshape(-1, SEQ, MODEL_WIDTH)
    layer_rows = layer_inputs.astype(jnp.float32)
    starts = span_starts.reshape(-1).astype(jnp.int32)
    probe_zero = jnp.zeros((N_SECTION,) + hidden_rows.shape, jnp.float32)

    def forward(layer_in, weights_in, probe_in):
        outputs = []
        current = hidden_rows
        for section_index in range(N_SECTION):
            section_weights = {key_name: tensor[section_index] for key_name, tensor in weights_in.items()}
            result = layer_apply(current + probe_in[section_index], layer_in[section_index].reshape(-1, SEQ, PER_LAYER), starts, section_weights)
            if section_index + 1 < N_SECTION:
                result = low(result)
                current = low_back(result)
            outputs.append(result)
        return tuple(outputs)
    outputs, backward = jax.vjp(forward, layer_rows, layer_weights, probe_zero)
    cotangents = [jnp.zeros_like(result_rows) for result_rows in outputs[:-1]]
    cotangents.append(cotangent.astype(jnp.float32).reshape(outputs[-1].shape))
    layer_grad, weight_grads, probe_grad = backward(tuple(cotangents))
    activation = jnp.stack(outputs).reshape(N_SECTION, MICRO, SEQS, SEQ, MODEL_WIDTH).astype(jnp.bfloat16)
    input_grad = probe_grad.reshape(N_SECTION, MICRO, SEQS, SEQ, MODEL_WIDTH)
    return (activation, input_grad, layer_grad, weight_grads['input_gain'], weight_grads['query_weight'], weight_grads['key_weight'], weight_grads['value_weight'], weight_grads['query_gain'], weight_grads['key_gain'], weight_grads['output_weight'], weight_grads['attention_gain'], weight_grads['laurel_left'], weight_grads['laurel_right'], weight_grads['laurel_gain'], weight_grads['prefeed_gain'], weight_grads['gate_weight'], weight_grads['up_weight'], weight_grads['down_weight'], weight_grads['postfeed_gain'], weight_grads['layer_gate'], weight_grads['layer_project'], weight_grads['layer_gain'])
```

```python
import math
from types import SimpleNamespace

import jax
import jax.numpy as jnp
from jax import lax
from jax.experimental import pallas as pl
from jax.experimental.pallas import tpu as pltpu
from jax.sharding import PartitionSpec as P

S, D, T = "section", "dp", "tensor"
MESH = pl.DeviceIdType.MESH
BF, F32 = jnp.bfloat16, jnp.float32
HEAD = 256
IMG = 64
EPS = 1e-06
RH = 0.5**0.5
NEG = -1e30
LANES = 128
GELU_C = math.sqrt(2.0 / math.pi)
GELU_K = 0.044715
VMEM_LIMIT = 60 << 20
HALVES = 2


def rms_of(v):
    return lax.rsqrt(jnp.mean(v * v, axis=-1, keepdims=True) + EPS)


def rms_back(v, gain, grad):
    r = rms_of(v)
    unit = v * r
    inner = grad * gain
    back = r * (inner - unit * jnp.mean(inner * unit, axis=-1, keepdims=True))
    return back, jnp.sum(grad * unit, axis=0, keepdims=True)


def plain_back(v, grad):
    r = rms_of(v)
    unit = v * r
    return r * (grad - unit * jnp.mean(grad * unit, axis=-1, keepdims=True))


def gelu(v):
    return 0.5 * v * (1.0 + jnp.tanh(GELU_C * (v + GELU_K * v * v * v)))


def gelu_both(v):
    square = v * v
    th = jnp.tanh(GELU_C * v * (1.0 + GELU_K * square))
    value = 0.5 * v * (1.0 + th)
    slope = 0.5 * (1.0 + th) + 0.5 * v * (1.0 - th * th) * GELU_C * (1.0 + 3.0 * GELU_K * square)
    return value, slope


def rotate(v, cos, sin):
    half = HEAD // 2
    front, back = v[:, :half], v[:, half:]
    return jnp.concatenate([front * cos - back * sin, back * cos + front * sin], axis=-1)


def rotate_back(g, cos, sin):
    half = HEAD // 2
    front, back = g[:, :half], g[:, half:]
    return jnp.concatenate([front * cos + back * sin, back * cos - front * sin], axis=-1)


def nn(x, w):
    return jnp.dot(x, w, preferred_element_type=F32)


def nt(x, w):
    return lax.dot_general(x, w, (((1,), (1,)), ((), ())), preferred_element_type=F32)


def tn(x, w):
    return lax.dot_general(x, w, (((0,), (0,)), ((), ())), preferred_element_type=F32)


def tiles(count, step):
    def wrap(fn):
        def one(j, carry):
            fn(pl.ds(pl.multiple_of(j * step, step), step))
            return carry

        lax.fori_loop(0, count // step, one, 0)

    return wrap


def place(n):
    s, d, t = lax.axis_index(S), lax.axis_index(D), lax.axis_index(T)
    return SimpleNamespace(s=s, d=d, t=t, a=lax.div(d, 2), b=lax.rem(d, 2), n=n, A=n // 2)


def rcopy(src, dst, send, recv, device):
    return pltpu.make_async_remote_copy(
        src_ref=src, dst_ref=dst, send_sem=send, recv_sem=recv, device_id=device, device_id_type=MESH
    )


def rows_of(index, size):
    return pl.ds(pl.multiple_of(index * size, size), size)


class Local:
    def __init__(self, sems):
        self.sems, self.used = sems, 0

    def __call__(self, src, dst):
        copy = pltpu.make_async_copy(src, dst, self.sems.at[self.used])
        self.used += 1
        copy.start()
        return copy


def greet(p, active, partner):
    barrier = pltpu.get_barrier_semaphore()

    def signal(device):
        pl.semaphore_signal(barrier, inc=1, device_id=device, device_id_type=MESH)

    if partner:
        signal((1 - p.s, p.d, p.t))

    @pl.when(active)
    def _():
        signal((p.s, p.d, 1 - p.t))
        signal((p.s, p.a * 2 + 1 - p.b, p.t))

        @pl.when(p.a > 0)
        def _():
            signal((p.s, (p.a - 1) * 2 + p.b, p.t))

        @pl.when(p.a < p.A - 1)
        def _():
            signal((p.s, (p.a + 1) * 2 + p.b, p.t))

    line = 2 + (p.a > 0).astype(jnp.int32) + (p.a < p.A - 1).astype(jnp.int32)
    pl.when(active)(lambda: pl.semaphore_wait(barrier, line + (1 if partner else 0)))
    if partner:
        pl.when(jnp.logical_not(active))(lambda: pl.semaphore_wait(barrier, 1))


def line_gather(p, buf, size, sems, cols=None):
    up_s, up_r, dn_s, dn_r, xs, xr = sems
    A = p.A
    above = (p.s, (p.a + 1) * 2 + p.b, p.t)
    below = (p.s, (p.a - 1) * 2 + p.b, p.t)
    side = (p.s, p.a * 2 + 1 - p.b, p.t)

    def at(col, row):
        return buf.at[col, rows_of(row, size)]

    def up(i, row):
        return rcopy(at(p.b, row), at(p.b, row), up_s.at[i], up_r.at[i], above)

    def down(i, row):
        return rcopy(at(p.b, row), at(p.b, row), dn_s.at[i], dn_r.at[i], below)

    def across(col, row):
        return rcopy(at(col, row), at(col, row), xs.at[row], xr.at[row], side)

    def when(cond, fn):
        pl.when(cond)(fn)

    when(p.a < A - 1, lambda: up(0, p.a).start())
    when(p.a > 0, lambda: down(0, p.a).start())
    across(p.b, p.a).start()
    for i in range(A - 1):

        @pl.when(p.a - 1 - i >= 0)
        def _():
            row = p.a - 1 - i
            up(i, row).wait_recv()
            if i + 1 < A - 1:
                when(p.a < A - 1, lambda: up(i + 1, row).start())
            across(p.b, row).start()

        @pl.when(p.a + 1 + i <= A - 1)
        def _():
            row = p.a + 1 + i
            down(i, row).wait_recv()
            if i + 1 < A - 1:
                when(p.a > 0, lambda: down(i + 1, row).start())
            across(p.b, row).start()

    def arrive():
        for row in range(A):
            across(1 - p.b, row).wait_recv()

    def finish():
        for i in range(A - 1):
            when((p.a < A - 1) & (p.a - i >= 0), lambda: up(i, p.a - i).wait_send())
            when((p.a > 0) & (p.a + i <= A - 1), lambda: down(i, p.a + i).wait_send())
        for row in range(A):
            across(p.b, row).wait_send()

    return arrive, finish


def line_scatter(p, acc, other, got, step_got, size, cuts, sems, out):
    xs, xr, us, ur, ds_, dr = sems
    A = p.A
    above = (p.s, (p.a + 1) * 2 + p.b, p.t)
    below = (p.s, (p.a - 1) * 2 + p.b, p.t)
    side = (p.s, p.a * 2 + 1 - p.b, p.t)

    def cols(h):
        return pl.ds(cuts[h][0], cuts[h][1])

    def across(h):
        return rcopy(other.at[:, cols(h)], got.at[:, cols(h)], xs.at[h], xr.at[h], side)

    def up(h, dest):
        return rcopy(
            other.at[pl.ds(dest * size, size), cols(h)],
            step_got.at[pl.ds(dest * size, size), cols(h)],
            us.at[h, dest],
            ur.at[h, dest],
            above,
        )

    def down(h, dest):
        slot = jnp.where(p.a - 1 == dest, A, dest)
        return rcopy(
            other.at[pl.ds(dest * size, size), cols(h)],
            step_got.at[rows_of(slot, size), cols(h)],
            ds_.at[h, dest],
            dr.at[h, dest],
            below,
        )

    def up_here(h, dest):
        rows = rows_of(dest, size) if not isinstance(dest, int) else pl.ds(dest * size, size)
        return rcopy(other.at[pl.ds(0, size), cols(h)], step_got.at[rows, cols(h)], us.at[h, dest], ur.at[h, dest], above)

    def down_here(h, dest, slot):
        rows = pl.ds(slot * size, size)
        return rcopy(other.at[pl.ds(0, size), cols(h)], step_got.at[rows, cols(h)], ds_.at[h, dest], dr.at[h, dest], below)

    def start(h):
        across(h).start()

    def carry(h):
        across(h).wait()
        for i in range(A - 1):
            hi, lo = A - 1 - i, i

            @pl.when(p.a < hi)
            def _():
                here = (pl.ds(hi * size, size), cols(h))
                total = acc[here] + got[here].astype(F32)
                other[here] = total.astype(BF)

                @pl.when(p.a > 0)
                def _():
                    up_here(h, hi).wait_recv()
                    other[here] = (acc[here] + got[here].astype(F32) + step_got[here].astype(F32)).astype(BF)

                up(h, hi).start()

            @pl.when(p.a > lo)
            def _():
                here = (pl.ds(lo * size, size), cols(h))
                total = acc[here] + got[here].astype(F32)
                other[here] = total.astype(BF)

                @pl.when(p.a < A - 1)
                def _():
                    down_here(h, lo, lo).wait_recv()
                    other[here] = (acc[here] + got[here].astype(F32) + step_got[here].astype(F32)).astype(BF)

                down(h, lo).start()

        mine = (rows_of(p.a, size), cols(h))
        out[:, cols(h)] = acc[mine] + got[mine].astype(F32)

        @pl.when(p.a > 0)
        def _():
            up_here(h, p.a).wait_recv()
            out[:, cols(h)] += step_got[mine].astype(F32)

        @pl.when(p.a < A - 1)
        def _():
            rcopy(
                other.at[pl.ds(0, size), cols(h)],
                step_got.at[pl.ds(A * size, size), cols(h)],
                ds_.at[h, p.a],
                dr.at[h, p.a],
                below,
            ).wait_recv()
            out[:, cols(h)] += step_got[pl.ds(A * size, size), cols(h)].astype(F32)

    def finish(h):
        for dest in range(A):
            pl.when(p.a < dest)(lambda: up(h, dest).wait_send())
            pl.when(p.a > dest)(lambda: down(h, dest).wait_send())

    return start, carry, finish


def dma(*shape):
    return pltpu.SemaphoreType.DMA(shape)


def gather_sems(A):
    return dict(gus=dma(A), gur=dma(A), gds=dma(A), gdr=dma(A), gxs=dma(A), gxr=dma(A))


def scatter_sems(A, parts):
    return dict(
        rxs=dma(parts), rxr=dma(parts), rus=dma(parts, A), rur=dma(parts, A), rds=dma(parts, A), rdr=dma(parts, A)
    )


HBM = pl.BlockSpec(memory_space=pltpu.HBM)
VM = pl.BlockSpec(memory_space=pltpu.VMEM)


def launch(kernel, cid, hbm_in, vmem_in, outs, scratch, kept=None, cost=None):
    kept = kept or {}
    names = [*hbm_in, *vmem_in]
    taken = [name for name in outs if name in kept]
    everything = names + [None] * len(taken) + [*outs, *scratch]

    def run(*refs):
        kernel(SimpleNamespace(**{k: v for k, v in zip(everything, refs) if k}))

    order = list(outs)
    results = pl.pallas_call(
        run,
        out_shape=[jax.ShapeDtypeStruct(*spec) for spec in outs.values()],
        in_specs=[HBM] * len(hbm_in) + [VM] * len(vmem_in) + [HBM] * len(taken),
        out_specs=[HBM] * len(outs),
        scratch_shapes=list(scratch.values()),
        input_output_aliases={len(names) + i: order.index(name) for i, name in enumerate(taken)},
        compiler_params=pltpu.CompilerParams(
            collective_id=cid, has_side_effects=True, vmem_limit_bytes=VMEM_LIMIT
        ),
    )(*hbm_in.values(), *vmem_in.values(), *[kept[name] for name in taken])
    return dict(zip(order, results))


def fetch_kernel(c, o):
    p = place(c.n)
    n, A, R, hb = c.n, c.n // 2, c.R, c.hb
    barrier = pltpu.get_barrier_semaphore()

    def signal(device):
        pl.semaphore_signal(barrier, inc=1, device_id=device, device_id_type=MESH)

    for k in range(1, n):
        signal((p.s, lax.rem(p.d + k, n), p.t))
    signal((p.s, p.d, 1 - p.t))
    signal((1 - p.s, p.d, p.t))
    pl.semaphore_wait(barrier, n + 1)

    @pl.when(p.s == 1)
    def _():
        pl.semaphore_wait(o.go, 1)

    above = (p.s, (p.a + 1) * 2 + p.b, p.t)
    below = (p.s, (p.a - 1) * 2 + p.b, p.t)
    side = (p.s, p.a * 2 + 1 - p.b, p.t)
    pair = (p.s, p.d, 1 - p.t)
    cuts = c.cuts
    local = Local(o.lsem)
    waits = []

    def shard(row, col):
        return rows_of(row * 2 + col, R)

    def piece(row, q, own):
        cs = pl.ds(*cuts[q])
        return o.pack.at[:, cs] if own else o.pk.at[shard(row, p.b), cs]

    def up(i, q, row):
        return rcopy(
            piece(row, q, i == 0), o.pk.at[shard(row, p.b), pl.ds(*cuts[q])], o.gus.at[i, q], o.gur.at[i, q], above
        )

    def down(i, q, row):
        return rcopy(
            piece(row, q, i == 0), o.pk.at[shard(row, p.b), pl.ds(*cuts[q])], o.gds.at[i, q], o.gdr.at[i, q], below
        )

    def across(q, row, own, col):
        return rcopy(
            o.pack.at[:, pl.ds(*cuts[q])] if own else o.pk.at[shard(row, col), pl.ds(*cuts[q])],
            o.pk.at[shard(row, col), pl.ds(*cuts[q])],
            o.gxs.at[row, q],
            o.gxr.at[row, q],
            side,
        )

    ffn = ((o.gate, o.gw), (o.up, o.uw), (o.down, o.dw))

    def block(m, source, half):
        return ffn[m][1].at[rows_of(source, R), rows_of(half, hb)]

    def trade(m, k):
        dest = lax.rem(p.d + k, n)
        return rcopy(
            ffn[m][0].at[:, rows_of(dest, hb)], block(m, p.d, p.t), o.ts.at[k, m], o.tr.at[k, m], (p.s, dest, p.t)
        )

    def came(m, k):
        source = lax.rem(p.d + n - k, n)
        return rcopy(
            ffn[m][0].at[:, rows_of(p.d, hb)], block(m, source, p.t), o.ts.at[k, m], o.tr.at[k, m], side
        )

    def share(m, k, half):
        source = lax.rem(p.d + n - k, n)
        src = ffn[m][0].at[:, rows_of(p.d, hb)] if k == 0 else block(m, source, half)
        return rcopy(src, block(m, source, half), o.ys.at[k, m], o.yr.at[k, m], pair)

    waits.append(local(o.pack, o.pk.at[shard(p.a, p.b)]))
    for m in range(3):
        waits.append(local(ffn[m][0].at[:, rows_of(p.d, hb)], block(m, p.d, p.t)))
        share(m, 0, p.t).start()
    for q in range(len(cuts)):
        pl.when(p.a < A - 1)(lambda: up(0, q, p.a).start())
        pl.when(p.a > 0)(lambda: down(0, q, p.a).start())
        across(q, p.a, True, p.b).start()
    for k in range(1, n):
        for m in range(3):
            trade(m, k).start()
    todo = [(m, k) for k in range(1, n) for m in range(3)]
    steps = [(i, q) for i in range(A - 1) for q in range(len(cuts))]
    share_each = -(-len(todo) // len(steps))
    for i, q in steps:

        @pl.when(p.a - 1 - i >= 0)
        def _():
            row = p.a - 1 - i
            up(i, q, row).wait_recv()
            if i + 1 < A - 1:
                pl.when(p.a < A - 1)(lambda: up(i + 1, q, row).start())
            across(q, row, False, p.b).start()

        @pl.when(p.a + 1 + i <= A - 1)
        def _():
            row = p.a + 1 + i
            down(i, q, row).wait_recv()
            if i + 1 < A - 1:
                pl.when(p.a > 0)(lambda: down(i + 1, q, row).start())
            across(q, row, False, p.b).start()

        for _ in range(min(share_each, len(todo))):
            m, k = todo.pop(0)
            came(m, k).wait_recv()
            share(m, k, p.t).start()
    for m, k in todo:
        came(m, k).wait_recv()
        share(m, k, p.t).start()

    @pl.when(p.s == 0)
    def _():
        pl.semaphore_signal(o.go, inc=1, device_id=(1 - p.s, p.d, p.t), device_id_type=MESH)

    for row in range(A):
        for q in range(len(cuts)):
            across(q, row, False, 1 - p.b).wait_recv()
    for k in range(n):
        for m in range(3):
            share(m, k, 1 - p.t).wait_recv()
    for i, q in steps:
        pl.when((p.a < A - 1) & (p.a - i >= 0))(lambda: up(i, q, p.a - i).wait_send())
        pl.when((p.a > 0) & (p.a + i <= A - 1))(lambda: down(i, q, p.a + i).wait_send())
    for row in range(A):
        for q in range(len(cuts)):
            across(q, row, False, p.b).wait_send()
    for k in range(n):
        for m in range(3):
            if k:
                trade(m, k).wait_send()
            share(m, k, p.t).wait_send()
    for copy in waits:
        copy.wait()
    last = local(o.pk.at[:, pl.ds(c.qkv + c.heads, LANES)], o.gcol)
    last.wait()
    o.grow_v[...] = o.gcol[...].astype(F32).T[c.rank : c.rank + 8]
    last = local(o.grow_v, o.grow)
    last.wait()


def load_weights(c, o, local):
    qn, on = c.qkv, c.heads
    got = [
        local(o.pk.at[:, pl.ds(qn + on, c.small)], o.sm_v),
        local(o.pk.at[:, pl.ds(0, qn)], o.qkv_v),
        local(o.pk.at[:, pl.ds(qn, on)], o.ot_v),
        local(o.gw, o.gw_v),
        local(o.uw, o.uw_v),
        local(o.dw, o.dw_v),
    ]
    return SimpleNamespace(sm=got[0], qkv=got[1], ot=got[2], gw=got[3], uw=got[4], dw=got[5])


def weight_scratch(c):
    return dict(
        sm_v=pltpu.VMEM((c.width, c.small), BF),
        qkv_v=pltpu.VMEM((c.width, c.qkv), BF),
        ot_v=pltpu.VMEM((c.width, c.heads), BF),
        gw_v=pltpu.VMEM((c.width, 2 * c.hb), BF),
        uw_v=pltpu.VMEM((c.width, 2 * c.hb), BF),
        dw_v=pltpu.VMEM((c.width, 2 * c.hb), BF),
    )


LL, LR, LG, LP = (0, 128), (128, 128), (256, 256), (512, 256)


def cols_of(cut):
    return (slice(None), pl.ds(*cut))


def forward_kernel(c, k, o):
    p = place(c.n)
    r, width, hb2 = c.r, c.width, 2 * c.hb
    A = p.A
    m = jnp.clip(k - p.s, 0, 1)
    active = (k - p.s >= 0) & (k - p.s <= 1)
    local = Local(o.lsem)
    pair = (p.s, p.d, 1 - p.t)

    greet(p, active, k >= 1)
    hand = k and rcopy(o.act.at[min(max(k - 1, 0), 1)], o.hid, o.hs.at[0], o.hr.at[0], (1 - p.s, p.d, p.t))
    if k >= 1:
        pl.when(p.s == 0)(hand.start)

    @pl.when(active)
    def _():
        w = load_weights(c, o, local)
        lv_copy = local(o.lin.at[m], o.lv)
        first = pltpu.make_async_copy(o.hidden.at[m], o.hid, o.fsem.at[0])

        @pl.when(p.s == 0)
        def _():
            first.start()
            first.wait()

        if k >= 1:
            pl.when(p.s == 1)(hand.wait_recv)
        mine, theirs = rows_of(p.t, r), rows_of(1 - p.t, r)
        gain = lambda i: o.gains[i : i + 1, :]

        def normed_of():
            x = o.hid[...].astype(F32)
            return x, x * rms_of(x) * gain(0)

        o.nbuf[mine, :] = normed_of()[1].astype(BF)
        send = rcopy(o.nbuf.at[mine], o.nbuf.at[mine], o.ys.at[0], o.yr.at[0], pair)
        send.start()
        w.sm.wait()
        lane = lax.broadcasted_iota(jnp.int32, (r, LANES), 1)
        mid = jnp.where(lane < c.rank, nn(o.nbuf[mine, :], o.sm_v[cols_of(LL)]), 0.0)
        o.lmid_v[...] = mid.astype(BF)
        o.lraw_v[...] = nt(o.lmid_v[...], o.sm_v[cols_of(LR)])
        w.qkv.wait()
        rcopy(o.nbuf.at[theirs], o.nbuf.at[theirs], o.ys.at[0], o.yr.at[0], pair).wait_recv()

        @tiles(c.qkv, 256)
        def _(at):
            o.qraw_v[:, at] = nn(o.nbuf[...], o.qkv_v[:, at])

        cos, sin = o.cos[...], o.sin[...]
        q_gain, k_gain = o.gains[6:7, 0:HEAD], o.gains[7:8, 0:HEAD]
        allowed = o.allowed[m] > 0.5
        kraw = o.qraw_v[:, pl.ds(c.heads, HEAD)]
        vraw = o.qraw_v[:, pl.ds(c.heads + HEAD, HEAD)]
        key = rotate(kraw * rms_of(kraw) * k_gain, cos, sin).astype(BF)
        value = (vraw * rms_of(vraw)).astype(BF)
        for h in range(c.heads // HEAD):
            at = pl.ds(h * HEAD, HEAD)
            raw = o.qraw_v[:, at]
            query = rotate(raw * rms_of(raw) * q_gain, cos, sin).astype(BF)
            scores = jnp.where(allowed, nt(query, key) * HEAD**-0.5, NEG)
            shifted = jnp.exp(scores - jnp.max(scores, axis=-1, keepdims=True))
            prob = shifted / jnp.sum(shifted, axis=-1, keepdims=True)
            o.heads_v[:, at] = nn(prob.astype(BF), value).astype(BF)
        w.ot.wait()

        @tiles(width, 256)
        def _(at):
            o.acc[0 : 2 * r, at] = nt(o.heads_v[...], o.ot_v[at, :])

        o.ysend[...] = o.acc[theirs, :].astype(BF)
        swap = rcopy(o.ysend, o.ygot, o.ys.at[1], o.yr.at[1], pair)
        swap.start()
        swap.wait()
        x, normed = normed_of()
        att = o.acc[mine, :] + o.ygot[...].astype(F32)
        o.att_v[...] = att
        lraw = o.lraw_v[...]
        comb = (x + att * rms_of(att) * gain(1) + normed + lraw * rms_of(lraw) * gain(2)) * RH
        o.comb_v[...] = comb
        o.xbuf[p.b, rows_of(p.a, r), :] = (comb * rms_of(comb) * gain(3)).astype(BF)
        send.wait_send()

        arrive, gathered = line_gather(p, o.xbuf, r, (o.gus, o.gur, o.gds, o.gdr, o.gxs, o.gxr))
        w.gw.wait()
        w.uw.wait()

        def hidden_part(col):
            @tiles(hb2, min(256, hb2))
            def _(at):
                gate = nn(o.xbuf[col], o.gw_v[:, at])
                up = nn(o.xbuf[col], o.uw_v[:, at])
                o.gate_v[col, :, at] = gate
                o.up_v[col, :, at] = up
                o.geglu_v[col, :, at] = (gelu(gate) * up).astype(BF)

        def down_part(col, dest, h):
            start, size = c.halves[h]

            @tiles(size, 256)
            def _(at):
                at = pl.ds(pl.multiple_of(start + at.start, 256), 256)
                dest[:, at] = nt(o.geglu_v[col], o.dw_v[at, :]).astype(dest.dtype)

        hidden_part(p.b)
        arrive()
        hidden_part(1 - p.b)
        w.dw.wait()
        start, carry, finish = line_scatter(
            p, o.acc, o.other, o.got, o.step_got, r, c.halves, (o.rxs, o.rxr, o.rus, o.rur, o.rds, o.rdr), o.down_v
        )
        for h in range(HALVES):
            down_part(1 - p.b, o.other, h)
            start(h)
        for h in range(HALVES):
            down_part(p.b, o.acc, h)
        for h in range(HALVES):
            carry(h)
        down = o.down_v[...]
        resid = o.comb_v[...] + down * rms_of(down) * gain(4)
        o.resid_v[...] = resid
        graw = nn(resid.astype(BF), o.sm_v[cols_of(LG)])
        o.graw_v[...] = graw
        lv_copy.wait()
        o.llow_v[...] = (gelu(graw) * o.lv[...].astype(F32)).astype(BF)
        proj = nt(o.llow_v[...], o.sm_v[cols_of(LP)])
        o.proj_v[...] = proj
        o.act_v[...] = (o.resid_v[...] + proj * rms_of(proj) * gain(5)).astype(BF)
        out = [
            local(o.hid, o.xlow.at[m]),
            local(o.nbuf, o.nfull.at[m]),
            local(o.qraw_v, o.qraw.at[m]),
            local(o.heads_v, o.heads.at[m]),
            local(o.att_v, o.att.at[m]),
            local(o.lmid_v, o.lmid.at[m]),
            local(o.lraw_v, o.lraw.at[m]),
            local(o.comb_v, o.comb.at[m]),
            local(o.xbuf, o.pfull.at[m]),
            local(o.gate_v, o.gate.at[m]),
            local(o.up_v, o.up.at[m]),
            local(o.geglu_v, o.geglu.at[m]),
            local(o.down_v, o.down.at[m]),
            local(o.resid_v, o.resid.at[m]),
            local(o.graw_v, o.graw.at[m]),
            local(o.llow_v, o.llow.at[m]),
            local(o.proj_v, o.proj.at[m]),
            local(o.act_v, o.act.at[m]),
        ]
        gathered()
        for h in range(HALVES):
            finish(h)
        for copy in out:
            copy.wait()

    if k >= 1:
        pl.when(p.s == 0)(hand.wait_send)


def stash_shapes(c):
    m, r, w, q = 2, c.r, c.width, 2 * c.r
    ar, hb2 = c.n // 2 * c.r, 2 * c.hb
    return dict(
        act=((m, r, w), BF),
        xlow=((m, r, w), BF),
        nfull=((m, q, w), BF),
        qraw=((m, q, c.qkv), F32),
        heads=((m, q, c.heads), BF),
        att=((m, r, w), F32),
        lmid=((m, r, LANES), BF),
        lraw=((m, r, w), F32),
        comb=((m, r, w), F32),
        pfull=((m, 2, ar, w), BF),
        gate=((m, 2, ar, hb2), F32),
        up=((m, 2, ar, hb2), F32),
        geglu=((m, 2, ar, hb2), BF),
        down=((m, r, w), F32),
        resid=((m, r, w), F32),
        graw=((m, r, c.per), F32),
        llow=((m, r, c.per), BF),
        proj=((m, r, w), F32),
    )


def scratch_of(shapes):
    return {name + chr(95) + chr(118): pltpu.VMEM(shape[1:], kind) for name, (shape, kind) in shapes.items()}


def line_scratch(c):
    ar = c.n // 2 * c.r
    return dict(
        xbuf=pltpu.VMEM((2, ar, c.width), BF),
        acc=pltpu.VMEM((ar, c.width), F32),
        other=pltpu.VMEM((ar, c.width), BF),
        got=pltpu.VMEM((ar, c.width), BF),
        step_got=pltpu.VMEM((ar + c.r, c.width), BF),
        ysend=pltpu.VMEM((c.r, c.width), BF),
        ygot=pltpu.VMEM((c.r, c.width), BF),
        lsem=dma(40),
        fsem=dma(1),
        hs=dma(1),
        hr=dma(1),
        ys=dma(2),
        yr=dma(2),
        **gather_sems(c.n // 2),
        **scatter_sems(c.n // 2, HALVES),
    )


def forward_tick(c, k, weights, data, tables, stash):
    shapes = stash_shapes(c)
    own = {name: shapes[name] for name in shapes if name not in ("xlow", "nfull", "pfull")}
    scratch = dict(
        hid=pltpu.VMEM((c.r, c.width), BF),
        nbuf=pltpu.VMEM((2 * c.r, c.width), BF),
        lv=pltpu.VMEM((c.r, c.per), BF),
        **scratch_of(own),
        **weight_scratch(c),
        **line_scratch(c),
    )
    return launch(
        lambda o: forward_kernel(c, k, o),
        k,
        dict(**weights, hidden=data.hidden, lin=data.lin),
        tables,
        shapes,
        scratch,
        stash,
    )


def backward_kernel(c, k, o):
    p = place(c.n)
    r, width, hb2 = c.r, c.width, 2 * c.hb
    A = p.A
    m = jnp.clip(2 - k - p.s, 0, 1)
    active = (2 - k - p.s >= 0) & (2 - k - p.s <= 1)
    local = Local(o.lsem)
    pair = (p.s, p.d, 1 - p.t)

    greet(p, active, k >= 1)
    hand = k and rcopy(o.ilow.at[min(max(2 - k, 0), 1)], o.hid, o.hs.at[0], o.hr.at[0], (1 - p.s, p.d, p.t))
    if k >= 1:
        pl.when(p.s == 1)(hand.start)

    @pl.when(active)
    def _():
        mine, theirs = rows_of(p.t, r), rows_of(1 - p.t, r)
        gain = lambda i: o.gains[i : i + 1, :]
        first = pltpu.make_async_copy(o.cot.at[m], o.hid, o.fsem.at[0])
        pl.when(p.s == 1)(first.start)
        need = {}
        need[0] = [local(o.proj.at[m], o.proj_v), local(o.graw.at[m], o.graw_v), local(o.lin.at[m], o.lv)]
        need[1] = [local(o.down.at[m], o.down_v)]
        w = load_weights(c, o, local)
        need[2] = [local(o.gate.at[m], o.gate_v), local(o.up.at[m], o.up_v)]
        need[3] = [local(o.comb.at[m], o.comb_v), local(o.att.at[m], o.att_v), local(o.lraw.at[m], o.lraw_v)]
        need[4] = [local(o.xlow.at[m], o.xlow_v), local(o.qraw.at[m], o.qraw_v)]

        def have(i):
            for copy in need[i]:
                copy.wait()

        pl.when(p.s == 1)(first.wait)
        if k >= 1:
            pl.when(p.s == 0)(hand.wait_recv)
        have(0)
        o.ggr_v[...] = jnp.zeros_like(o.ggr_v)
        dres = o.hid[...].astype(F32)
        dproj, o.ggr_v[5:6, :] = rms_back(o.proj_v[...], gain(5), dres)
        o.plow_v[...] = dproj.astype(BF)
        w.sm.wait()
        dmid = nn(o.plow_v[...], o.sm_v[cols_of(LP)])
        value, slope = gelu_both(o.graw_v[...])
        o.lgrad_v[...] = value * dmid
        o.grlow_v[...] = (dmid * o.lv[...].astype(F32) * slope).astype(BF)
        dres = o.hid[...].astype(F32) + nt(o.grlow_v[...], o.sm_v[cols_of(LG)])
        o.dcomb_v[...] = dres
        have(1)
        ddown, o.ggr_v[4:5, :] = rms_back(o.down_v[...], gain(4), dres)
        o.xbuf[p.b, rows_of(p.a, r), :] = ddown.astype(BF)
        arrive, gathered = line_gather(p, o.xbuf, r, (o.gus, o.gur, o.gds, o.gdr, o.gxs, o.gxr))
        w.dw.wait()
        have(2)

        def hidden_part(col):
            @tiles(hb2, min(256, hb2))
            def _(at):
                dgeglu = nn(o.xbuf[col], o.dw_v[:, at])
                value, slope = gelu_both(o.gate_v[col, :, at])
                o.dul_v[col, :, at] = (dgeglu * value).astype(BF)
                o.dgl_v[col, :, at] = (dgeglu * o.up_v[col, :, at] * slope).astype(BF)

        def down_part(col, dest, h):
            start, size = c.halves[h]

            @tiles(size, 256)
            def _(at):
                at = pl.ds(pl.multiple_of(start + at.start, 256), 256)
                part = nt(o.dgl_v[col], o.gw_v[at, :]) + nt(o.dul_v[col], o.uw_v[at, :])
                dest[:, at] = part.astype(dest.dtype)

        hidden_part(p.b)
        arrive()
        hidden_part(1 - p.b)
        w.gw.wait()
        w.uw.wait()
        start, carry, finish = line_scatter(
            p, o.acc, o.other, o.got, o.step_got, r, c.halves, (o.rxs, o.rxr, o.rus, o.rur, o.rds, o.rdr), o.down_v
        )
        for h in range(HALVES):
            down_part(1 - p.b, o.other, h)
            start(h)
        for h in range(HALVES):
            down_part(p.b, o.acc, h)
        for h in range(HALVES):
            carry(h)
        have(3)
        dcomb, o.ggr_v[3:4, :] = rms_back(o.comb_v[...], gain(3), o.down_v[...])
        even = (o.dcomb_v[...] + dcomb) * RH
        o.dcomb_v[...] = even
        datt, o.ggr_v[1:2, :] = rms_back(o.att_v[...], gain(1), even)
        o.abuf[mine, :] = datt.astype(BF)
        send = rcopy(o.abuf.at[mine], o.abuf.at[mine], o.ys.at[0], o.yr.at[0], pair)
        send.start()
        dlraw, o.ggr_v[2:3, :] = rms_back(o.lraw_v[...], gain(2), o.dcomb_v[...])
        o.lrlow_v[...] = dlraw.astype(BF)
        o.lmg_v[...] = nn(o.lrlow_v[...], o.sm_v[cols_of(LR)]).astype(BF)
        o.proj_v[...] = o.dcomb_v[...] + nt(o.lmg_v[...], o.sm_v[cols_of(LL)])
        w.ot.wait()
        rcopy(o.abuf.at[theirs], o.abuf.at[theirs], o.ys.at[0], o.yr.at[0], pair).wait_recv()

        @tiles(c.heads, 256)
        def _(at):
            o.hgrad_v[:, at] = nn(o.abuf[...], o.ot_v[:, at]).astype(BF)

        have(4)
        cos, sin = o.cos[...], o.sin[...]
        q_gain, k_gain = o.gains[6:7, 0:HEAD], o.gains[7:8, 0:HEAD]
        allowed = o.allowed[m] > 0.5
        k_at, v_at = pl.ds(c.heads, HEAD), pl.ds(c.heads + HEAD, HEAD)
        kraw, vraw = o.qraw_v[:, k_at], o.qraw_v[:, v_at]
        key = rotate(kraw * rms_of(kraw) * k_gain, cos, sin).astype(BF)
        value = (vraw * rms_of(vraw)).astype(BF)
        dkey = jnp.zeros(kraw.shape, F32)
        dvalue = jnp.zeros(vraw.shape, F32)
        dq_gain = jnp.zeros((1, HEAD), F32)
        for h in range(c.heads // HEAD):
            at = pl.ds(h * HEAD, HEAD)
            raw = o.qraw_v[:, at]
            query = rotate(raw * rms_of(raw) * q_gain, cos, sin).astype(BF)
            scores = jnp.where(allowed, nt(query, key) * HEAD**-0.5, NEG)
            shifted = jnp.exp(scores - jnp.max(scores, axis=-1, keepdims=True))
            prob = shifted / jnp.sum(shifted, axis=-1, keepdims=True)
            hgrad = o.hgrad_v[:, at]
            dprob = nt(hgrad, value)
            dvalue = dvalue + tn(prob.astype(BF), hgrad)
            inner = jnp.sum(prob * dprob, axis=-1, keepdims=True)
            dscore = (prob * (dprob - inner)).astype(BF)
            dquery = nn(dscore, key) * HEAD**-0.5
            dkey = dkey + tn(dscore, query) * HEAD**-0.5
            draw, dg = rms_back(raw, q_gain, rotate_back(dquery, cos, sin))
            dq_gain = dq_gain + dg
            o.dqkv_v[:, at] = draw.astype(BF)
        draw, dk_gain = rms_back(kraw, k_gain, rotate_back(dkey, cos, sin))
        o.dqkv_v[:, k_at] = draw.astype(BF)
        o.dqkv_v[:, v_at] = plain_back(vraw, dvalue).astype(BF)
        o.ggr_v[6:7, 0:HEAD] = dq_gain
        o.ggr_v[7:8, 0:HEAD] = dk_gain
        w.qkv.wait()

        @tiles(width, 256)
        def _(at):
            o.acc[0 : 2 * r, at] = nt(o.dqkv_v[...], o.qkv_v[at, :])

        o.ysend[...] = o.acc[theirs, :].astype(BF)
        swap = rcopy(o.ysend, o.ygot, o.ys.at[1], o.yr.at[1], pair)
        swap.start()
        swap.wait()
        dnorm = o.proj_v[...] + o.acc[mine, :] + o.ygot[...].astype(F32)
        dx, o.ggr_v[0:1, :] = rms_back(o.xlow_v[...].astype(F32), gain(0), dnorm)
        dx = dx + o.dcomb_v[...]
        o.igrad_v[...] = dx
        o.ilow_v[...] = dx.astype(BF)
        send.wait_send()
        out = [
            local(o.igrad_v, o.igrad.at[m]),
            local(o.ilow_v, o.ilow.at[m]),
            local(o.lgrad_v, o.lgrad.at[m]),
            local(o.plow_v, o.plow.at[m]),
            local(o.grlow_v, o.grlow.at[m]),
            local(o.xbuf, o.dfull.at[m]),
            local(o.dgl_v, o.dgl.at[m]),
            local(o.dul_v, o.dul.at[m]),
            local(o.lrlow_v, o.lrlow.at[m]),
            local(o.lmg_v, o.lmg.at[m]),
            local(o.abuf, o.afull.at[m]),
            local(o.dqkv_v, o.dqkv.at[m]),
            local(o.ggr_v, o.ggr.at[m]),
        ]
        gathered()
        for h in range(HALVES):
            finish(h)
        for copy in out:
            copy.wait()

    if k >= 1:
        pl.when(p.s == 1)(hand.wait_send)


def grad_shapes(c):
    m, r, w, q = 2, c.r, c.width, 2 * c.r
    ar, hb2 = c.n // 2 * c.r, 2 * c.hb
    return dict(
        igrad=((m, r, w), F32),
        ilow=((m, r, w), BF),
        lgrad=((m, r, c.per), F32),
        plow=((m, r, w), BF),
        grlow=((m, r, c.per), BF),
        dfull=((m, 2, ar, w), BF),
        dgl=((m, 2, ar, hb2), BF),
        dul=((m, 2, ar, hb2), BF),
        lrlow=((m, r, w), BF),
        lmg=((m, r, LANES), BF),
        afull=((m, q, w), BF),
        dqkv=((m, q, c.qkv), BF),
        ggr=((m, 8, w), F32),
    )


READ = ("proj", "graw", "down", "gate", "up", "comb", "att", "lraw", "xlow", "qraw")


def backward_tick(c, k, weights, data, tables, stash, grads):
    shapes = grad_shapes(c)
    kept_shapes = stash_shapes(c)
    own = {name: shapes[name] for name in shapes if name not in ("dfull", "afull")}
    scratch = dict(
        hid=pltpu.VMEM((c.r, c.width), BF),
        abuf=pltpu.VMEM((2 * c.r, c.width), BF),
        lv=pltpu.VMEM((c.r, c.per), BF),
        dcomb_v=pltpu.VMEM((c.r, c.width), F32),
        hgrad_v=pltpu.VMEM((2 * c.r, c.heads), BF),
        **scratch_of(own),
        **scratch_of({name: kept_shapes[name] for name in READ}),
        **weight_scratch(c),
        **line_scratch(c),
    )
    return launch(
        lambda o: backward_kernel(c, k, o),
        3 + k,
        dict(**weights, cot=data.cot, lin=data.lin, **{name: stash[name] for name in READ}),
        tables,
        shapes,
        scratch,
        grads,
    )


def return_kernel(c, o):
    p = place(c.n)
    n, A, R, hb = c.n, c.n // 2, c.R, c.hb
    pair = (p.s, p.d, 1 - p.t)
    side = (p.s, p.a * 2 + 1 - p.b, p.t)
    barrier = pltpu.get_barrier_semaphore()

    def signal(device):
        pl.semaphore_signal(barrier, inc=1, device_id=device, device_id_type=MESH)

    for k in range(1, n):
        signal((p.s, lax.rem(p.d + k, n), p.t))
    signal(pair)
    pl.semaphore_wait(barrier, n)
    local = Local(o.lsem)
    ffn = (o.dg, o.du, o.dd)

    def swap(m, k):
        dest = lax.rem(p.d + k, n)
        return rcopy(
            ffn[m].at[rows_of(dest, R), rows_of(1 - p.t, hb)],
            o.fgot.at[m, rows_of(dest, R)],
            o.ys.at[m, k],
            o.yr.at[m, k],
            pair,
        )

    def trade(m, k):
        dest = lax.rem(p.d + k, n)
        return rcopy(
            o.fown.at[m, rows_of(dest, R)], o.gf.at[m, :, rows_of(p.d, hb)], o.ts.at[m, k], o.tr.at[m, k], (p.s, dest, p.t)
        )

    def came(m, k):
        source = lax.rem(p.d + n - k, n)
        return rcopy(
            o.fown.at[m, rows_of(p.d, R)], o.gf.at[m, :, rows_of(source, hb)], o.ts.at[m, k], o.tr.at[m, k], side
        )

    attn = (o.dqkv, o.dot, o.dsm)
    loads = []
    for row in range(A):
        for q, part in enumerate(attn):
            cs = pl.ds(*c.parts[q])
            loads.append(local(part.at[rows_of(row * 2 + 1 - p.b, R)], o.other.at[pl.ds(row * R, R), cs]))
            loads.append(local(part.at[rows_of(row * 2 + p.b, R)], o.acc.at[pl.ds(row * R, R), cs]))
    owns = [local(ffn[m].at[:, rows_of(p.t, hb)], o.fown.at[m]) for m in range(3)]
    for m in range(3):
        for k in [*range(1, n), 0]:
            swap(m, k).start()
    for copy in loads:
        copy.wait()
    start, carry, finish = line_scatter(
        p, o.acc, o.other, o.got, o.step_got, R, c.parts, (o.rxs, o.rxr, o.rus, o.rur, o.rds, o.rdr), o.gp_v
    )
    for q in range(len(c.parts)):
        start(q)
    mine_copies = []
    for q in range(max(len(c.parts), 3)):
        if q < 3:
            owns[q].wait()
            for k in [*range(1, n), 0]:
                rows = rows_of(lax.rem(p.d + k, n), R)
                swap(q, k).wait_recv()
                total = o.fown[q, rows, :].astype(F32) + o.fgot[q, rows, :].astype(F32)
                o.fown[q, rows, :] = total.astype(BF)
                if k:
                    trade(q, k).start()
                else:
                    mine_copies.append(local(o.fown.at[q, rows], o.gf.at[q, :, rows_of(p.d, hb)]))
        if q < len(c.parts):
            carry(q)
    shared = pl.ds(c.qkv + c.heads, c.small)
    o.ssend[...] = o.gp_v[:, shared].astype(BF)
    last = rcopy(o.ssend, o.sgot, o.ss.at[0], o.sr.at[0], pair)
    last.start()
    last.wait()
    o.gp_v[:, shared] += o.sgot[...].astype(F32)
    out = local(o.gp_v, o.gp)
    for m in range(3):
        for k in range(n):
            swap(m, k).wait_send()
            if k:
                came(m, k).wait_recv()
                trade(m, k).wait_send()
    for q in range(len(c.parts)):
        finish(q)
    for copy in [*mine_copies, out]:
        copy.wait()


def fetch_weights(c, pack, gate, up, down):
    n, A, q = c.n, c.n // 2, len(c.cuts)
    outs = dict(
        pk=((c.width, c.total), BF),
        gw=((c.width, 2 * c.hb), BF),
        uw=((c.width, 2 * c.hb), BF),
        dw=((c.width, 2 * c.hb), BF),
        grow=((8, c.width), F32),
    )
    scratch = dict(
        gcol=pltpu.VMEM((c.width, LANES), BF),
        grow_v=pltpu.VMEM((8, c.width), F32),
        gus=dma(A, q), gur=dma(A, q), gds=dma(A, q), gdr=dma(A, q), gxs=dma(A, q), gxr=dma(A, q),
        ts=dma(n, 3), tr=dma(n, 3), ys=dma(n, 3), yr=dma(n, 3), lsem=dma(6),
        go=pltpu.SemaphoreType.REGULAR,
    )
    return launch(
        lambda o: fetch_kernel(c, o), 6, dict(pack=pack, gate=gate, up=up, down=down), {}, outs, scratch
    )


def return_grads(c, dqkv, dot, dsm, dg, du, dd):
    n, A = c.n, c.n // 2
    R = c.R
    outs = dict(gp=((R, c.total), F32), gf=((3, R, n * c.hb), BF))
    scratch = dict(
        acc=pltpu.VMEM((A * R, c.total), BF),
        other=pltpu.VMEM((A * R, c.total), BF),
        got=pltpu.VMEM((A * R, c.total), BF),
        step_got=pltpu.VMEM((A * R + R, c.total), BF),
        gp_v=pltpu.VMEM((R, c.total), F32),
        fown=pltpu.VMEM((3, c.width, c.hb), BF),
        fgot=pltpu.VMEM((3, c.width, c.hb), BF),
        ssend=pltpu.VMEM((R, c.small), BF),
        sgot=pltpu.VMEM((R, c.small), BF),
        ys=dma(3, n), yr=dma(3, n), ts=dma(3, n), tr=dma(3, n), ss=dma(1), sr=dma(1), lsem=dma(6 * A + 8),
        **scatter_sems(A, len(c.parts)),
    )
    return launch(lambda o: return_kernel(c, o), 7, dict(dqkv=dqkv, dot=dot, dsm=dsm, dg=dg, du=du, dd=dd), {}, outs, scratch)


def spread(gain, n, rows):
    return jnp.pad(gain, (0, rows - gain.shape[0]))


def body(
    hidden, layer_inputs, span_starts, cotangent, input_gain, query_weight, key_projection, value_projection,
    query_gain, key_norm_gain, output_weight, attention_gain, laurel_left, laurel_right, laurel_gain, prefeed_gain,
    gate_weight, up_weight, down_weight, postfeed_gain, layer_gate, layer_project, layer_gain,
):
    n, nt_ = lax.axis_size(D), lax.axis_size(T)
    t = lax.axis_index(T)
    rank = laurel_left.shape[2]
    width = hidden.shape[3]
    R = width // n
    heads = query_weight.shape[2]
    qkv = heads + 2 * HEAD
    per = layer_gate.shape[2]
    small = 2 * LANES + 2 * per
    c = SimpleNamespace(
        n=n, R=R, r=hidden.shape[2], width=width, heads=heads, qkv=qkv, per=per, small=small, rank=rank,
        total=qkv + heads + small, hb=gate_weight.shape[2] // n,
        cuts=((0, qkv), (qkv, heads), (qkv + heads, small)),
        parts=((0, qkv), (qkv, heads), (qkv + heads, small)),
        halves=tuple((h * width // HALVES, width // HALVES) for h in range(HALVES)),
    )
    gains = jnp.stack(
        [
            input_gain[0], attention_gain[0], laurel_gain[0], prefeed_gain[0], postfeed_gain[0], layer_gain[0],
            spread(query_gain[0], n, R), spread(key_norm_gain[0], n, R),
        ],
        axis=1,
    )
    pad = lambda v, k: jnp.pad(v, ((0, 0), (0, LANES - k)))
    pack = jnp.concatenate(
        [
            query_weight[0], key_projection[0], value_projection[0], output_weight[0].T,
            pad(jnp.concatenate([laurel_left[0], gains], axis=1), rank + 8), pad(laurel_right[0].T, rank),
            layer_gate[0], layer_project[0].T,
        ],
        axis=1,
    )
    weights = fetch_weights(c, pack, gate_weight[0], up_weight[0], down_weight[0].T)
    columns = weights.pop("grow")
    short = HEAD // n
    head_gains = columns[6:].reshape(2, n, R)[:, :, :short].reshape(2, HEAD)
    gain_rows = jnp.concatenate([columns[:6], jnp.pad(head_gains, ((0, 0), (0, width - HEAD)))], axis=0)

    span = c.r * nt_
    position = jnp.arange(span, dtype=jnp.int32)
    begin = span_starts[:, 0][:, None]
    inside = (position[None] >= begin) & (position[None] < begin + IMG)
    allowed = (position[None, :] <= position[:, None])[None] | (inside[:, :, None] & inside[:, None, :])
    half = HEAD // 2
    frequency = jnp.exp(jnp.arange(half, dtype=F32) * (-2.0 * math.log(10000.0) / HEAD))
    angles = jnp.arange(span, dtype=F32)[:, None] * frequency[None, :]
    tables = dict(gains=gain_rows, cos=jnp.cos(angles), sin=jnp.sin(angles), allowed=allowed.astype(F32))
    data = SimpleNamespace(hidden=hidden[:, 0], lin=layer_inputs[0, :, 0], cot=cotangent[:, 0])

    stash, grads = None, None
    for k in range(3):
        stash = forward_tick(c, k, weights, data, tables, stash)
    for k in range(3):
        grads = backward_tick(c, k, weights, data, tables, stash, grads)
    f, g = SimpleNamespace(**stash), SimpleNamespace(**grads)

    def pair_grad(inputs, outs):
        inputs = inputs.reshape(-1, inputs.shape[-1])
        return tn(inputs, outs.reshape(-1, outs.shape[-1])).astype(BF)

    nlow = lax.dynamic_slice_in_dim(f.nfull, t * c.r, c.r, axis=1)
    sums = g.ggr[0] + g.ggr[1]
    head_sums = jnp.pad(sums[6:, :HEAD].reshape(2, n, short), ((0, 0), (0, 0), (0, R - short))).reshape(2, width)
    gain_cols = jnp.concatenate([sums[:6], head_sums], axis=0).T.astype(BF)
    left = pair_grad(nlow, g.lmg)
    left = jnp.concatenate([left[:, :rank], gain_cols, left[:, rank + 8 :]], axis=1)
    dsm = jnp.concatenate(
        [left, pair_grad(g.lrlow, f.lmid), pair_grad(f.resid.astype(BF), g.grlow), pair_grad(g.plow, f.llow)], axis=1
    )
    done = return_grads(
        c, pair_grad(f.nfull, g.dqkv), pair_grad(g.afull, f.heads), dsm,
        pair_grad(f.pfull, g.dgl), pair_grad(f.pfull, g.dul), pair_grad(g.dfull, f.geglu),
    )
    gp, gf = done["gp"], done["gf"].astype(F32)
    base = qkv + heads
    gain_out = gp[:, base + rank : base + rank + 8].T
    one = lambda i: gain_out[i][None]
    return (
        f.act[None, :, None],
        g.igrad[None, :, None],
        g.lgrad[None, :, None],
        one(0),
        gp[:, :heads][None],
        gp[:, heads : heads + HEAD][None],
        gp[:, heads + HEAD : qkv][None],
        gain_out[6, :short][None],
        gain_out[7, :short][None],
        gp[:, qkv:base].T[None],
        one(1),
        gp[:, base : base + rank][None],
        gp[:, base + LANES : base + LANES + rank].T[None],
        one(2),
        one(3),
        gf[0][None],
        gf[1][None],
        gf[2].T[None],
        one(4),
        gp[:, base + 2 * LANES : base + 2 * LANES + per][None],
        gp[:, base + 2 * LANES + per :].T[None],
        one(5),
    )


def solution(mesh):
    rows, cols = P(S, D, T), P(S, T, D)
    vec, tall, flat = P(S, D), P(S, D, None), P(S, None, D)
    seq, out = P(None, D, T, None), P(S, None, D, T, None)
    weights = (
        vec, rows, rows, rows, vec, vec, cols, vec, tall, flat, vec, vec, rows, rows, cols, vec, tall, flat, vec,
    )
    return jax.shard_map(
        body,
        mesh=mesh,
        in_specs=(seq, out, P(None, D), seq, *weights),
        out_specs=(out, out, out, *weights),
        check_vma=False,
    )
```

```python
import math
from types import SimpleNamespace

import jax
import jax.numpy as jnp
from jax import lax
from jax.experimental import pallas as pl
from jax.experimental.pallas import tpu as pltpu
from jax.sharding import PartitionSpec as P

S, D, T = "section", "dp", "tensor"
MESH = pl.DeviceIdType.MESH
BF, F32 = jnp.bfloat16, jnp.float32
HEAD = 256
IMG = 64
EPS = 1e-06
RH = 0.5**0.5
NEG = -1e30
LANES = 128
GELU_C = math.sqrt(2.0 / math.pi)
GELU_K = 0.044715
VMEM_LIMIT = 60 << 20
HALVES = 2
GATHER_PARTS = 2


def rms_of(v):
    return lax.rsqrt(jnp.mean(v * v, axis=-1, keepdims=True) + EPS)


def rms_back(v, gain, grad):
    r = rms_of(v)
    unit = v * r
    inner = grad * gain
    back = r * (inner - unit * jnp.mean(inner * unit, axis=-1, keepdims=True))
    return back, jnp.sum(grad * unit, axis=0, keepdims=True)


def plain_back(v, grad):
    r = rms_of(v)
    unit = v * r
    return r * (grad - unit * jnp.mean(grad * unit, axis=-1, keepdims=True))


def gelu(v):
    return 0.5 * v * (1.0 + jnp.tanh(GELU_C * (v + GELU_K * v * v * v)))


def gelu_both(v):
    square = v * v
    th = jnp.tanh(GELU_C * v * (1.0 + GELU_K * square))
    value = 0.5 * v * (1.0 + th)
    slope = 0.5 * (1.0 + th) + 0.5 * v * (1.0 - th * th) * GELU_C * (1.0 + 3.0 * GELU_K * square)
    return value, slope


def rotate(v, cos, sin):
    half = HEAD // 2
    front, back = v[:, :half], v[:, half:]
    return jnp.concatenate([front * cos - back * sin, back * cos + front * sin], axis=-1)


def rotate_back(g, cos, sin):
    half = HEAD // 2
    front, back = g[:, :half], g[:, half:]
    return jnp.concatenate([front * cos + back * sin, back * cos - front * sin], axis=-1)


def nn(x, w):
    return jnp.dot(x, w, preferred_element_type=F32)


def nt(x, w):
    return lax.dot_general(x, w, (((1,), (1,)), ((), ())), preferred_element_type=F32)


def tn(x, w):
    return lax.dot_general(x, w, (((0,), (0,)), ((), ())), preferred_element_type=F32)


def tiles(count, step):
    def wrap(fn):
        def one(j, carry):
            fn(pl.ds(pl.multiple_of(j * step, step), step))
            return carry

        lax.fori_loop(0, count // step, one, 0)

    return wrap


def place(n):
    s, d, t = lax.axis_index(S), lax.axis_index(D), lax.axis_index(T)
    return SimpleNamespace(s=s, d=d, t=t, a=lax.div(d, 2), b=lax.rem(d, 2), n=n, A=n // 2)


def rcopy(src, dst, send, recv, device):
    return pltpu.make_async_remote_copy(
        src_ref=src, dst_ref=dst, send_sem=send, recv_sem=recv, device_id=device, device_id_type=MESH
    )


def rows_of(index, size):
    return pl.ds(pl.multiple_of(index * size, size), size)


class Local:
    def __init__(self, sems):
        self.sems, self.used = sems, 0

    def __call__(self, src, dst):
        copy = pltpu.make_async_copy(src, dst, self.sems.at[self.used])
        self.used += 1
        copy.start()
        return copy


def greet(p, active, partner):
    barrier = pltpu.get_barrier_semaphore()

    def signal(device):
        pl.semaphore_signal(barrier, inc=1, device_id=device, device_id_type=MESH)

    if partner:
        signal((1 - p.s, p.d, p.t))

    @pl.when(active)
    def _():
        signal((p.s, p.d, 1 - p.t))
        signal((p.s, p.a * 2 + 1 - p.b, p.t))

        steps_of(p, lambda row: signal((p.s, row * 2 + p.b, p.t)))

    line = 2 + p.A - 1
    pl.when(active)(lambda: pl.semaphore_wait(barrier, line + (1 if partner else 0)))
    if partner:
        pl.when(jnp.logical_not(active))(lambda: pl.semaphore_wait(barrier, 1))


def steps_of(p, fn, far_first=False):
    for delta in range(p.A - 1, 0, -1) if far_first else range(1, p.A):
        pl.when(p.a - delta >= 0)(lambda: fn(p.a - delta))
        pl.when(p.a + delta < p.A)(lambda: fn(p.a + delta))


def line_gather(p, buf, size, sems):
    zs, zr, xs, xr = sems
    side = (p.s, p.a * 2 + 1 - p.b, p.t)
    part = size // GATHER_PARTS

    def at(col, row, g):
        return buf.at[col, pl.ds(pl.multiple_of(row * size + g * part, part), part)]

    def along(row, g):
        return rcopy(at(p.b, p.a, g), at(p.b, p.a, g), zs.at[row, g], zr.at[p.a, g], (p.s, row * 2 + p.b, p.t))

    def came(row, g):
        return rcopy(at(p.b, row, g), at(p.b, row, g), zs.at[row, g], zr.at[row, g], side)

    def across(col, row, g):
        return rcopy(at(col, row, g), at(col, row, g), xs.at[row, g], xr.at[row, g], side)

    def each(fn):
        def run(row):
            for g in range(GATHER_PARTS):
                fn(row, g)

        return run

    for g in range(GATHER_PARTS):
        steps_of(p, lambda row: along(row, g).start(), True)
        across(p.b, p.a, g).start()

    def forward(row, g):
        came(row, g).wait_recv()
        across(p.b, row, g).start()

    steps_of(p, each(forward))

    def arrive():
        for row in range(p.A):
            each(lambda row, g: across(1 - p.b, row, g).wait_recv())(row)

    def finish():
        steps_of(p, each(lambda row, g: along(row, g).wait_send()))
        for row in range(p.A):
            each(lambda row, g: across(p.b, row, g).wait_send())(row)

    return arrive, finish


def line_scatter(p, acc, other, got, step_got, size, cuts, sems, out):
    xs, xr, zs, zr = sems
    side = (p.s, p.a * 2 + 1 - p.b, p.t)

    def part(row, h):
        return (rows_of(row, size), pl.ds(cuts[h][0], cuts[h][1]))

    def across(h, row):
        at = part(row, h)
        return rcopy(other.at[at], got.at[at], xs.at[h, row], xr.at[h, row], side)

    def along(h, row):
        return rcopy(
            other.at[part(row, h)], step_got.at[part(p.a, h)], zs.at[h, row], zr.at[h, p.a], (p.s, row * 2 + p.b, p.t)
        )

    def came(h, row):
        return rcopy(other.at[part(row, h)], step_got.at[part(row, h)], zs.at[h, row], zr.at[h, row], side)

    def start(h):
        steps_of(p, lambda row: across(h, row).start(), True)
        across(h, p.a).start()

    def carry(h):
        def pass_on(row):
            at = part(row, h)
            across(h, row).wait()
            other[at] = (acc[at] + got[at].astype(F32)).astype(BF)
            along(h, row).start()

        steps_of(p, pass_on, True)

    def collect(h):
        across(h, p.a).wait()
        at = part(p.a, h)
        cols = (slice(None), at[1])
        out[cols] = acc[at] + got[at].astype(F32)

        def add(row):
            came(h, row).wait_recv()
            out[cols] += step_got[part(row, h)].astype(F32)

        steps_of(p, add)

    def finish(h):
        steps_of(p, lambda row: along(h, row).wait_send())

    return start, carry, collect, finish


def lowest(mask, n):
    bit = 0
    while (1 << bit) < n and not mask >> bit & 1:
        bit += 1
    return bit


def flip(d, mask):
    bit = 0
    result = d
    while 1 << bit <= mask:
        if mask >> bit & 1:
            result = result + (1 - 2 * lax.rem(lax.div(d, 1 << bit), 2)) * (1 << bit)
        bit += 1
    return result


def cube_scatter(p, acc, got, size, cuts, sems, out):
    send, recv = sems
    n = p.n

    def cols(h):
        return pl.ds(cuts[h][0], cuts[h][1])

    def block(mask):
        return rows_of(flip(p.d, mask), size)

    def message(h, mask):
        bit = lowest(mask, n)
        return rcopy(
            acc.at[block(mask), cols(h)],
            got.at[pl.ds((mask - 1) * size, size), cols(h)],
            send.at[h, mask],
            recv.at[h, mask],
            (p.s, flip(p.d, 1 << bit), p.t),
        )

    def stage(h, bit):
        for mask in range(1, n):
            if lowest(mask, n) == bit:
                at = (block(mask), cols(h))
                total = None
                for below in range(bit):
                    came = mask | 1 << below
                    message(h, came).wait_recv()
                    term = got[pl.ds((came - 1) * size, size), cols(h)].astype(F32)
                    total = term if total is None else total + term
                if total is not None:
                    acc[at] = (acc[at].astype(F32) + total).astype(BF)
                message(h, mask).start()

    def last(h):
        total = acc[block(0), cols(h)].astype(F32)
        for below in range(lowest(0, n)):
            message(h, 1 << below).wait_recv()
            total = total + got[pl.ds(((1 << below) - 1) * size, size), cols(h)].astype(F32)
        out[:, cols(h)] = total

    def finish(h):
        for mask in range(1, n):
            message(h, mask).wait_send()

    return stage, last, finish


def dma(*shape):
    return pltpu.SemaphoreType.DMA(shape)


def gather_sems(A):
    g = GATHER_PARTS
    return dict(gzs=dma(A, g), gzr=dma(A, g), gxs=dma(A, g), gxr=dma(A, g))


def scatter_sems(A, parts):
    return dict(rxs=dma(parts, A), rxr=dma(parts, A), rzs=dma(parts, A), rzr=dma(parts, A))


HBM = pl.BlockSpec(memory_space=pltpu.HBM)
VM = pl.BlockSpec(memory_space=pltpu.VMEM)


def launch(kernel, cid, hbm_in, vmem_in, outs, scratch, kept=None, cost=None):
    kept = kept or {}
    names = [*hbm_in, *vmem_in]
    taken = [name for name in outs if name in kept]
    everything = names + [None] * len(taken) + [*outs, *scratch]

    def run(*refs):
        kernel(SimpleNamespace(**{k: v for k, v in zip(everything, refs) if k}))

    order = list(outs)
    results = pl.pallas_call(
        run,
        out_shape=[jax.ShapeDtypeStruct(*spec) for spec in outs.values()],
        in_specs=[HBM] * len(hbm_in) + [VM] * len(vmem_in) + [HBM] * len(taken),
        out_specs=[HBM] * len(outs),
        scratch_shapes=list(scratch.values()),
        input_output_aliases={len(names) + i: order.index(name) for i, name in enumerate(taken)},
        compiler_params=pltpu.CompilerParams(
            collective_id=cid, has_side_effects=cid is not None, vmem_limit_bytes=VMEM_LIMIT
        ),
    )(*hbm_in.values(), *vmem_in.values(), *[kept[name] for name in taken])
    return dict(zip(order, results))


def fetch_kernel(c, o):
    p = place(c.n)
    n, A, R, hb = c.n, c.n // 2, c.R, c.hb
    barrier = pltpu.get_barrier_semaphore()

    def signal(device):
        pl.semaphore_signal(barrier, inc=1, device_id=device, device_id_type=MESH)

    for k in range(1, n):
        signal((p.s, lax.rem(p.d + k, n), p.t))
    signal((p.s, p.d, 1 - p.t))
    signal((1 - p.s, p.d, p.t))
    pl.semaphore_wait(barrier, n + 1)

    @pl.when(p.s == 1)
    def _():
        pl.semaphore_wait(o.go, 1)

    side = (p.s, p.a * 2 + 1 - p.b, p.t)
    pair = (p.s, p.d, 1 - p.t)
    cuts = c.cuts
    bits = lowest(0, n)
    local = Local(o.lsem)
    waits = []

    def give(mask, bit, q):
        rows, cs = rows_of(flip(p.d, mask), R), pl.ds(*cuts[q])
        src = o.pk.at[rows, cs] if mask else o.pack.at[:, cs]
        far = mask | 1 << bit
        return rcopy(src, o.pk.at[rows, cs], o.gs.at[far, q], o.gr.at[far, q], (p.s, flip(p.d, 1 << bit), p.t))

    def taken(mask, q):
        at = (rows_of(flip(p.d, mask), R), pl.ds(*cuts[q]))
        return rcopy(o.pk.at[at], o.pk.at[at], o.gs.at[mask, q], o.gr.at[mask, q], side)

    def pass_on(mask, q):
        if mask:
            taken(mask, q).wait_recv()
        for bit in reversed(range(lowest(mask, n))):
            give(mask, bit, q).start()

    ffn = ((o.gate, o.gw), (o.up, o.uw), (o.down, o.dw))

    def block(m, source, half):
        return ffn[m][1].at[rows_of(source, R), rows_of(half, hb)]

    def trade(m, k):
        dest = lax.rem(p.d + k, n)
        return rcopy(
            ffn[m][0].at[:, rows_of(dest, hb)], block(m, p.d, p.t), o.ts.at[k, m], o.tr.at[k, m], (p.s, dest, p.t)
        )

    def came(m, k):
        source = lax.rem(p.d + n - k, n)
        return rcopy(
            ffn[m][0].at[:, rows_of(p.d, hb)], block(m, source, p.t), o.ts.at[k, m], o.tr.at[k, m], side
        )

    def share(m, k, half):
        source = lax.rem(p.d + n - k, n)
        src = ffn[m][0].at[:, rows_of(p.d, hb)] if k == 0 else block(m, source, half)
        return rcopy(src, block(m, source, half), o.ys.at[k, m], o.yr.at[k, m], pair)

    bounce = [local(o.pack, o.pack_v)]
    for m in range(3):
        bounce.append(local(ffn[m][0].at[:, rows_of(p.d, hb)], o.block_v.at[m]))
    events = []
    inner = sorted((mask for mask in range(2, n, 2)), key=lambda mask: (-lowest(mask, n), mask))
    for q in range(len(cuts)):
        events.append((0.0 + 0.1 * q, lambda q=q: pass_on(0, q)))
        for i, mask in enumerate(inner):
            events.append((c.ag[0] + c.ag[1] * q + c.ag[2] * i, lambda q=q, mask=mask: pass_on(mask, q)))
    for k in range(n):
        for m in range(3):
            at = m * n + k if c.by_matrix else k * 3 + m
            if k:
                events.append((c.tr[0] + c.tr[1] * at, lambda m=m, k=k: trade(m, k).start()))
                events.append((c.tr[2] + c.tr[3] * at, lambda m=m, k=k: (came(m, k).wait_recv(), share(m, k, p.t).start())))
            else:
                events.append((c.tr[0] + c.tr[1] * at, lambda m=m: share(m, 0, p.t).start()))
    for _, run in sorted(events, key=lambda e: e[0]):
        run()
    for copy in bounce:
        copy.wait()
    waits.append(local(o.pack_v, o.pk.at[rows_of(p.d, R)]))
    for m in range(3):
        waits.append(local(o.block_v.at[m], block(m, p.d, p.t)))

    @pl.when(p.s == 0)
    def _():
        pl.semaphore_signal(o.go, inc=1, device_id=(1 - p.s, p.d, p.t), device_id_type=MESH)

    for q in range(len(cuts)):
        for mask in range(1, n, 2):
            taken(mask, q).wait_recv()
    for k in range(n):
        for m in range(3):
            share(m, k, 1 - p.t).wait_recv()
    for q in range(len(cuts)):
        for mask in range(0, n, 2):
            for bit in range(lowest(mask, n)):
                give(mask, bit, q).wait_send()
    for k in range(n):
        for m in range(3):
            if k:
                trade(m, k).wait_send()
            share(m, k, p.t).wait_send()
    for copy in waits:
        copy.wait()
    last = local(o.pk.at[:, pl.ds(c.qkv + c.heads, LANES)], o.gcol)
    last.wait()
    o.grow_v[...] = o.gcol[...].astype(F32).T[c.rank : c.rank + 8]
    last = local(o.grow_v, o.grow)
    last.wait()


def load_weights(c, o, local):
    qn, on = c.qkv, c.heads
    got = [
        local(o.pk.at[:, pl.ds(qn + on, c.small)], o.sm_v),
        local(o.pk.at[:, pl.ds(0, qn)], o.qkv_v),
        local(o.pk.at[:, pl.ds(qn, on)], o.ot_v),
        local(o.gw, o.gw_v),
        local(o.uw, o.uw_v),
        local(o.dw, o.dw_v),
    ]
    return SimpleNamespace(sm=got[0], qkv=got[1], ot=got[2], gw=got[3], uw=got[4], dw=got[5])


def weight_scratch(c):
    return dict(
        sm_v=pltpu.VMEM((c.width, c.small), BF),
        qkv_v=pltpu.VMEM((c.width, c.qkv), BF),
        ot_v=pltpu.VMEM((c.width, c.heads), BF),
        gw_v=pltpu.VMEM((c.width, 2 * c.hb), BF),
        uw_v=pltpu.VMEM((c.width, 2 * c.hb), BF),
        dw_v=pltpu.VMEM((c.width, 2 * c.hb), BF),
    )


LL, LR, LG, LP = (0, 128), (128, 128), (256, 256), (512, 256)


def cols_of(cut):
    return (slice(None), pl.ds(*cut))


def forward_kernel(c, k, o):
    p = place(c.n)
    r, width, hb2 = c.r, c.width, 2 * c.hb
    A = p.A
    m = jnp.clip(k - p.s, 0, 1)
    active = (k - p.s >= 0) & (k - p.s <= 1)
    local = Local(o.lsem)
    pair = (p.s, p.d, 1 - p.t)

    greet(p, active, k >= 1)
    hand = k and rcopy(o.act.at[min(max(k - 1, 0), 1)], o.hid, o.hs.at[0], o.hr.at[0], (1 - p.s, p.d, p.t))
    if k >= 1:
        pl.when(p.s == 0)(hand.start)

    @pl.when(active)
    def _():
        w = load_weights(c, o, local)
        lv_copy = local(o.lin.at[m], o.lv)
        first = pltpu.make_async_copy(o.hidden.at[m], o.hid, o.fsem.at[0])

        @pl.when(p.s == 0)
        def _():
            first.start()
            first.wait()

        if k >= 1:
            pl.when(p.s == 1)(hand.wait_recv)
        mine, theirs = rows_of(p.t, r), rows_of(1 - p.t, r)
        gain = lambda i: o.gains[i : i + 1, :]

        def normed_of():
            x = o.hid[...].astype(F32)
            return x, x * rms_of(x) * gain(0)

        o.nbuf[mine, :] = normed_of()[1].astype(BF)
        send = rcopy(o.nbuf.at[mine], o.nbuf.at[mine], o.ys.at[0], o.yr.at[0], pair)
        send.start()
        w.sm.wait()
        lane = lax.broadcasted_iota(jnp.int32, (r, LANES), 1)
        mid = jnp.where(lane < c.rank, nn(o.nbuf[mine, :], o.sm_v[cols_of(LL)]), 0.0)
        o.lmid_v[...] = mid.astype(BF)
        o.lraw_v[...] = nt(o.lmid_v[...], o.sm_v[cols_of(LR)])
        w.qkv.wait()
        rcopy(o.nbuf.at[theirs], o.nbuf.at[theirs], o.ys.at[0], o.yr.at[0], pair).wait_recv()

        @tiles(c.qkv, 256)
        def _(at):
            o.qraw_v[:, at] = nn(o.nbuf[...], o.qkv_v[:, at])

        cos, sin = o.cos[...], o.sin[...]
        q_gain, k_gain = o.gains[6:7, 0:HEAD], o.gains[7:8, 0:HEAD]
        allowed = o.allowed[m] > 0.5
        kraw = o.qraw_v[:, pl.ds(c.heads, HEAD)]
        vraw = o.qraw_v[:, pl.ds(c.heads + HEAD, HEAD)]
        key = rotate(kraw * rms_of(kraw) * k_gain, cos, sin).astype(BF)
        value = (vraw * rms_of(vraw)).astype(BF)
        for h in range(c.heads // HEAD):
            at = pl.ds(h * HEAD, HEAD)
            raw = o.qraw_v[:, at]
            query = rotate(raw * rms_of(raw) * q_gain, cos, sin).astype(BF)
            scores = jnp.where(allowed, nt(query, key) * HEAD**-0.5, NEG)
            shifted = jnp.exp(scores - jnp.max(scores, axis=-1, keepdims=True))
            prob = shifted / jnp.sum(shifted, axis=-1, keepdims=True)
            o.heads_v[:, at] = nn(prob.astype(BF), value).astype(BF)
        w.ot.wait()

        @tiles(width, 256)
        def _(at):
            o.acc[0 : 2 * r, at] = nt(o.heads_v[...], o.ot_v[at, :])

        o.ysend[...] = o.acc[theirs, :].astype(BF)
        swap = rcopy(o.ysend, o.ygot, o.ys.at[1], o.yr.at[1], pair)
        swap.start()
        swap.wait()
        x, normed = normed_of()
        att = o.acc[mine, :] + o.ygot[...].astype(F32)
        o.att_v[...] = att
        lraw = o.lraw_v[...]
        comb = (x + att * rms_of(att) * gain(1) + normed + lraw * rms_of(lraw) * gain(2)) * RH
        o.comb_v[...] = comb
        o.xbuf[p.b, rows_of(p.a, r), :] = (comb * rms_of(comb) * gain(3)).astype(BF)
        send.wait_send()

        arrive, gathered = line_gather(p, o.xbuf, r, (o.gzs, o.gzr, o.gxs, o.gxr))
        w.gw.wait()
        w.uw.wait()

        def hidden_part(col):
            @tiles(hb2, min(256, hb2))
            def _(at):
                gate = nn(o.xbuf[col], o.gw_v[:, at])
                up = nn(o.xbuf[col], o.uw_v[:, at])
                o.gate_v[col, :, at] = gate
                o.up_v[col, :, at] = up
                o.geglu_v[col, :, at] = (gelu(gate) * up).astype(BF)

        def down_part(col, dest, h):
            start, size = c.halves[h]

            @tiles(size, 256)
            def _(at):
                at = pl.ds(pl.multiple_of(start + at.start, 256), 256)
                dest[:, at] = nt(o.geglu_v[col], o.dw_v[at, :]).astype(dest.dtype)

        hidden_part(p.b)
        arrive()
        hidden_part(1 - p.b)
        w.dw.wait()
        start, carry, collect, finish = line_scatter(
            p, o.acc, o.other, o.got, o.step_got, r, c.halves, (o.rxs, o.rxr, o.rzs, o.rzr), o.down_v
        )
        for h in range(HALVES):
            down_part(1 - p.b, o.other, h)
            start(h)
        for h in range(HALVES):
            down_part(p.b, o.acc, h)
            carry(h)
        for h in range(HALVES):
            collect(h)
        down = o.down_v[...]
        resid = o.comb_v[...] + down * rms_of(down) * gain(4)
        o.resid_v[...] = resid
        graw = nn(resid.astype(BF), o.sm_v[cols_of(LG)])
        o.graw_v[...] = graw
        lv_copy.wait()
        o.llow_v[...] = (gelu(graw) * o.lv[...].astype(F32)).astype(BF)
        proj = nt(o.llow_v[...], o.sm_v[cols_of(LP)])
        o.proj_v[...] = proj
        o.act_v[...] = (o.resid_v[...] + proj * rms_of(proj) * gain(5)).astype(BF)
        out = [
            local(o.hid, o.xlow.at[m]),
            local(o.nbuf, o.nfull.at[m]),
            local(o.qraw_v, o.qraw.at[m]),
            local(o.heads_v, o.heads.at[m]),
            local(o.att_v, o.att.at[m]),
            local(o.lmid_v, o.lmid.at[m]),
            local(o.lraw_v, o.lraw.at[m]),
            local(o.comb_v, o.comb.at[m]),
            local(o.xbuf, o.pfull.at[m]),
            local(o.gate_v, o.gate.at[m]),
            local(o.up_v, o.up.at[m]),
            local(o.geglu_v, o.geglu.at[m]),
            local(o.down_v, o.down.at[m]),
            local(o.resid_v, o.resid.at[m]),
            local(o.graw_v, o.graw.at[m]),
            local(o.llow_v, o.llow.at[m]),
            local(o.proj_v, o.proj.at[m]),
            local(o.act_v, o.act.at[m]),
        ]
        gathered()
        for h in range(HALVES):
            finish(h)
        for copy in out:
            copy.wait()

    if k >= 1:
        pl.when(p.s == 0)(hand.wait_send)


def stash_shapes(c):
    m, r, w, q = 2, c.r, c.width, 2 * c.r
    ar, hb2 = c.n // 2 * c.r, 2 * c.hb
    return dict(
        act=((m, r, w), BF),
        xlow=((m, r, w), BF),
        nfull=((m, q, w), BF),
        qraw=((m, q, c.qkv), F32),
        heads=((m, q, c.heads), BF),
        att=((m, r, w), F32),
        lmid=((m, r, LANES), BF),
        lraw=((m, r, w), F32),
        comb=((m, r, w), F32),
        pfull=((m, 2, ar, w), BF),
        gate=((m, 2, ar, hb2), F32),
        up=((m, 2, ar, hb2), F32),
        geglu=((m, 2, ar, hb2), BF),
        down=((m, r, w), F32),
        resid=((m, r, w), F32),
        graw=((m, r, c.per), F32),
        llow=((m, r, c.per), BF),
        proj=((m, r, w), F32),
    )


TAIL = "_v"


def scratch_of(shapes):
    return {name + TAIL: pltpu.VMEM(shape[1:], kind) for name, (shape, kind) in shapes.items()}


def line_scratch(c):
    ar = c.n // 2 * c.r
    return dict(
        xbuf=pltpu.VMEM((2, ar, c.width), BF),
        acc=pltpu.VMEM((ar, c.width), F32),
        other=pltpu.VMEM((ar, c.width), BF),
        got=pltpu.VMEM((ar, c.width), BF),
        step_got=pltpu.VMEM((ar, c.width), BF),
        ysend=pltpu.VMEM((c.r, c.width), BF),
        ygot=pltpu.VMEM((c.r, c.width), BF),
        lsem=dma(40),
        fsem=dma(1),
        hs=dma(1),
        hr=dma(1),
        ys=dma(2),
        yr=dma(2),
        **gather_sems(c.n // 2),
        **scatter_sems(c.n // 2, HALVES),
    )


def forward_tick(c, k, weights, data, tables, stash):
    shapes = stash_shapes(c)
    own = {name: shapes[name] for name in shapes if name not in ("xlow", "nfull", "pfull")}
    scratch = dict(
        hid=pltpu.VMEM((c.r, c.width), BF),
        nbuf=pltpu.VMEM((2 * c.r, c.width), BF),
        lv=pltpu.VMEM((c.r, c.per), BF),
        **scratch_of(own),
        **weight_scratch(c),
        **line_scratch(c),
    )
    return launch(
        lambda o: forward_kernel(c, k, o),
        k,
        dict(**weights, hidden=data.hidden, lin=data.lin),
        tables,
        shapes,
        scratch,
        stash,
    )


def backward_kernel(c, k, o):
    p = place(c.n)
    r, width, hb2 = c.r, c.width, 2 * c.hb
    A = p.A
    m = jnp.clip(2 - k - p.s, 0, 1)
    active = (2 - k - p.s >= 0) & (2 - k - p.s <= 1)
    local = Local(o.lsem)
    pair = (p.s, p.d, 1 - p.t)

    greet(p, active, k >= 1)
    hand = k and rcopy(o.ilow.at[min(max(2 - k, 0), 1)], o.hid, o.hs.at[0], o.hr.at[0], (1 - p.s, p.d, p.t))
    if k >= 1:
        pl.when(p.s == 1)(hand.start)

    @pl.when(active)
    def _():
        mine, theirs = rows_of(p.t, r), rows_of(1 - p.t, r)
        gain = lambda i: o.gains[i : i + 1, :]
        first = pltpu.make_async_copy(o.cot.at[m], o.hid, o.fsem.at[0])
        pl.when(p.s == 1)(first.start)
        need = {}
        need[0] = [local(o.proj.at[m], o.proj_v), local(o.graw.at[m], o.graw_v), local(o.lin.at[m], o.lv)]
        need[1] = [local(o.down.at[m], o.down_v)]
        w = load_weights(c, o, local)
        need[2] = [local(o.gate.at[m], o.gate_v), local(o.up.at[m], o.up_v)]
        need[3] = [local(o.comb.at[m], o.comb_v), local(o.att.at[m], o.att_v), local(o.lraw.at[m], o.lraw_v)]
        need[4] = [local(o.xlow.at[m], o.xlow_v), local(o.qraw.at[m], o.qraw_v)]

        def have(i):
            for copy in need[i]:
                copy.wait()

        pl.when(p.s == 1)(first.wait)
        if k >= 1:
            pl.when(p.s == 0)(hand.wait_recv)
        have(0)
        o.ggr_v[...] = jnp.zeros_like(o.ggr_v)
        dres = o.hid[...].astype(F32)
        dproj, o.ggr_v[5:6, :] = rms_back(o.proj_v[...], gain(5), dres)
        o.plow_v[...] = dproj.astype(BF)
        w.sm.wait()
        dmid = nn(o.plow_v[...], o.sm_v[cols_of(LP)])
        value, slope = gelu_both(o.graw_v[...])
        o.lgrad_v[...] = value * dmid
        o.grlow_v[...] = (dmid * o.lv[...].astype(F32) * slope).astype(BF)
        dres = o.hid[...].astype(F32) + nt(o.grlow_v[...], o.sm_v[cols_of(LG)])
        o.dcomb_v[...] = dres
        have(1)
        ddown, o.ggr_v[4:5, :] = rms_back(o.down_v[...], gain(4), dres)
        o.xbuf[p.b, rows_of(p.a, r), :] = ddown.astype(BF)
        arrive, gathered = line_gather(p, o.xbuf, r, (o.gzs, o.gzr, o.gxs, o.gxr))
        w.dw.wait()
        have(2)

        def hidden_part(col):
            @tiles(hb2, min(256, hb2))
            def _(at):
                dgeglu = nn(o.xbuf[col], o.dw_v[:, at])
                value, slope = gelu_both(o.gate_v[col, :, at])
                o.dul_v[col, :, at] = (dgeglu * value).astype(BF)
                o.dgl_v[col, :, at] = (dgeglu * o.up_v[col, :, at] * slope).astype(BF)

        def down_part(col, dest, h):
            start, size = c.halves[h]

            @tiles(size, 256)
            def _(at):
                at = pl.ds(pl.multiple_of(start + at.start, 256), 256)
                part = nt(o.dgl_v[col], o.gw_v[at, :]) + nt(o.dul_v[col], o.uw_v[at, :])
                dest[:, at] = part.astype(dest.dtype)

        hidden_part(p.b)
        arrive()
        hidden_part(1 - p.b)
        w.gw.wait()
        w.uw.wait()
        start, carry, collect, finish = line_scatter(
            p, o.acc, o.other, o.got, o.step_got, r, c.halves, (o.rxs, o.rxr, o.rzs, o.rzr), o.down_v
        )
        for h in range(HALVES):
            down_part(1 - p.b, o.other, h)
            start(h)
        for h in range(HALVES):
            down_part(p.b, o.acc, h)
            carry(h)
        for h in range(HALVES):
            collect(h)
        have(3)
        dcomb, o.ggr_v[3:4, :] = rms_back(o.comb_v[...], gain(3), o.down_v[...])
        even = (o.dcomb_v[...] + dcomb) * RH
        o.dcomb_v[...] = even
        datt, o.ggr_v[1:2, :] = rms_back(o.att_v[...], gain(1), even)
        o.abuf[mine, :] = datt.astype(BF)
        send = rcopy(o.abuf.at[mine], o.abuf.at[mine], o.ys.at[0], o.yr.at[0], pair)
        send.start()
        dlraw, o.ggr_v[2:3, :] = rms_back(o.lraw_v[...], gain(2), o.dcomb_v[...])
        o.lrlow_v[...] = dlraw.astype(BF)
        o.lmg_v[...] = nn(o.lrlow_v[...], o.sm_v[cols_of(LR)]).astype(BF)
        o.proj_v[...] = o.dcomb_v[...] + nt(o.lmg_v[...], o.sm_v[cols_of(LL)])
        w.ot.wait()
        rcopy(o.abuf.at[theirs], o.abuf.at[theirs], o.ys.at[0], o.yr.at[0], pair).wait_recv()

        @tiles(c.heads, 256)
        def _(at):
            o.hgrad_v[:, at] = nn(o.abuf[...], o.ot_v[:, at]).astype(BF)

        have(4)
        cos, sin = o.cos[...], o.sin[...]
        q_gain, k_gain = o.gains[6:7, 0:HEAD], o.gains[7:8, 0:HEAD]
        allowed = o.allowed[m] > 0.5
        k_at, v_at = pl.ds(c.heads, HEAD), pl.ds(c.heads + HEAD, HEAD)
        kraw, vraw = o.qraw_v[:, k_at], o.qraw_v[:, v_at]
        key = rotate(kraw * rms_of(kraw) * k_gain, cos, sin).astype(BF)
        value = (vraw * rms_of(vraw)).astype(BF)
        dkey = jnp.zeros(kraw.shape, F32)
        dvalue = jnp.zeros(vraw.shape, F32)
        dq_gain = jnp.zeros((1, HEAD), F32)
        for h in range(c.heads // HEAD):
            at = pl.ds(h * HEAD, HEAD)
            raw = o.qraw_v[:, at]
            query = rotate(raw * rms_of(raw) * q_gain, cos, sin).astype(BF)
            scores = jnp.where(allowed, nt(query, key) * HEAD**-0.5, NEG)
            shifted = jnp.exp(scores - jnp.max(scores, axis=-1, keepdims=True))
            prob = shifted / jnp.sum(shifted, axis=-1, keepdims=True)
            hgrad = o.hgrad_v[:, at]
            dprob = nt(hgrad, value)
            dvalue = dvalue + tn(prob.astype(BF), hgrad)
            inner = jnp.sum(prob * dprob, axis=-1, keepdims=True)
            dscore = (prob * (dprob - inner)).astype(BF)
            dquery = nn(dscore, key) * HEAD**-0.5
            dkey = dkey + tn(dscore, query) * HEAD**-0.5
            draw, dg = rms_back(raw, q_gain, rotate_back(dquery, cos, sin))
            dq_gain = dq_gain + dg
            o.dqkv_v[:, at] = draw.astype(BF)
        draw, dk_gain = rms_back(kraw, k_gain, rotate_back(dkey, cos, sin))
        o.dqkv_v[:, k_at] = draw.astype(BF)
        o.dqkv_v[:, v_at] = plain_back(vraw, dvalue).astype(BF)
        o.ggr_v[6:7, 0:HEAD] = dq_gain
        o.ggr_v[7:8, 0:HEAD] = dk_gain
        w.qkv.wait()

        @tiles(width, 256)
        def _(at):
            o.acc[0 : 2 * r, at] = nt(o.dqkv_v[...], o.qkv_v[at, :])

        o.ysend[...] = o.acc[theirs, :].astype(BF)
        swap = rcopy(o.ysend, o.ygot, o.ys.at[1], o.yr.at[1], pair)
        swap.start()
        swap.wait()
        dnorm = o.proj_v[...] + o.acc[mine, :] + o.ygot[...].astype(F32)
        dx, o.ggr_v[0:1, :] = rms_back(o.xlow_v[...].astype(F32), gain(0), dnorm)
        dx = dx + o.dcomb_v[...]
        o.igrad_v[...] = dx
        o.ilow_v[...] = dx.astype(BF)
        send.wait_send()
        out = [
            local(o.igrad_v, o.igrad.at[m]),
            local(o.ilow_v, o.ilow.at[m]),
            local(o.lgrad_v, o.lgrad.at[m]),
            local(o.plow_v, o.plow.at[m]),
            local(o.grlow_v, o.grlow.at[m]),
            local(o.xbuf, o.dfull.at[m]),
            local(o.dgl_v, o.dgl.at[m]),
            local(o.dul_v, o.dul.at[m]),
            local(o.lrlow_v, o.lrlow.at[m]),
            local(o.lmg_v, o.lmg.at[m]),
            local(o.abuf, o.afull.at[m]),
            local(o.dqkv_v, o.dqkv.at[m]),
            local(o.ggr_v, o.ggr.at[m]),
        ]
        gathered()
        for h in range(HALVES):
            finish(h)
        for copy in out:
            copy.wait()

    if k >= 1:
        pl.when(p.s == 1)(hand.wait_send)


def grad_shapes(c):
    m, r, w, q = 2, c.r, c.width, 2 * c.r
    ar, hb2 = c.n // 2 * c.r, 2 * c.hb
    return dict(
        igrad=((m, r, w), F32),
        ilow=((m, r, w), BF),
        lgrad=((m, r, c.per), F32),
        plow=((m, r, w), BF),
        grlow=((m, r, c.per), BF),
        dfull=((m, 2, ar, w), BF),
        dgl=((m, 2, ar, hb2), BF),
        dul=((m, 2, ar, hb2), BF),
        lrlow=((m, r, w), BF),
        lmg=((m, r, LANES), BF),
        afull=((m, q, w), BF),
        dqkv=((m, q, c.qkv), BF),
        ggr=((m, 8, w), F32),
    )


READ = ("proj", "graw", "down", "gate", "up", "comb", "att", "lraw", "xlow", "qraw")


def backward_tick(c, k, weights, data, tables, stash, grads):
    shapes = grad_shapes(c)
    kept_shapes = stash_shapes(c)
    own = {name: shapes[name] for name in shapes if name not in ("dfull", "afull")}
    scratch = dict(
        hid=pltpu.VMEM((c.r, c.width), BF),
        abuf=pltpu.VMEM((2 * c.r, c.width), BF),
        lv=pltpu.VMEM((c.r, c.per), BF),
        dcomb_v=pltpu.VMEM((c.r, c.width), F32),
        hgrad_v=pltpu.VMEM((2 * c.r, c.heads), BF),
        **scratch_of(own),
        **scratch_of({name: kept_shapes[name] for name in READ}),
        **weight_scratch(c),
        **line_scratch(c),
    )
    return launch(
        lambda o: backward_kernel(c, k, o),
        3 + k,
        dict(**weights, cot=data.cot, lin=data.lin, **{name: stash[name] for name in READ}),
        tables,
        shapes,
        scratch,
        grads,
    )


def return_kernel(c, o):
    p = place(c.n)
    n, A, R, hb = c.n, c.n // 2, c.R, c.hb
    pair = (p.s, p.d, 1 - p.t)
    side = (p.s, p.a * 2 + 1 - p.b, p.t)
    barrier = pltpu.get_barrier_semaphore()

    def signal(device):
        pl.semaphore_signal(barrier, inc=1, device_id=device, device_id_type=MESH)

    for k in range(1, n):
        signal((p.s, lax.rem(p.d + k, n), p.t))
    signal(pair)
    pl.semaphore_wait(barrier, n)
    local = Local(o.lsem)
    ffn = (o.dg, o.du, o.dd)

    def swap(m, k):
        dest = lax.rem(p.d + k, n)
        return rcopy(
            ffn[m].at[rows_of(dest, R), rows_of(1 - p.t, hb)],
            o.fgot.at[m, rows_of(dest, R)],
            o.ys.at[m, k],
            o.yr.at[m, k],
            pair,
        )

    def ffn_out(m, source):
        return (o.gg, o.gu, o.gd)[m].at[:, rows_of(source, hb)]

    def trade(m, k):
        dest = lax.rem(p.d + k, n)
        return rcopy(
            o.fown.at[m, rows_of(dest, R)], ffn_out(m, p.d), o.ts.at[m, k], o.tr.at[m, k], (p.s, dest, p.t)
        )

    def came(m, k):
        source = lax.rem(p.d + n - k, n)
        return rcopy(o.fown.at[m, rows_of(p.d, R)], ffn_out(m, source), o.ts.at[m, k], o.tr.at[m, k], side)

    owns = [local(ffn[m].at[:, rows_of(p.t, hb)], o.fown.at[m]) for m in range(3)]
    order = [*range(1, n), 0]
    for m in range(3):
        for k in order:
            swap(m, k).start()
    need = [
        local(getattr(o, name), getattr(o, name + TAIL))
        for name in ("nfull", "dqkv", "afull", "heads", "lrlow", "lmid", "resid", "grlow", "plow", "llow", "lmg", "gcol")
    ]
    stage, last, finish = cube_scatter(p, o.acc, o.got, R, c.parts, (o.rs, o.rr), o.gp_v)
    mine_copies = []

    def grad(x, y, at, block=512):
        tokens = 2 * x.shape[1]

        @tiles(c.width, block)
        def _(rows):
            left = x[:, :, rows].reshape(tokens, block)
            o.acc[rows, at] = tn(left, y[...].reshape(tokens, y.shape[2])).astype(BF)

    def ffn_block(m, k):
        rows = rows_of(lax.rem(p.d + k, n), R)
        if k == order[0]:
            owns[m].wait()
        swap(m, k).wait_recv()
        total = o.fown[m, rows, :].astype(F32) + o.fgot[m, rows, :].astype(F32)
        o.fown[m, rows, :] = total.astype(BF)
        if k:
            trade(m, k).start()
        else:
            mine_copies.append(local(o.fown.at[m, rows], ffn_out(m, p.d)))

    def part_grad(h):
        begin, size = c.parts[h]
        base = c.qkv + c.heads
        if begin < c.qkv:
            grad(o.nfull_v, o.dqkv_v.at[:, :, pl.ds(begin, size)], pl.ds(begin, size))
        elif begin < base:
            grad(o.afull_v, o.heads_v.at[:, :, pl.ds(begin - c.qkv, size)], pl.ds(begin, size))
        elif begin == base:
            mine = rows_of(p.t, c.r)
            lane = lax.broadcasted_iota(jnp.int32, (512, LANES), 1)

            @tiles(c.width, 512)
            def _(rows):
                left = tn(o.nfull_v[0, mine, rows], o.lmg_v[0]) + tn(o.nfull_v[1, mine, rows], o.lmg_v[1])
                gains = o.gcol_v[rows, :].astype(F32)
                o.acc[rows, pl.ds(begin, LANES)] = jnp.where(lane < c.rank, left, gains).astype(BF)

            grad(o.lrlow_v, o.lmid_v, pl.ds(begin + LANES, LANES))
            o.rlow_v[...] = o.resid_v[...].astype(BF)
            grad(o.rlow_v, o.grlow_v, pl.ds(begin + 2 * LANES, c.per))
        else:
            grad(o.plow_v, o.llow_v, pl.ds(begin, c.per))

    for copy in need:
        copy.wait()
    events = []
    for m in range(3):
        for i, k in enumerate(order):
            events.append((c.kg[0] + c.kg[1] * (m * n + i), lambda m=m, k=k: ffn_block(m, k)))
    for h in range(len(c.parts)):
        events.append((c.kg[2] * h, lambda h=h: (part_grad(h), stage(h, 0))))
        for bit in range(1, lowest(0, n)):
            events.append((c.kg[3] + c.kg[4] * h + c.kg[5] * (bit - 1), lambda h=h, bit=bit: stage(h, bit)))
        events.append((c.kg[3] + c.kg[4] * h + c.kg[5] * (lowest(0, n) - 1), lambda h=h: last(h)))
    for _, run in sorted(events, key=lambda e: e[0]):
        run()
    shared = pl.ds(c.qkv + c.heads, c.small)
    o.ssend[...] = o.gp_v[:, shared].astype(BF)
    rest = rcopy(o.ssend, o.sgot, o.ss.at[0], o.sr.at[0], pair)
    rest.start()
    rest.wait()
    o.gp_v[:, shared] += o.sgot[...].astype(F32)
    out = local(o.gp_v, o.gp)
    for m in range(3):
        for k in range(n):
            swap(m, k).wait_send()
            if k:
                came(m, k).wait_recv()
                trade(m, k).wait_send()
    for q in range(len(c.parts)):
        finish(q)
    for copy in [*mine_copies, out]:
        copy.wait()


def fetch_weights(c, pack, gate, up, down):
    n, A, q = c.n, c.n // 2, len(c.cuts)
    outs = dict(
        pk=((c.width, c.total), BF),
        gw=((c.width, 2 * c.hb), BF),
        uw=((c.width, 2 * c.hb), BF),
        dw=((c.width, 2 * c.hb), BF),
        grow=((8, c.width), F32),
    )
    scratch = dict(
        gcol=pltpu.VMEM((c.width, LANES), BF),
        pack_v=pltpu.VMEM((c.R, c.total), BF),
        block_v=pltpu.VMEM((3, c.R, c.hb), BF),
        grow_v=pltpu.VMEM((8, c.width), F32),
        gs=dma(n, q), gr=dma(n, q),
        ts=dma(n, 3), tr=dma(n, 3), ys=dma(n, 3), yr=dma(n, 3), lsem=dma(12),
        go=pltpu.SemaphoreType.REGULAR,
    )
    return launch(
        lambda o: fetch_kernel(c, o), 6, dict(pack=pack, gate=gate, up=up, down=down), {}, outs, scratch
    )


def return_grads(c, f, g, gcol, dg, du, dd):
    n, A = c.n, c.n // 2
    R = c.R
    flat = ((R, n * c.hb), BF)
    outs = dict(gp=((R, c.total), F32), gg=flat, gu=flat, gd=flat)
    arrays = dict(
        nfull=f.nfull, dqkv=g.dqkv, afull=g.afull, heads=f.heads, lrlow=g.lrlow, lmid=f.lmid, resid=f.resid,
        grlow=g.grlow, plow=g.plow, llow=f.llow, lmg=g.lmg, gcol=gcol,
    )
    scratch = dict(
        acc=pltpu.VMEM((c.width, c.total), BF),
        got=pltpu.VMEM(((n - 1) * R, c.total), BF),
        gp_v=pltpu.VMEM((R, c.total), F32),
        fown=pltpu.VMEM((3, c.width, c.hb), BF),
        fgot=pltpu.VMEM((3, c.width, c.hb), BF),
        ssend=pltpu.VMEM((R, c.small), BF),
        sgot=pltpu.VMEM((R, c.small), BF),
        rlow_v=pltpu.VMEM(f.resid.shape, BF),
        ys=dma(3, n), yr=dma(3, n), ts=dma(3, n), tr=dma(3, n), ss=dma(1), sr=dma(1), lsem=dma(24),
        **{name + TAIL: pltpu.VMEM(v.shape, v.dtype) for name, v in arrays.items()},
        rs=dma(len(c.parts), n), rr=dma(len(c.parts), n),
    )
    return launch(lambda o: return_kernel(c, o), 7, dict(**arrays, dg=dg, du=du, dd=dd), {}, outs, scratch)


def widen_kernel(c, o):
    local = Local(o.lsem)
    loads = [local(o.gp, o.gp_v), local(o.gg, o.g_v.at[0]), local(o.gu, o.g_v.at[1]), local(o.gd, o.g_v.at[2])]
    base = c.qkv + c.heads
    loads[0].wait()
    out = [
        local(o.gp_v.at[:, pl.ds(0, c.heads)], o.q),
        local(o.gp_v.at[:, pl.ds(c.heads, HEAD)], o.k),
        local(o.gp_v.at[:, pl.ds(c.heads + HEAD, HEAD)], o.v),
        local(o.gp_v.at[:, pl.ds(base, LANES)], o.left),
        local(o.gp_v.at[:, pl.ds(base + 2 * LANES, c.per)], o.lg),
    ]
    o.t_v[...] = o.gp_v[:, pl.ds(c.qkv, c.heads)].T
    out.append(local(o.t_v, o.out))
    for m in range(3):
        loads[1 + m].wait()
        o.w_v[m] = o.g_v[m].astype(F32)
        out.append(local(o.w_v.at[m], (o.wg, o.wu, o.wd)[m]))
    for copy in out:
        copy.wait()


def widen(c, done):
    R, wide = c.R, c.n * c.hb
    outs = dict(
        q=((R, c.heads), F32), k=((R, HEAD), F32), v=((R, HEAD), F32), left=((R, LANES), F32), lg=((R, c.per), F32),
        out=((c.heads, R), F32), wg=((R, wide), F32), wu=((R, wide), F32), wd=((R, wide), F32),
    )
    scratch = dict(
        gp_v=pltpu.VMEM((R, c.total), F32), t_v=pltpu.VMEM((c.heads, R), F32),
        g_v=pltpu.VMEM((3, R, wide), BF), w_v=pltpu.VMEM((3, R, wide), F32), lsem=dma(16),
    )
    return launch(lambda o: widen_kernel(c, o), None, done, {}, outs, scratch)


def spread(gain, n, rows):
    return jnp.pad(gain, (0, rows - gain.shape[0]))


def body(
    hidden, layer_inputs, span_starts, cotangent, input_gain, query_weight, key_projection, value_projection,
    query_gain, key_norm_gain, output_weight, attention_gain, laurel_left, laurel_right, laurel_gain, prefeed_gain,
    gate_weight, up_weight, down_weight, postfeed_gain, layer_gate, layer_project, layer_gain,
):
    n, nt_ = lax.axis_size(D), lax.axis_size(T)
    t = lax.axis_index(T)
    rank = laurel_left.shape[2]
    width = hidden.shape[3]
    R = width // n
    heads = query_weight.shape[2]
    qkv = heads + 2 * HEAD
    per = layer_gate.shape[2]
    small = 2 * LANES + 2 * per
    base = qkv + heads
    c = SimpleNamespace(
        n=n, R=R, r=hidden.shape[2], width=width, heads=heads, qkv=qkv, per=per, small=small, rank=rank,
        total=qkv + heads + small, hb=gate_weight.shape[2] // n,
        cuts=((0, qkv), (qkv, heads), (qkv + heads, small)),
        parts=(*((i, 512) for i in range(0, qkv + heads, 512)), (base, small - per), (base + small - per, per)),
        ag=(12.0, 6.0, 12.0), tr=(1.0, 2.5, 30.0, 3.0), by_matrix=True, kg=(6.0, 2.9, 2.0, 20.0, 12.0, 12.0),
        halves=tuple((h * width // HALVES, width // HALVES) for h in range(HALVES)),
    )
    gains = jnp.stack(
        [
            input_gain[0], attention_gain[0], laurel_gain[0], prefeed_gain[0], postfeed_gain[0], layer_gain[0],
            spread(query_gain[0], n, R), spread(key_norm_gain[0], n, R),
        ],
        axis=1,
    )
    pad = lambda v, k: jnp.pad(v, ((0, 0), (0, LANES - k)))
    pack = jnp.concatenate(
        [
            query_weight[0], key_projection[0], value_projection[0], output_weight[0].T,
            pad(jnp.concatenate([laurel_left[0], gains], axis=1), rank + 8), pad(laurel_right[0].T, rank),
            layer_gate[0], layer_project[0].T,
        ],
        axis=1,
    )
    weights = fetch_weights(c, pack, gate_weight[0], up_weight[0], down_weight[0].T)
    columns = weights.pop("grow")
    short = HEAD // n
    head_gains = columns[6:].reshape(2, n, R)[:, :, :short].reshape(2, HEAD)
    gain_rows = jnp.concatenate([columns[:6], jnp.pad(head_gains, ((0, 0), (0, width - HEAD)))], axis=0)

    span = c.r * nt_
    position = jnp.arange(span, dtype=jnp.int32)
    begin = span_starts[:, 0][:, None]
    inside = (position[None] >= begin) & (position[None] < begin + IMG)
    allowed = (position[None, :] <= position[:, None])[None] | (inside[:, :, None] & inside[:, None, :])
    half = HEAD // 2
    frequency = jnp.exp(jnp.arange(half, dtype=F32) * (-2.0 * math.log(10000.0) / HEAD))
    angles = jnp.arange(span, dtype=F32)[:, None] * frequency[None, :]
    tables = dict(gains=gain_rows, cos=jnp.cos(angles), sin=jnp.sin(angles), allowed=allowed.astype(F32))
    data = SimpleNamespace(hidden=hidden[:, 0], lin=layer_inputs[0, :, 0], cot=cotangent[:, 0])

    stash, grads = None, None
    for k in range(3):
        stash = forward_tick(c, k, weights, data, tables, stash)
    for k in range(3):
        grads = backward_tick(c, k, weights, data, tables, stash, grads)
    f, g = SimpleNamespace(**stash), SimpleNamespace(**grads)

    def pair_grad(inputs, outs):
        inputs = inputs.reshape(-1, inputs.shape[-1])
        return tn(inputs, outs.reshape(-1, outs.shape[-1])).astype(BF)

    sums = g.ggr[0] + g.ggr[1]
    head_sums = jnp.pad(sums[6:, :HEAD].reshape(2, n, short), ((0, 0), (0, 0), (0, R - short))).reshape(2, width)
    gain_cols = jnp.concatenate([sums[:6], head_sums], axis=0).T
    gcol = jnp.pad(gain_cols, ((0, 0), (rank, LANES - rank - 8))).astype(BF)
    done = return_grads(
        c, f, g, gcol, pair_grad(f.pfull, g.dgl), pair_grad(f.pfull, g.dul), pair_grad(g.dfull, f.geglu)
    )
    w = SimpleNamespace(**widen(c, done))
    gp = done["gp"]
    base = qkv + heads
    gain_out = w.left[:, rank : rank + 8].T
    one = lambda i: gain_out[i][None]
    return (
        f.act[None, :, None],
        g.igrad[None, :, None],
        g.lgrad[None, :, None],
        one(0),
        w.q[None],
        w.k[None],
        w.v[None],
        gain_out[6, :short][None],
        gain_out[7, :short][None],
        w.out[None],
        one(1),
        w.left[:, :rank][None],
        gp[:, base + LANES : base + LANES + rank].T[None],
        one(2),
        one(3),
        w.wg[None],
        w.wu[None],
        w.wd.T[None],
        one(4),
        w.lg[None],
        gp[:, base + 2 * LANES + per :].T[None],
        one(5),
    )


def solution(mesh):
    rows, cols = P(S, D, T), P(S, T, D)
    vec, tall, flat = P(S, D), P(S, D, None), P(S, None, D)
    seq, out = P(None, D, T, None), P(S, None, D, T, None)
    weights = (
        vec, rows, rows, rows, vec, vec, cols, vec, tall, flat, vec, vec, rows, rows, cols, vec, tall, flat, vec,
    )
    return jax.shard_map(
        body,
        mesh=mesh,
        in_specs=(seq, out, P(None, D), seq, *weights),
        out_specs=(out, out, out, *weights),
        check_vma=False,
    )
```

```python
import math
from types import SimpleNamespace

import jax
import jax.numpy as jnp
from jax import lax
from jax.experimental import pallas as pl
from jax.experimental.pallas import tpu as pltpu
from jax.sharding import PartitionSpec as P

S, D, T = "section", "dp", "tensor"
MESH = pl.DeviceIdType.MESH
BF, F32 = jnp.bfloat16, jnp.float32
HEAD = 256
IMG = 64
EPS = 1e-06
RH = 0.5**0.5
NEG = -1e30
LANES = 128
GELU_C = math.sqrt(2.0 / math.pi)
GELU_K = 0.044715
VMEM_LIMIT = 60 << 20
HALVES = 2
GATHER_PARTS = 2


def rms_of(v):
    return lax.rsqrt(jnp.mean(v * v, axis=-1, keepdims=True) + EPS)


def rms_back(v, gain, grad):
    r = rms_of(v)
    unit = v * r
    inner = grad * gain
    back = r * (inner - unit * jnp.mean(inner * unit, axis=-1, keepdims=True))
    return back, jnp.sum(grad * unit, axis=0, keepdims=True)


def plain_back(v, grad):
    r = rms_of(v)
    unit = v * r
    return r * (grad - unit * jnp.mean(grad * unit, axis=-1, keepdims=True))


def gelu(v):
    return 0.5 * v * (1.0 + jnp.tanh(GELU_C * (v + GELU_K * v * v * v)))


def gelu_both(v):
    square = v * v
    th = jnp.tanh(GELU_C * v * (1.0 + GELU_K * square))
    value = 0.5 * v * (1.0 + th)
    slope = 0.5 * (1.0 + th) + 0.5 * v * (1.0 - th * th) * GELU_C * (1.0 + 3.0 * GELU_K * square)
    return value, slope


def rotate(v, cos, sin):
    half = HEAD // 2
    front, back = v[:, :half], v[:, half:]
    return jnp.concatenate([front * cos - back * sin, back * cos + front * sin], axis=-1)


def rotate_back(g, cos, sin):
    half = HEAD // 2
    front, back = g[:, :half], g[:, half:]
    return jnp.concatenate([front * cos + back * sin, back * cos - front * sin], axis=-1)


def nn(x, w):
    return jnp.dot(x, w, preferred_element_type=F32)


def nt(x, w):
    return lax.dot_general(x, w, (((1,), (1,)), ((), ())), preferred_element_type=F32)


def tn(x, w):
    return lax.dot_general(x, w, (((0,), (0,)), ((), ())), preferred_element_type=F32)


def tiles(count, step):
    def wrap(fn):
        def one(j, carry):
            fn(pl.ds(pl.multiple_of(j * step, step), step))
            return carry

        lax.fori_loop(0, count // step, one, 0)

    return wrap


def place(n):
    s, d, t = lax.axis_index(S), lax.axis_index(D), lax.axis_index(T)
    return SimpleNamespace(s=s, d=d, t=t, a=lax.div(d, 2), b=lax.rem(d, 2), n=n, A=n // 2)


def rcopy(src, dst, send, recv, device):
    return pltpu.make_async_remote_copy(
        src_ref=src, dst_ref=dst, send_sem=send, recv_sem=recv, device_id=device, device_id_type=MESH
    )


def rows_of(index, size):
    return pl.ds(pl.multiple_of(index * size, size), size)


class Local:
    def __init__(self, sems):
        self.sems, self.used = sems, 0

    def __call__(self, src, dst):
        copy = pltpu.make_async_copy(src, dst, self.sems.at[self.used])
        self.used += 1
        copy.start()
        return copy


def steps_of(p, fn, far_first=False):
    for delta in range(p.A - 1, 0, -1) if far_first else range(1, p.A):
        pl.when(p.a - delta >= 0)(lambda: fn(p.a - delta))
        pl.when(p.a + delta < p.A)(lambda: fn(p.a + delta))


def line_gather(p, buf, size, sems):
    zs, zr, xs, xr = sems
    side = (p.s, p.a * 2 + 1 - p.b, p.t)
    part = size // GATHER_PARTS

    def at(col, row, g):
        return buf.at[col, pl.ds(pl.multiple_of(row * size + g * part, part), part)]

    def along(row, g):
        return rcopy(at(p.b, p.a, g), at(p.b, p.a, g), zs.at[row, g], zr.at[p.a, g], (p.s, row * 2 + p.b, p.t))

    def came(row, g):
        return rcopy(at(p.b, row, g), at(p.b, row, g), zs.at[row, g], zr.at[row, g], side)

    def across(col, row, g):
        return rcopy(at(col, row, g), at(col, row, g), xs.at[row, g], xr.at[row, g], side)

    def each(fn):
        def run(row):
            for g in range(GATHER_PARTS):
                fn(row, g)

        return run

    for g in range(GATHER_PARTS):
        steps_of(p, lambda row: along(row, g).start(), True)
        across(p.b, p.a, g).start()

    def forward(row, g):
        came(row, g).wait_recv()
        across(p.b, row, g).start()

    def arrive():
        for row in range(p.A):
            each(lambda row, g: across(1 - p.b, row, g).wait_recv())(row)

    def finish():
        steps_of(p, each(lambda row, g: along(row, g).wait_send()))
        for row in range(p.A):
            each(lambda row, g: across(p.b, row, g).wait_send())(row)

    return lambda: steps_of(p, each(forward)), arrive, finish


def line_scatter(p, acc, other, got, step_got, size, cuts, sems, out):
    xs, xr, zs, zr = sems
    side = (p.s, p.a * 2 + 1 - p.b, p.t)

    def part(row, h):
        return (rows_of(row, size), pl.ds(cuts[h][0], cuts[h][1]))

    def across(h, row):
        at = part(row, h)
        return rcopy(other.at[at], got.at[at], xs.at[h, row], xr.at[h, row], side)

    def along(h, row):
        return rcopy(
            other.at[part(row, h)], step_got.at[part(p.a, h)], zs.at[h, row], zr.at[h, p.a], (p.s, row * 2 + p.b, p.t)
        )

    def came(h, row):
        return rcopy(other.at[part(row, h)], step_got.at[part(row, h)], zs.at[h, row], zr.at[h, row], side)

    def start(h):
        steps_of(p, lambda row: across(h, row).start(), True)
        across(h, p.a).start()

    def carry(h):
        def pass_on(row):
            at = part(row, h)
            across(h, row).wait()
            other[at] = (acc[at] + got[at].astype(F32)).astype(BF)
            along(h, row).start()

        steps_of(p, pass_on, True)

    def collect(h):
        across(h, p.a).wait()
        at = part(p.a, h)
        cols = (slice(None), at[1])
        out[cols] = acc[at] + got[at].astype(F32)

        def add(row):
            came(h, row).wait_recv()
            out[cols] += step_got[part(row, h)].astype(F32)

        steps_of(p, add)

    def finish(h):
        steps_of(p, lambda row: along(h, row).wait_send())

    return start, carry, collect, finish


def lowest(mask, n):
    bit = 0
    while (1 << bit) < n and not mask >> bit & 1:
        bit += 1
    return bit


def flip(d, mask):
    bit = 0
    result = d
    while 1 << bit <= mask:
        if mask >> bit & 1:
            result = result + (1 - 2 * lax.rem(lax.div(d, 1 << bit), 2)) * (1 << bit)
        bit += 1
    return result


def cube_scatter(p, acc, got, size, cuts, sems, out):
    send, recv = sems
    n = p.n

    def cols(h):
        return pl.ds(cuts[h][0], cuts[h][1])

    def block(mask):
        return rows_of(flip(p.d, mask), size)

    def message(h, mask):
        bit = lowest(mask, n)
        return rcopy(
            acc.at[block(mask), cols(h)],
            got.at[pl.ds((mask - 1) * size, size), cols(h)],
            send.at[h, mask],
            recv.at[h, mask],
            (p.s, flip(p.d, 1 << bit), p.t),
        )

    def stage(h, bit):
        for mask in range(1, n):
            if lowest(mask, n) == bit:
                at = (block(mask), cols(h))
                total = None
                for below in range(bit):
                    came = mask | 1 << below
                    message(h, came).wait_recv()
                    term = got[pl.ds((came - 1) * size, size), cols(h)].astype(F32)
                    total = term if total is None else total + term
                if total is not None:
                    acc[at] = (acc[at].astype(F32) + total).astype(BF)
                message(h, mask).start()

    def last(h):
        total = acc[block(0), cols(h)].astype(F32)
        for below in range(lowest(0, n)):
            message(h, 1 << below).wait_recv()
            total = total + got[pl.ds(((1 << below) - 1) * size, size), cols(h)].astype(F32)
        out[:, cols(h)] = total

    def finish(h):
        for mask in range(1, n):
            message(h, mask).wait_send()

    return stage, last, finish


def dma(*shape):
    return pltpu.SemaphoreType.DMA(shape)


def gather_sems(A):
    g = GATHER_PARTS
    return dict(gzs=dma(A, g), gzr=dma(A, g), gxs=dma(A, g), gxr=dma(A, g))


def scatter_sems(A, parts):
    return dict(rxs=dma(parts, A), rxr=dma(parts, A), rzs=dma(parts, A), rzr=dma(parts, A))


HBM = pl.BlockSpec(memory_space=pltpu.HBM)
VM = pl.BlockSpec(memory_space=pltpu.VMEM)


def launch(kernel, cid, hbm_in, vmem_in, outs, scratch):
    everything = [*hbm_in, *vmem_in, *outs, *scratch]

    def run(*refs):
        kernel(SimpleNamespace(**dict(zip(everything, refs))))

    results = pl.pallas_call(
        run,
        out_shape=[jax.ShapeDtypeStruct(*spec) for spec in outs.values()],
        in_specs=[HBM] * len(hbm_in) + [VM] * len(vmem_in),
        out_specs=[HBM] * len(outs),
        scratch_shapes=list(scratch.values()),
        compiler_params=pltpu.CompilerParams(
            collective_id=cid, has_side_effects=cid is not None, vmem_limit_bytes=VMEM_LIMIT
        ),
    )(*hbm_in.values(), *vmem_in.values())
    return dict(zip(outs, results))


def fetch_kernel(c, o):
    p = place(c.n)
    n, A, R, hb = c.n, c.n // 2, c.R, c.hb
    barrier = pltpu.get_barrier_semaphore()

    def signal(device):
        pl.semaphore_signal(barrier, inc=1, device_id=device, device_id_type=MESH)

    for k in range(1, n):
        signal((p.s, lax.rem(p.d + k, n), p.t))
    signal((p.s, p.d, 1 - p.t))
    signal((1 - p.s, p.d, p.t))
    pl.semaphore_wait(barrier, n + 1)

    @pl.when(p.s == 1)
    def _():
        pl.semaphore_wait(o.go, 1)

    side = (p.s, p.a * 2 + 1 - p.b, p.t)
    pair = (p.s, p.d, 1 - p.t)
    cuts = c.cuts
    bits = lowest(0, n)
    local = Local(o.lsem)
    waits = []

    def give(mask, bit, q):
        rows, cs = rows_of(flip(p.d, mask), R), pl.ds(*cuts[q])
        src = o.pk.at[rows, cs] if mask else o.pack.at[:, cs]
        far = mask | 1 << bit
        return rcopy(src, o.pk.at[rows, cs], o.gs.at[far, q], o.gr.at[far, q], (p.s, flip(p.d, 1 << bit), p.t))

    def taken(mask, q):
        at = (rows_of(flip(p.d, mask), R), pl.ds(*cuts[q]))
        return rcopy(o.pk.at[at], o.pk.at[at], o.gs.at[mask, q], o.gr.at[mask, q], side)

    def pass_on(mask, q):
        if mask:
            taken(mask, q).wait_recv()
        for bit in reversed(range(lowest(mask, n))):
            give(mask, bit, q).start()

    ffn = ((o.gate, o.gw), (o.up, o.uw), (o.down, o.dw))

    def block(m, source, half):
        return ffn[m][1].at[rows_of(source, R), rows_of(half, hb)]

    def trade(m, k):
        dest = lax.rem(p.d + k, n)
        return rcopy(
            ffn[m][0].at[:, rows_of(dest, hb)], block(m, p.d, p.t), o.ts.at[k, m], o.tr.at[k, m], (p.s, dest, p.t)
        )

    def came(m, k):
        source = lax.rem(p.d + n - k, n)
        return rcopy(
            ffn[m][0].at[:, rows_of(p.d, hb)], block(m, source, p.t), o.ts.at[k, m], o.tr.at[k, m], side
        )

    def share(m, k, half):
        source = lax.rem(p.d + n - k, n)
        src = ffn[m][0].at[:, rows_of(p.d, hb)] if k == 0 else block(m, source, half)
        return rcopy(src, block(m, source, half), o.ys.at[k, m], o.yr.at[k, m], pair)

    bounce = [local(o.pack, o.pack_v)]
    for m in range(3):
        bounce.append(local(ffn[m][0].at[:, rows_of(p.d, hb)], o.block_v.at[m]))
    events = []
    inner = sorted((mask for mask in range(2, n, 2)), key=lambda mask: (-lowest(mask, n), mask))
    for q in range(len(cuts)):
        events.append((0.0 + 0.1 * q, lambda q=q: pass_on(0, q)))
        for i, mask in enumerate(inner):
            events.append((c.ag[0] + c.ag[1] * q + c.ag[2] * i, lambda q=q, mask=mask: pass_on(mask, q)))
    for k in range(n):
        for m in range(3):
            at = m * n + k if c.by_matrix else k * 3 + m
            if k:
                events.append((c.tr[0] + c.tr[1] * at, lambda m=m, k=k: trade(m, k).start()))
                events.append((c.tr[2] + c.tr[3] * at, lambda m=m, k=k: (came(m, k).wait_recv(), share(m, k, p.t).start())))
            else:
                events.append((c.tr[0] + c.tr[1] * at, lambda m=m: share(m, 0, p.t).start()))
    for _, run in sorted(events, key=lambda e: e[0]):
        run()
    for copy in bounce:
        copy.wait()
    waits.append(local(o.pack_v, o.pk.at[rows_of(p.d, R)]))
    for m in range(3):
        waits.append(local(o.block_v.at[m], block(m, p.d, p.t)))

    @pl.when(p.s == 0)
    def _():
        pl.semaphore_signal(o.go, inc=1, device_id=(1 - p.s, p.d, p.t), device_id_type=MESH)

    for q in range(len(cuts)):
        for mask in range(1, n, 2):
            taken(mask, q).wait_recv()
    for k in range(n):
        for m in range(3):
            share(m, k, 1 - p.t).wait_recv()
    for q in range(len(cuts)):
        for mask in range(0, n, 2):
            for bit in range(lowest(mask, n)):
                give(mask, bit, q).wait_send()
    for k in range(n):
        for m in range(3):
            if k:
                trade(m, k).wait_send()
            share(m, k, p.t).wait_send()
    for copy in waits:
        copy.wait()
    last = local(o.pk.at[:, pl.ds(c.qkv + c.heads, LANES)], o.gcol)
    last.wait()
    o.grow_v[...] = o.gcol[...].astype(F32).T[c.rank : c.rank + 8]
    last = local(o.grow_v, o.grow)
    last.wait()


def load_weights(c, o, local):
    qn, on = c.qkv, c.heads
    got = [
        local(o.pk.at[:, pl.ds(qn + on, c.small)], o.sm_v),
        local(o.pk.at[:, pl.ds(0, qn)], o.qkv_v),
        local(o.pk.at[:, pl.ds(qn, on)], o.ot_v),
        local(o.gw, o.gw_v),
        local(o.uw, o.uw_v),
        local(o.dw, o.dw_v),
    ]
    return SimpleNamespace(sm=got[0], qkv=got[1], ot=got[2], gw=got[3], uw=got[4], dw=got[5])


def weight_scratch(c):
    return dict(
        sm_v=pltpu.VMEM((c.width, c.small), BF),
        qkv_v=pltpu.VMEM((c.width, c.qkv), BF),
        ot_v=pltpu.VMEM((c.width, c.heads), BF),
        gw_v=pltpu.VMEM((c.width, 2 * c.hb), BF),
        uw_v=pltpu.VMEM((c.width, 2 * c.hb), BF),
        dw_v=pltpu.VMEM((c.width, 2 * c.hb), BF),
    )


LL, LR, LG, LP = (0, 128), (128, 128), (256, 256), (512, 256)


def cols_of(cut):
    return (slice(None), pl.ds(*cut))


def enter(p, o, sender):
    barrier = pltpu.get_barrier_semaphore()

    def signal(device):
        pl.semaphore_signal(barrier, inc=1, device_id=device, device_id_type=MESH)

    partner = (1 - p.s, p.d, p.t)
    pl.when(p.s == sender)(lambda: signal(partner))
    line_greet(p, signal)
    line = p.A + 1
    pl.semaphore_wait(barrier, jnp.where(p.s == sender, line, line + 1))

    @pl.when(p.s == 1 - sender)
    def _():
        pl.semaphore_signal(o.ready, inc=1, device_id=partner, device_id_type=MESH)


def line_greet(p, signal):
    signal((p.s, p.d, 1 - p.t))
    signal((p.s, p.a * 2 + 1 - p.b, p.t))
    steps_of(p, lambda row: signal((p.s, row * 2 + p.b, p.t)))


def again(p):
    barrier = pltpu.get_barrier_semaphore()
    line_greet(p, lambda device: pl.semaphore_signal(barrier, inc=1, device_id=device, device_id_type=MESH))
    pl.semaphore_wait(barrier, p.A + 1)


def view(c, o, m, buffers, sems):
    slot = m if c.slots == 2 else 0
    names = {name: getattr(o, name + str(slot)) for name in buffers}
    names.update({name: getattr(o, name + str(m)) for name in sems})
    return SimpleNamespace(**names)


def twice(c, buffers, sems):
    out = {}
    for slot in range(c.slots):
        out.update({name + str(slot): spec for name, spec in buffers.items()})
    for m in range(2):
        out.update({name + str(m): spec for name, spec in sems.items()})
    return out


def run_stages(c, p, order, stages):
    if c.slots == 1:
        order = [item for m in range(2) for item in order if item[1] == m]
    for name, m in order:
        if c.slots == 1 and name == FIRST and m == 1:
            stages[0][LAST]()
            again(p)
        stages[m][name]()
    for m in range(2) if c.slots == 2 else (1,):
        stages[m][LAST]()


FIRST, GIVE, OWN, REST, SUMS, PASS, LAST = range(7)
BEGIN, PROJ, JOIN, TAIL_STAGE, MIDDLE, HEADS_STAGE, ENTRY = range(10, 17)


def line_stages(c, p, v, hidden_part, down_part, ready):
    start, carry, collect, finish = line_scatter(
        p, v.acc, v.other, v.got, v.step_got, c.r, c.halves, (v.rxs, v.rxr, v.rzs, v.rzr), v.down_v
    )
    link = SimpleNamespace()

    def begin():
        link.forward, link.arrive, link.gathered = line_gather(p, v.xbuf, c.r, (v.gzs, v.gzr, v.gxs, v.gxr))

    def own():
        ready(0)
        hidden_part(p.b)

    def rest():
        link.arrive()
        hidden_part(1 - p.b)
        ready(1)
        for h in range(HALVES):
            down_part(1 - p.b, v.other, h)
            start(h)
        for h in range(HALVES):
            down_part(p.b, v.acc, h)

    def sums():
        for h in range(HALVES):
            carry(h)

    def total():
        for h in range(HALVES):
            collect(h)

    def end():
        link.gathered()
        for h in range(HALVES):
            finish(h)

    return SimpleNamespace(begin=begin, give=lambda: link.forward(), own=own, rest=rest, sums=sums, total=total, end=end)


def once(*copies):
    state = [False]

    def run():
        if not state[0]:
            state[0] = True
            for copy in copies:
                copy.wait()

    return run


def forward_stages(c, p, o, v, m, w, local):
    r, width, hb2 = c.r, c.width, 2 * c.hb
    pair = (p.s, p.d, 1 - p.t)
    mine, theirs = rows_of(p.t, r), rows_of(1 - p.t, r)
    gain = lambda i: o.gains[i : i + 1, :]
    hand = rcopy(v.act_v, v.hid, v.hs.at[0], v.hr.at[0], (1 - p.s, p.d, p.t))
    first = pltpu.make_async_copy(o.hidden.at[m], v.hid, v.fsem.at[0])
    send = rcopy(v.nbuf.at[mine], v.nbuf.at[mine], v.ys.at[0], v.yr.at[0], pair)
    swap = rcopy(v.ysend, v.ygot, v.ys.at[1], v.yr.at[1], pair)
    keep = []

    def stash(*pairs):
        keep.extend(local(src, dst.at[m]) for src, dst in pairs)

    def normed_of():
        x = v.hid[...].astype(F32)
        return x, x * rms_of(x) * gain(0)

    def begin():
        lv = local(o.lin.at[m], v.lv)
        v.lv_wait = lv.wait

        @pl.when(p.s == 0)
        def _():
            first.start()
            first.wait()

        pl.when(p.s == 1)(hand.wait_recv)
        v.nbuf[mine, :] = normed_of()[1].astype(BF)
        send.start()
        w.sm()
        lane = lax.broadcasted_iota(jnp.int32, (r, LANES), 1)
        mid = jnp.where(lane < c.rank, nn(v.nbuf[mine, :], o.sm_v[cols_of(LL)]), 0.0)
        v.lmid_v[...] = mid.astype(BF)
        v.lraw_v[...] = nt(v.lmid_v[...], o.sm_v[cols_of(LR)])
        stash((v.hid, o.xlow), (v.lmid_v, o.lmid), (v.lraw_v, o.lraw))

    def proj():
        w.qkv()
        rcopy(v.nbuf.at[theirs], v.nbuf.at[theirs], v.ys.at[0], v.yr.at[0], pair).wait_recv()

        @tiles(c.qkv, 256)
        def _(at):
            v.qraw_v[:, at] = nn(v.nbuf[...], o.qkv_v[:, at])

        cos, sin = o.cos[...], o.sin[...]
        q_gain, k_gain = o.gains[6:7, 0:HEAD], o.gains[7:8, 0:HEAD]
        allowed = o.allowed[m] > 0.5
        kraw = v.qraw_v[:, pl.ds(c.heads, HEAD)]
        vraw = v.qraw_v[:, pl.ds(c.heads + HEAD, HEAD)]
        key = rotate(kraw * rms_of(kraw) * k_gain, cos, sin).astype(BF)
        value = (vraw * rms_of(vraw)).astype(BF)
        for h in range(c.heads // HEAD):
            at = pl.ds(h * HEAD, HEAD)
            raw = v.qraw_v[:, at]
            query = rotate(raw * rms_of(raw) * q_gain, cos, sin).astype(BF)
            scores = jnp.where(allowed, nt(query, key) * HEAD**-0.5, NEG)
            shifted = jnp.exp(scores - jnp.max(scores, axis=-1, keepdims=True))
            prob = shifted / jnp.sum(shifted, axis=-1, keepdims=True)
            v.heads_v[:, at] = nn(prob.astype(BF), value).astype(BF)
        w.ot()

        @tiles(width, 256)
        def _(at):
            v.acc[0 : 2 * r, at] = nt(v.heads_v[...], o.ot_v[at, :])

        v.ysend[...] = v.acc[theirs, :].astype(BF)
        swap.start()
        stash((v.nbuf, o.nfull), (v.qraw_v, o.qraw), (v.heads_v, o.heads))

    def join():
        x, normed = normed_of()
        swap.wait()
        att = v.acc[mine, :] + v.ygot[...].astype(F32)
        v.att_v[...] = att
        lraw = v.lraw_v[...]
        comb = (x + att * rms_of(att) * gain(1) + normed + lraw * rms_of(lraw) * gain(2)) * RH
        v.comb_v[...] = comb
        v.xbuf[p.b, rows_of(p.a, r), :] = (comb * rms_of(comb) * gain(3)).astype(BF)
        line.begin()
        stash((v.att_v, o.att), (v.comb_v, o.comb))

    def hidden_part(col):
        @tiles(hb2, min(256, hb2))
        def _(at):
            gate = nn(v.xbuf[col], o.gw_v[:, at])
            up = nn(v.xbuf[col], o.uw_v[:, at])
            v.gate_v[col, :, at] = gate.astype(BF)
            v.up_v[col, :, at] = up.astype(BF)
            v.geglu_v[col, :, at] = (gelu(gate) * up).astype(BF)

    def down_part(col, dest, h):
        start, size = c.halves[h]

        @tiles(size, 256)
        def _(at):
            at = pl.ds(pl.multiple_of(start + at.start, 256), 256)
            dest[:, at] = nt(v.geglu_v[col], o.dw_v[at, :]).astype(dest.dtype)

    def ready(i):
        if i == 0:
            w.gw()
            w.uw()
        else:
            w.dw()

    line = line_stages(c, p, v, hidden_part, down_part, ready)

    def rest():
        line.rest()
        stash((v.xbuf, o.pfull), (v.gate_v, o.gate), (v.up_v, o.up), (v.geglu_v, o.geglu))

    def tail():
        line.total()
        down = v.down_v[...]
        v.resid_v[...] = v.comb_v[...] + down * rms_of(down) * gain(4)
        graw = nn(v.resid_v[...].astype(BF), o.sm_v[cols_of(LG)])
        v.graw_v[...] = graw
        v.lv_wait()
        v.llow_v[...] = (gelu(graw) * v.lv[...].astype(F32)).astype(BF)
        proj = nt(v.llow_v[...], o.sm_v[cols_of(LP)])
        v.proj_v[...] = proj
        v.act_v[...] = (v.resid_v[...] + proj * rms_of(proj) * gain(5)).astype(BF)

        @pl.when(p.s == 0)
        def _():
            if m == 0:
                pl.semaphore_wait(o.ready, 1)
            hand.start()

        stash((v.down_v, o.down), (v.resid_v, o.resid), (v.graw_v, o.graw), (v.llow_v, o.llow), (v.proj_v, o.proj))
        stash((v.act_v, o.act))

    def end():
        send.wait_send()
        line.end()
        pl.when(p.s == 0)(hand.wait_send)
        for copy in keep:
            copy.wait()

    return {
        FIRST: begin, PROJ: proj, JOIN: join, GIVE: line.give, OWN: line.own, REST: rest, SUMS: line.sums,
        TAIL_STAGE: tail, LAST: end,
    }


FORWARD_ORDER = (
    (FIRST, 0), (PROJ, 0), (JOIN, 0), (FIRST, 1), (PROJ, 1), (GIVE, 0), (JOIN, 1), (OWN, 0), (GIVE, 1), (REST, 0),
    (OWN, 1), (SUMS, 0), (REST, 1), (TAIL_STAGE, 0), (SUMS, 1), (TAIL_STAGE, 1),
)


def waits_of(c, o, local):
    got = load_weights(c, o, local)
    return SimpleNamespace(**{name: once(copy) for name, copy in vars(got).items()})


def forward_kernel(c, o):
    p = place(c.n)
    local = Local(o.lsem)
    w = waits_of(c, o, local)
    enter(p, o, 0)
    views = [view(c, o, m, forward_buffers(c), stage_sems(c) | dict(hid=None)) for m in range(2)]
    stages = [forward_stages(c, p, o, views[m], m, w, local) for m in range(2)]
    run_stages(c, p, FORWARD_ORDER, stages)


def stash_shapes(c):
    m, r, w, q = 2, c.r, c.width, 2 * c.r
    ar, hb2 = c.n // 2 * c.r, 2 * c.hb
    return dict(
        act=((m, r, w), BF),
        xlow=((m, r, w), BF),
        nfull=((m, q, w), BF),
        qraw=((m, q, c.qkv), F32),
        heads=((m, q, c.heads), BF),
        att=((m, r, w), F32),
        lmid=((m, r, LANES), BF),
        lraw=((m, r, w), F32),
        comb=((m, r, w), F32),
        pfull=((m, 2, ar, w), BF),
        gate=((m, 2, ar, hb2), BF),
        up=((m, 2, ar, hb2), BF),
        geglu=((m, 2, ar, hb2), BF),
        down=((m, r, w), F32),
        resid=((m, r, w), F32),
        graw=((m, r, c.per), F32),
        llow=((m, r, c.per), BF),
        proj=((m, r, w), F32),
    )


TAIL = "_v"


def scratch_of(shapes):
    return {name + TAIL: pltpu.VMEM(shape[1:], kind) for name, (shape, kind) in shapes.items()}


def line_buffers(c):
    ar = c.n // 2 * c.r
    return dict(
        xbuf=pltpu.VMEM((2, ar, c.width), BF),
        acc=pltpu.VMEM((ar, c.width), F32),
        other=pltpu.VMEM((ar, c.width), BF),
        got=pltpu.VMEM((ar, c.width), BF),
        step_got=pltpu.VMEM((ar, c.width), BF),
        ysend=pltpu.VMEM((c.r, c.width), BF),
        ygot=pltpu.VMEM((c.r, c.width), BF),
        lv=pltpu.VMEM((c.r, c.per), BF),
    )


def stage_sems(c):
    return dict(
        fsem=dma(1), hs=dma(1), hr=dma(1), ys=dma(2), yr=dma(2), **gather_sems(c.n // 2), **scatter_sems(c.n // 2, HALVES)
    )


def forward_buffers(c):
    shapes = stash_shapes(c)
    own = {name: shapes[name] for name in shapes if name not in ("xlow", "nfull", "pfull")}
    return dict(nbuf=pltpu.VMEM((2 * c.r, c.width), BF), **scratch_of(own), **line_buffers(c))


def shared_scratch(c):
    return dict(**weight_scratch(c), lsem=dma(80), ready=pltpu.SemaphoreType.REGULAR)


def forward_pass(c, weights, data, tables):
    scratch = dict(
        **twice(c, forward_buffers(c), stage_sems(c) | dict(hid=pltpu.VMEM((c.r, c.width), BF))), **shared_scratch(c)
    )
    return launch(
        lambda o: forward_kernel(c, o),
        0,
        dict(**weights, hidden=data.hidden, lin=data.lin),
        tables,
        stash_shapes(c),
        scratch,
    )


def backward_stages(c, p, o, v, m, w, local):
    r, width, hb2 = c.r, c.width, 2 * c.hb
    pair = (p.s, p.d, 1 - p.t)
    mine, theirs = rows_of(p.t, r), rows_of(1 - p.t, r)
    gain = lambda i: o.gains[i : i + 1, :]
    hand = rcopy(v.hid, v.hid, v.hs.at[0], v.hr.at[0], (1 - p.s, p.d, p.t))
    first = pltpu.make_async_copy(o.cot.at[m], v.hid, v.fsem.at[0])
    send = rcopy(v.abuf.at[mine], v.abuf.at[mine], v.ys.at[0], v.yr.at[0], pair)
    swap = rcopy(v.ysend, v.ygot, v.ys.at[1], v.yr.at[1], pair)
    keep, need = [], {}

    def stash(*pairs):
        keep.extend(local(src, dst.at[m]) for src, dst in pairs)

    def fetch():
        loads = (
            ((o.proj, v.proj_v), (o.graw, v.graw_v), (o.lin, v.lv)),
            ((o.down, v.down_v),),
            ((o.gate, v.gate_v), (o.up, v.up_v)),
            ((o.comb, v.comb_v), (o.att, v.att_v), (o.lraw, v.lraw_v)),
            ((o.xlow, v.xlow_v), (o.qraw, v.qraw_v)),
        )
        for i, group in enumerate(loads):
            need[i] = [local(src.at[m], dst) for src, dst in group]

    def have(i):
        for copy in need[i]:
            copy.wait()

    def begin():
        if c.slots == 1:
            fetch()

        @pl.when(p.s == 1)
        def _():
            first.start()
            first.wait()

        pl.when(p.s == 0)(hand.wait_recv)
        have(0)
        v.ggr_v[...] = jnp.zeros_like(v.ggr_v)
        dproj, v.ggr_v[5:6, :] = rms_back(v.proj_v[...], gain(5), v.hid[...].astype(F32))
        v.plow_v[...] = dproj.astype(BF)
        w.sm()
        dmid = nn(v.plow_v[...], o.sm_v[cols_of(LP)])
        value, slope = gelu_both(v.graw_v[...])
        v.lgrad_v[...] = value * dmid
        v.grlow_v[...] = (dmid * v.lv[...].astype(F32) * slope).astype(BF)
        dres = v.hid[...].astype(F32) + nt(v.grlow_v[...], o.sm_v[cols_of(LG)])
        v.igrad_v[...] = dres
        have(1)
        ddown, v.ggr_v[4:5, :] = rms_back(v.down_v[...], gain(4), dres)
        v.xbuf[p.b, rows_of(p.a, r), :] = ddown.astype(BF)
        line.begin()
        stash((v.lgrad_v, o.lgrad), (v.plow_v, o.plow), (v.grlow_v, o.grlow))

    def hidden_part(col):
        @tiles(hb2, min(256, hb2))
        def _(at):
            dgeglu = nn(v.xbuf[col], o.dw_v[:, at])
            value, slope = gelu_both(v.gate_v[col, :, at].astype(F32))
            up = v.up_v[col, :, at].astype(F32)
            v.up_v[col, :, at] = (dgeglu * value).astype(BF)
            v.gate_v[col, :, at] = (dgeglu * up * slope).astype(BF)

    def down_part(col, dest, h):
        start, size = c.halves[h]

        @tiles(size, 256)
        def _(at):
            at = pl.ds(pl.multiple_of(start + at.start, 256), 256)
            part = nt(v.gate_v[col], o.gw_v[at, :]) + nt(v.up_v[col], o.uw_v[at, :])
            dest[:, at] = part.astype(dest.dtype)

    def ready(i):
        if i == 0:
            w.dw()
            have(2)
        else:
            w.gw()
            w.uw()

    line = line_stages(c, p, v, hidden_part, down_part, ready)

    def rest():
        line.rest()
        stash((v.xbuf, o.dfull), (v.gate_v, o.dgl), (v.up_v, o.dul))

    def middle():
        line.total()
        have(3)
        dcomb, v.ggr_v[3:4, :] = rms_back(v.comb_v[...], gain(3), v.down_v[...])
        even = (v.igrad_v[...] + dcomb) * RH
        v.igrad_v[...] = even
        datt, v.ggr_v[1:2, :] = rms_back(v.att_v[...], gain(1), even)
        v.abuf[mine, :] = datt.astype(BF)
        send.start()
        dlraw, v.ggr_v[2:3, :] = rms_back(v.lraw_v[...], gain(2), v.igrad_v[...])
        v.lrlow_v[...] = dlraw.astype(BF)
        v.lmg_v[...] = nn(v.lrlow_v[...], o.sm_v[cols_of(LR)]).astype(BF)
        v.proj_v[...] = v.igrad_v[...] + nt(v.lmg_v[...], o.sm_v[cols_of(LL)])
        stash((v.lrlow_v, o.lrlow), (v.lmg_v, o.lmg))

    def heads():
        w.ot()
        rcopy(v.abuf.at[theirs], v.abuf.at[theirs], v.ys.at[0], v.yr.at[0], pair).wait_recv()

        @tiles(c.heads, 256)
        def _(at):
            v.hgrad_v[:, at] = nn(v.abuf[...], o.ot_v[:, at]).astype(BF)

        have(4)
        cos, sin = o.cos[...], o.sin[...]
        q_gain, k_gain = o.gains[6:7, 0:HEAD], o.gains[7:8, 0:HEAD]
        allowed = o.allowed[m] > 0.5
        k_at, v_at = pl.ds(c.heads, HEAD), pl.ds(c.heads + HEAD, HEAD)
        kraw, vraw = v.qraw_v[:, k_at], v.qraw_v[:, v_at]
        key = rotate(kraw * rms_of(kraw) * k_gain, cos, sin).astype(BF)
        value = (vraw * rms_of(vraw)).astype(BF)
        dkey = jnp.zeros(kraw.shape, F32)
        dvalue = jnp.zeros(vraw.shape, F32)
        dq_gain = jnp.zeros((1, HEAD), F32)
        for h in range(c.heads // HEAD):
            at = pl.ds(h * HEAD, HEAD)
            raw = v.qraw_v[:, at]
            query = rotate(raw * rms_of(raw) * q_gain, cos, sin).astype(BF)
            scores = jnp.where(allowed, nt(query, key) * HEAD**-0.5, NEG)
            shifted = jnp.exp(scores - jnp.max(scores, axis=-1, keepdims=True))
            prob = shifted / jnp.sum(shifted, axis=-1, keepdims=True)
            hgrad = v.hgrad_v[:, at]
            dprob = nt(hgrad, value)
            dvalue = dvalue + tn(prob.astype(BF), hgrad)
            inner = jnp.sum(prob * dprob, axis=-1, keepdims=True)
            dscore = (prob * (dprob - inner)).astype(BF)
            dquery = nn(dscore, key) * HEAD**-0.5
            dkey = dkey + tn(dscore, query) * HEAD**-0.5
            draw, dg = rms_back(raw, q_gain, rotate_back(dquery, cos, sin))
            dq_gain = dq_gain + dg
            v.dqkv_v[:, at] = draw.astype(BF)
        draw, dk_gain = rms_back(kraw, k_gain, rotate_back(dkey, cos, sin))
        v.dqkv_v[:, k_at] = draw.astype(BF)
        v.dqkv_v[:, v_at] = plain_back(vraw, dvalue).astype(BF)
        v.ggr_v[6:7, 0:HEAD] = dq_gain
        v.ggr_v[7:8, 0:HEAD] = dk_gain
        w.qkv()

        @tiles(width, 256)
        def _(at):
            v.acc[0 : 2 * r, at] = nt(v.dqkv_v[...], o.qkv_v[at, :])

        v.ysend[...] = v.acc[theirs, :].astype(BF)
        swap.start()
        stash((v.abuf, o.afull), (v.dqkv_v, o.dqkv))

    def entry():
        swap.wait()
        dnorm = v.proj_v[...] + v.acc[mine, :] + v.ygot[...].astype(F32)
        dx, v.ggr_v[0:1, :] = rms_back(v.xlow_v[...].astype(F32), gain(0), dnorm)
        dx = dx + v.igrad_v[...]
        v.igrad_v[...] = dx

        @pl.when(p.s == 1)
        def _():
            v.hid[...] = dx.astype(BF)
            if m == 0:
                pl.semaphore_wait(o.ready, 1)
            hand.start()

        stash((v.igrad_v, o.igrad), (v.ggr_v, o.ggr))

    def end():
        send.wait_send()
        line.end()
        pl.when(p.s == 1)(hand.wait_send)
        for copy in keep:
            copy.wait()

    return {
        FIRST: begin, GIVE: line.give, OWN: line.own, REST: rest, SUMS: line.sums, MIDDLE: middle, HEADS_STAGE: heads,
        ENTRY: entry, LAST: end, BEGIN: fetch,
    }


BACKWARD_ORDER = (
    (FIRST, 0), (GIVE, 0), (OWN, 0), (FIRST, 1), (REST, 0), (GIVE, 1), (OWN, 1), (SUMS, 0), (REST, 1), (MIDDLE, 0),
    (HEADS_STAGE, 0), (SUMS, 1), (ENTRY, 0), (MIDDLE, 1), (HEADS_STAGE, 1), (ENTRY, 1),
)


def backward_kernel(c, o):
    p = place(c.n)
    local = Local(o.lsem)
    views = [view(c, o, m, backward_buffers(c), stage_sems(c) | dict(hid=None)) for m in range(2)]
    late = {}
    w = SimpleNamespace(**{name: (lambda name=name: late[name]()) for name in ("sm", "qkv", "ot", "gw", "uw", "dw")})
    stages = [backward_stages(c, p, o, views[m], m, w, local) for m in range(2)]
    if c.slots == 2:
        stages[0][BEGIN]()
    late.update(vars(waits_of(c, o, local)))
    if c.slots == 2:
        stages[1][BEGIN]()
    enter(p, o, 1)
    run_stages(c, p, BACKWARD_ORDER, stages)


def grad_shapes(c):
    m, r, w, q = 2, c.r, c.width, 2 * c.r
    ar, hb2 = c.n // 2 * c.r, 2 * c.hb
    return dict(
        igrad=((m, r, w), F32),
        lgrad=((m, r, c.per), F32),
        plow=((m, r, w), BF),
        grlow=((m, r, c.per), BF),
        dfull=((m, 2, ar, w), BF),
        dgl=((m, 2, ar, hb2), BF),
        dul=((m, 2, ar, hb2), BF),
        lrlow=((m, r, w), BF),
        lmg=((m, r, LANES), BF),
        afull=((m, q, w), BF),
        dqkv=((m, q, c.qkv), BF),
        ggr=((m, 8, w), F32),
    )


READ = ("proj", "graw", "down", "gate", "up", "comb", "att", "lraw", "xlow", "qraw")


def backward_buffers(c):
    shapes, kept = grad_shapes(c), stash_shapes(c)
    own = {name: shapes[name] for name in shapes if name not in ("dfull", "afull", "dgl", "dul")}
    return dict(
        abuf=pltpu.VMEM((2 * c.r, c.width), BF),
        hgrad_v=pltpu.VMEM((2 * c.r, c.heads), BF),
        **scratch_of(own),
        **scratch_of({name: kept[name] for name in READ}),
        **line_buffers(c),
    )


def backward_pass(c, weights, data, tables, stash):
    scratch = dict(
        **twice(c, backward_buffers(c), stage_sems(c) | dict(hid=pltpu.VMEM((c.r, c.width), BF))), **shared_scratch(c)
    )
    return launch(
        lambda o: backward_kernel(c, o),
        3,
        dict(**weights, cot=data.cot, lin=data.lin, **{name: stash[name] for name in READ}),
        tables,
        grad_shapes(c),
        scratch,
    )


def return_kernel(c, o):
    p = place(c.n)
    n, A, R, hb = c.n, c.n // 2, c.R, c.hb
    pair = (p.s, p.d, 1 - p.t)
    side = (p.s, p.a * 2 + 1 - p.b, p.t)
    barrier = pltpu.get_barrier_semaphore()

    def signal(device):
        pl.semaphore_signal(barrier, inc=1, device_id=device, device_id_type=MESH)

    for k in range(1, n):
        signal((p.s, lax.rem(p.d + k, n), p.t))
    signal(pair)
    pl.semaphore_wait(barrier, n)
    local = Local(o.lsem)
    ffn = (o.dg, o.du, o.dd)

    def swap(m, k):
        dest = lax.rem(p.d + k, n)
        return rcopy(
            ffn[m].at[rows_of(dest, R), rows_of(1 - p.t, hb)],
            o.fgot.at[m, rows_of(dest, R)],
            o.ys.at[m, k],
            o.yr.at[m, k],
            pair,
        )

    def ffn_out(m, source):
        return (o.gg, o.gu, o.gd)[m].at[:, rows_of(source, hb)]

    def trade(m, k):
        dest = lax.rem(p.d + k, n)
        return rcopy(
            o.fown.at[m, rows_of(dest, R)], ffn_out(m, p.d), o.ts.at[m, k], o.tr.at[m, k], (p.s, dest, p.t)
        )

    def came(m, k):
        source = lax.rem(p.d + n - k, n)
        return rcopy(o.fown.at[m, rows_of(p.d, R)], ffn_out(m, source), o.ts.at[m, k], o.tr.at[m, k], side)

    owns = [local(ffn[m].at[:, rows_of(p.t, hb)], o.fown.at[m]) for m in range(3)]
    order = [*range(1, n), 0]
    for m in range(3):
        for k in order:
            swap(m, k).start()
    need = [
        local(getattr(o, name), getattr(o, name + TAIL))
        for name in ("nfull", "dqkv", "afull", "heads", "lrlow", "lmid", "resid", "grlow", "plow", "llow", "lmg", "gcol")
    ]
    stage, last, finish = cube_scatter(p, o.acc, o.got, R, c.parts, (o.rs, o.rr), o.gp_v)
    mine_copies = []

    def grad(x, y, at, block=512):
        tokens = 2 * x.shape[1]

        @tiles(c.width, block)
        def _(rows):
            left = x[:, :, rows].reshape(tokens, block)
            o.acc[rows, at] = tn(left, y[...].reshape(tokens, y.shape[2])).astype(BF)

    def ffn_block(m, k):
        rows = rows_of(lax.rem(p.d + k, n), R)
        if k == order[0]:
            owns[m].wait()
        swap(m, k).wait_recv()
        total = o.fown[m, rows, :].astype(F32) + o.fgot[m, rows, :].astype(F32)
        o.fown[m, rows, :] = total.astype(BF)
        if k:
            trade(m, k).start()
        else:
            mine_copies.append(local(o.fown.at[m, rows], ffn_out(m, p.d)))

    def part_grad(h):
        begin, size = c.parts[h]
        base = c.qkv + c.heads
        if begin < c.qkv:
            grad(o.nfull_v, o.dqkv_v.at[:, :, pl.ds(begin, size)], pl.ds(begin, size))
        elif begin < base:
            grad(o.afull_v, o.heads_v.at[:, :, pl.ds(begin - c.qkv, size)], pl.ds(begin, size))
        elif begin == base:
            mine = rows_of(p.t, c.r)
            lane = lax.broadcasted_iota(jnp.int32, (512, LANES), 1)

            @tiles(c.width, 512)
            def _(rows):
                left = tn(o.nfull_v[0, mine, rows], o.lmg_v[0]) + tn(o.nfull_v[1, mine, rows], o.lmg_v[1])
                gains = o.gcol_v[rows, :].astype(F32)
                o.acc[rows, pl.ds(begin, LANES)] = jnp.where(lane < c.rank, left, gains).astype(BF)

            grad(o.lrlow_v, o.lmid_v, pl.ds(begin + LANES, LANES))
            o.rlow_v[...] = o.resid_v[...].astype(BF)
            grad(o.rlow_v, o.grlow_v, pl.ds(begin + 2 * LANES, c.per))
        else:
            grad(o.plow_v, o.llow_v, pl.ds(begin, c.per))

    for copy in need:
        copy.wait()
    events = []
    for m in range(3):
        for i, k in enumerate(order):
            events.append((c.kg[0] + c.kg[1] * (m * n + i), lambda m=m, k=k: ffn_block(m, k)))
    for h in range(len(c.parts)):
        events.append((c.kg[2] * h, lambda h=h: (part_grad(h), stage(h, 0))))
        for bit in range(1, lowest(0, n)):
            events.append((c.kg[3] + c.kg[4] * h + c.kg[5] * (bit - 1), lambda h=h, bit=bit: stage(h, bit)))
        events.append((c.kg[3] + c.kg[4] * h + c.kg[5] * (lowest(0, n) - 1), lambda h=h: last(h)))
    for _, run in sorted(events, key=lambda e: e[0]):
        run()
    shared = pl.ds(c.qkv + c.heads, c.small)
    o.ssend[...] = o.gp_v[:, shared].astype(BF)
    rest = rcopy(o.ssend, o.sgot, o.ss.at[0], o.sr.at[0], pair)
    rest.start()
    rest.wait()
    o.gp_v[:, shared] += o.sgot[...].astype(F32)
    out = local(o.gp_v, o.gp)
    for m in range(3):
        for k in range(n):
            swap(m, k).wait_send()
            if k:
                came(m, k).wait_recv()
                trade(m, k).wait_send()
    for q in range(len(c.parts)):
        finish(q)
    for copy in [*mine_copies, out]:
        copy.wait()


def fetch_weights(c, pack, gate, up, down):
    n, A, q = c.n, c.n // 2, len(c.cuts)
    outs = dict(
        pk=((c.width, c.total), BF),
        gw=((c.width, 2 * c.hb), BF),
        uw=((c.width, 2 * c.hb), BF),
        dw=((c.width, 2 * c.hb), BF),
        grow=((8, c.width), F32),
    )
    scratch = dict(
        gcol=pltpu.VMEM((c.width, LANES), BF),
        pack_v=pltpu.VMEM((c.R, c.total), BF),
        block_v=pltpu.VMEM((3, c.R, c.hb), BF),
        grow_v=pltpu.VMEM((8, c.width), F32),
        gs=dma(n, q), gr=dma(n, q),
        ts=dma(n, 3), tr=dma(n, 3), ys=dma(n, 3), yr=dma(n, 3), lsem=dma(12),
        go=pltpu.SemaphoreType.REGULAR,
    )
    return launch(
        lambda o: fetch_kernel(c, o), 6, dict(pack=pack, gate=gate, up=up, down=down), {}, outs, scratch
    )


def return_grads(c, f, g, gcol, dg, du, dd):
    n, A = c.n, c.n // 2
    R = c.R
    flat = ((R, n * c.hb), BF)
    outs = dict(gp=((R, c.total), F32), gg=flat, gu=flat, gd=flat)
    arrays = dict(
        nfull=f.nfull, dqkv=g.dqkv, afull=g.afull, heads=f.heads, lrlow=g.lrlow, lmid=f.lmid, resid=f.resid,
        grlow=g.grlow, plow=g.plow, llow=f.llow, lmg=g.lmg, gcol=gcol,
    )
    scratch = dict(
        acc=pltpu.VMEM((c.width, c.total), BF),
        got=pltpu.VMEM(((n - 1) * R, c.total), BF),
        gp_v=pltpu.VMEM((R, c.total), F32),
        fown=pltpu.VMEM((3, c.width, c.hb), BF),
        fgot=pltpu.VMEM((3, c.width, c.hb), BF),
        ssend=pltpu.VMEM((R, c.small), BF),
        sgot=pltpu.VMEM((R, c.small), BF),
        rlow_v=pltpu.VMEM(f.resid.shape, BF),
        ys=dma(3, n), yr=dma(3, n), ts=dma(3, n), tr=dma(3, n), ss=dma(1), sr=dma(1), lsem=dma(24),
        **{name + TAIL: pltpu.VMEM(v.shape, v.dtype) for name, v in arrays.items()},
        rs=dma(len(c.parts), n), rr=dma(len(c.parts), n),
    )
    return launch(lambda o: return_kernel(c, o), 7, dict(**arrays, dg=dg, du=du, dd=dd), {}, outs, scratch)


def widen_kernel(c, o):
    local = Local(o.lsem)
    loads = [local(o.gp, o.gp_v), local(o.gg, o.g_v.at[0]), local(o.gu, o.g_v.at[1]), local(o.gd, o.g_v.at[2])]
    base = c.qkv + c.heads
    loads[0].wait()
    out = [
        local(o.gp_v.at[:, pl.ds(0, c.heads)], o.q),
        local(o.gp_v.at[:, pl.ds(c.heads, HEAD)], o.k),
        local(o.gp_v.at[:, pl.ds(c.heads + HEAD, HEAD)], o.v),
        local(o.gp_v.at[:, pl.ds(base, LANES)], o.left),
        local(o.gp_v.at[:, pl.ds(base + 2 * LANES, c.per)], o.lg),
    ]
    o.t_v[...] = o.gp_v[:, pl.ds(c.qkv, c.heads)].T
    out.append(local(o.t_v, o.out))
    for m in range(3):
        loads[1 + m].wait()
        o.w_v[m] = o.g_v[m].astype(F32)
        out.append(local(o.w_v.at[m], (o.wg, o.wu, o.wd)[m]))
    for copy in out:
        copy.wait()


def widen(c, done):
    R, wide = c.R, c.n * c.hb
    outs = dict(
        q=((R, c.heads), F32), k=((R, HEAD), F32), v=((R, HEAD), F32), left=((R, LANES), F32), lg=((R, c.per), F32),
        out=((c.heads, R), F32), wg=((R, wide), F32), wu=((R, wide), F32), wd=((R, wide), F32),
    )
    scratch = dict(
        gp_v=pltpu.VMEM((R, c.total), F32), t_v=pltpu.VMEM((c.heads, R), F32),
        g_v=pltpu.VMEM((3, R, wide), BF), w_v=pltpu.VMEM((3, R, wide), F32), lsem=dma(16),
    )
    return launch(lambda o: widen_kernel(c, o), None, done, {}, outs, scratch)


def spread(gain, n, rows):
    return jnp.pad(gain, (0, rows - gain.shape[0]))


def body(
    hidden, layer_inputs, span_starts, cotangent, input_gain, query_weight, key_projection, value_projection,
    query_gain, key_norm_gain, output_weight, attention_gain, laurel_left, laurel_right, laurel_gain, prefeed_gain,
    gate_weight, up_weight, down_weight, postfeed_gain, layer_gate, layer_project, layer_gain,
):
    n, nt_ = lax.axis_size(D), lax.axis_size(T)
    t = lax.axis_index(T)
    rank = laurel_left.shape[2]
    width = hidden.shape[3]
    R = width // n
    heads = query_weight.shape[2]
    qkv = heads + 2 * HEAD
    per = layer_gate.shape[2]
    small = 2 * LANES + 2 * per
    base = qkv + heads
    c = SimpleNamespace(
        n=n, R=R, r=hidden.shape[2], width=width, heads=heads, qkv=qkv, per=per, small=small, rank=rank,
        total=qkv + heads + small, hb=gate_weight.shape[2] // n,
        cuts=((0, qkv), (qkv, heads), (qkv + heads, small)),
        parts=(*((i, 512) for i in range(0, qkv + heads, 512)), (base, small - per), (base + small - per, per)),
        slots=2 if n <= 8 else 1, ag=(12.0, 6.0, 12.0), tr=(1.0, 2.5, 30.0, 3.0), by_matrix=True, kg=(6.0, 2.9, 2.0, 20.0, 12.0, 12.0),
        halves=tuple((h * width // HALVES, width // HALVES) for h in range(HALVES)),
    )
    gains = jnp.stack(
        [
            input_gain[0], attention_gain[0], laurel_gain[0], prefeed_gain[0], postfeed_gain[0], layer_gain[0],
            spread(query_gain[0], n, R), spread(key_norm_gain[0], n, R),
        ],
        axis=1,
    )
    pad = lambda v, k: jnp.pad(v, ((0, 0), (0, LANES - k)))
    pack = jnp.concatenate(
        [
            query_weight[0], key_projection[0], value_projection[0], output_weight[0].T,
            pad(jnp.concatenate([laurel_left[0], gains], axis=1), rank + 8), pad(laurel_right[0].T, rank),
            layer_gate[0], layer_project[0].T,
        ],
        axis=1,
    )
    weights = fetch_weights(c, pack, gate_weight[0], up_weight[0], down_weight[0].T)
    columns = weights.pop("grow")
    short = HEAD // n
    head_gains = columns[6:].reshape(2, n, R)[:, :, :short].reshape(2, HEAD)
    gain_rows = jnp.concatenate([columns[:6], jnp.pad(head_gains, ((0, 0), (0, width - HEAD)))], axis=0)

    span = c.r * nt_
    position = jnp.arange(span, dtype=jnp.int32)
    begin = span_starts[:, 0][:, None]
    inside = (position[None] >= begin) & (position[None] < begin + IMG)
    allowed = (position[None, :] <= position[:, None])[None] | (inside[:, :, None] & inside[:, None, :])
    half = HEAD // 2
    frequency = jnp.exp(jnp.arange(half, dtype=F32) * (-2.0 * math.log(10000.0) / HEAD))
    angles = jnp.arange(span, dtype=F32)[:, None] * frequency[None, :]
    tables = dict(gains=gain_rows, cos=jnp.cos(angles), sin=jnp.sin(angles), allowed=allowed.astype(F32))
    data = SimpleNamespace(hidden=hidden[:, 0], lin=layer_inputs[0, :, 0], cot=cotangent[:, 0])

    stash = forward_pass(c, weights, data, tables)
    grads = backward_pass(c, weights, data, tables, stash)
    f, g = SimpleNamespace(**stash), SimpleNamespace(**grads)

    def pair_grad(inputs, outs):
        inputs = inputs.reshape(-1, inputs.shape[-1])
        return tn(inputs, outs.reshape(-1, outs.shape[-1])).astype(BF)

    sums = g.ggr[0] + g.ggr[1]
    head_sums = jnp.pad(sums[6:, :HEAD].reshape(2, n, short), ((0, 0), (0, 0), (0, R - short))).reshape(2, width)
    gain_cols = jnp.concatenate([sums[:6], head_sums], axis=0).T
    gcol = jnp.pad(gain_cols, ((0, 0), (rank, LANES - rank - 8))).astype(BF)
    done = return_grads(
        c, f, g, gcol, pair_grad(f.pfull, g.dgl), pair_grad(f.pfull, g.dul), pair_grad(g.dfull, f.geglu)
    )
    w = SimpleNamespace(**widen(c, done))
    gp = done["gp"]
    base = qkv + heads
    gain_out = w.left[:, rank : rank + 8].T
    one = lambda i: gain_out[i][None]
    return (
        f.act[None, :, None],
        g.igrad[None, :, None],
        g.lgrad[None, :, None],
        one(0),
        w.q[None],
        w.k[None],
        w.v[None],
        gain_out[6, :short][None],
        gain_out[7, :short][None],
        w.out[None],
        one(1),
        w.left[:, :rank][None],
        gp[:, base + LANES : base + LANES + rank].T[None],
        one(2),
        one(3),
        w.wg[None],
        w.wu[None],
        w.wd.T[None],
        one(4),
        w.lg[None],
        gp[:, base + 2 * LANES + per :].T[None],
        one(5),
    )


def solution(mesh):
    rows, cols = P(S, D, T), P(S, T, D)
    vec, tall, flat = P(S, D), P(S, D, None), P(S, None, D)
    seq, out = P(None, D, T, None), P(S, None, D, T, None)
    weights = (
        vec, rows, rows, rows, vec, vec, cols, vec, tall, flat, vec, vec, rows, rows, cols, vec, tall, flat, vec,
    )
    return jax.shard_map(
        body,
        mesh=mesh,
        in_specs=(seq, out, P(None, D), seq, *weights),
        out_specs=(out, out, out, *weights),
        check_vma=False,
    )
```

```python
import math
from types import SimpleNamespace

import jax
import jax.numpy as jnp
from jax import lax
from jax.experimental import pallas as pl
from jax.experimental.pallas import tpu as pltpu
from jax.sharding import PartitionSpec as P

S, D, T = "section", "dp", "tensor"
MESH = pl.DeviceIdType.MESH
BF, F32 = jnp.bfloat16, jnp.float32
HEAD = 256
IMG = 64
EPS = 1e-06
RH = 0.5**0.5
NEG = -1e30
LANES = 128
GELU_C = math.sqrt(2.0 / math.pi)
GELU_K = 0.044715
VMEM_LIMIT = 61 << 20
HALVES = 2
GATHER_PARTS = 2
GO_AT = 60.0
KG = (2.5, 3.0, (2.1, 3.2, 4.3), 0.6, 2.6)


def rms_of(v):
    return lax.rsqrt(jnp.mean(v * v, axis=-1, keepdims=True) + EPS)


def rms_back(v, gain, grad):
    r = rms_of(v)
    unit = v * r
    inner = grad * gain
    back = r * (inner - unit * jnp.mean(inner * unit, axis=-1, keepdims=True))
    return back, jnp.sum(grad * unit, axis=0, keepdims=True)


def plain_back(v, grad):
    r = rms_of(v)
    unit = v * r
    return r * (grad - unit * jnp.mean(grad * unit, axis=-1, keepdims=True))


def gelu(v):
    return 0.5 * v * (1.0 + jnp.tanh(GELU_C * (v + GELU_K * v * v * v)))


def gelu_both(v):
    square = v * v
    th = jnp.tanh(GELU_C * v * (1.0 + GELU_K * square))
    value = 0.5 * v * (1.0 + th)
    slope = 0.5 * (1.0 + th) + 0.5 * v * (1.0 - th * th) * GELU_C * (1.0 + 3.0 * GELU_K * square)
    return value, slope


def rotate(v, cos, sin):
    half = HEAD // 2
    front, back = v[:, :half], v[:, half:]
    return jnp.concatenate([front * cos - back * sin, back * cos + front * sin], axis=-1)


def rotate_back(g, cos, sin):
    half = HEAD // 2
    front, back = g[:, :half], g[:, half:]
    return jnp.concatenate([front * cos + back * sin, back * cos - front * sin], axis=-1)


def nn(x, w):
    return jnp.dot(x, w, preferred_element_type=F32)


def nt(x, w):
    return lax.dot_general(x, w, (((1,), (1,)), ((), ())), preferred_element_type=F32)


def tn(x, w):
    return lax.dot_general(x, w, (((0,), (0,)), ((), ())), preferred_element_type=F32)


def tiles(count, step):
    def wrap(fn):
        def one(j, carry):
            fn(pl.ds(pl.multiple_of(j * step, step), step))
            return carry

        lax.fori_loop(0, count // step, one, 0)

    return wrap


def place(n):
    s, d, t = lax.axis_index(S), lax.axis_index(D), lax.axis_index(T)
    return SimpleNamespace(s=s, d=d, t=t, a=lax.div(d, 2), b=lax.rem(d, 2), n=n, A=n // 2)


def rcopy(src, dst, send, recv, device):
    return pltpu.make_async_remote_copy(
        src_ref=src, dst_ref=dst, send_sem=send, recv_sem=recv, device_id=device, device_id_type=MESH
    )


def rows_of(index, size):
    return pl.ds(pl.multiple_of(index * size, size), size)


class Local:
    def __init__(self, sems):
        self.sems, self.used = sems, 0

    def __call__(self, src, dst):
        copy = pltpu.make_async_copy(src, dst, self.sems.at[self.used])
        self.used += 1
        copy.start()
        return copy


def steps_of(p, fn, far_first=False):
    for delta in range(p.A - 1, 0, -1) if far_first else range(1, p.A):
        pl.when(p.a - delta >= 0)(lambda: fn(p.a - delta))
        pl.when(p.a + delta < p.A)(lambda: fn(p.a + delta))


def line_gather(p, buf, size, sems):
    zs, zr, xs, xr = sems
    side = (p.s, p.a * 2 + 1 - p.b, p.t)
    part = size // GATHER_PARTS

    def at(col, row, g):
        return buf.at[col, pl.ds(pl.multiple_of(row * size + g * part, part), part)]

    def along(row, g):
        return rcopy(at(p.b, p.a, g), at(p.b, p.a, g), zs.at[row, g], zr.at[p.a, g], (p.s, row * 2 + p.b, p.t))

    def came(row, g):
        return rcopy(at(p.b, row, g), at(p.b, row, g), zs.at[row, g], zr.at[row, g], side)

    def across(col, row, g):
        return rcopy(at(col, row, g), at(col, row, g), xs.at[row, g], xr.at[row, g], side)

    def each(fn):
        def run(row):
            for g in range(GATHER_PARTS):
                fn(row, g)

        return run

    for g in range(GATHER_PARTS):
        steps_of(p, lambda row: along(row, g).start(), True)
        across(p.b, p.a, g).start()

    def forward(row, g):
        came(row, g).wait_recv()
        across(p.b, row, g).start()

    def arrive():
        for row in range(p.A):
            each(lambda row, g: across(1 - p.b, row, g).wait_recv())(row)

    def finish():
        steps_of(p, each(lambda row, g: along(row, g).wait_send()))
        for row in range(p.A):
            each(lambda row, g: across(p.b, row, g).wait_send())(row)

    return lambda: steps_of(p, each(forward)), arrive, finish


def line_scatter(p, acc, other, got, step_got, size, cuts, sems, out):
    xs, xr, zs, zr = sems
    side = (p.s, p.a * 2 + 1 - p.b, p.t)

    def part(row, h):
        return (rows_of(row, size), pl.ds(cuts[h][0], cuts[h][1]))

    def across(h, row):
        at = part(row, h)
        return rcopy(other.at[at], got.at[at], xs.at[h, row], xr.at[h, row], side)

    def along(h, row):
        return rcopy(
            other.at[part(row, h)], step_got.at[part(p.a, h)], zs.at[h, row], zr.at[h, p.a], (p.s, row * 2 + p.b, p.t)
        )

    def came(h, row):
        return rcopy(other.at[part(row, h)], step_got.at[part(row, h)], zs.at[h, row], zr.at[h, row], side)

    def start(h):
        steps_of(p, lambda row: across(h, row).start(), True)
        across(h, p.a).start()

    def carry(h):
        def pass_on(row):
            at = part(row, h)
            across(h, row).wait()
            other[at] = (acc[at] + got[at].astype(F32)).astype(BF)
            along(h, row).start()

        steps_of(p, pass_on, True)

    def collect(h):
        across(h, p.a).wait()
        at = part(p.a, h)
        cols = (slice(None), at[1])
        out[cols] = acc[at] + got[at].astype(F32)

        def add(row):
            came(h, row).wait_recv()
            out[cols] += step_got[part(row, h)].astype(F32)

        steps_of(p, add)

    def finish(h):
        steps_of(p, lambda row: along(h, row).wait_send())

    return start, carry, collect, finish


def lowest(mask, n):
    bit = 0
    while (1 << bit) < n and not mask >> bit & 1:
        bit += 1
    return bit


def flip(d, mask):
    bit = 0
    result = d
    while 1 << bit <= mask:
        if mask >> bit & 1:
            result = result + (1 - 2 * lax.rem(lax.div(d, 1 << bit), 2)) * (1 << bit)
        bit += 1
    return result


def cube_scatter(p, acc, got, size, cuts, sems, out):
    send, recv = sems
    n = p.n

    def cols(h):
        return pl.ds(cuts[h][0], cuts[h][1])

    def block(mask):
        return rows_of(flip(p.d, mask), size)

    def message(h, mask):
        bit = lowest(mask, n)
        return rcopy(
            acc.at[block(mask), cols(h)],
            got.at[pl.ds((mask - 1) * size, size), cols(h)],
            send.at[h, mask],
            recv.at[h, mask],
            (p.s, flip(p.d, 1 << bit), p.t),
        )

    def stage(h, bit):
        for mask in range(1, n):
            if lowest(mask, n) == bit:
                at = (block(mask), cols(h))
                total = None
                for below in range(bit):
                    came = mask | 1 << below
                    message(h, came).wait_recv()
                    term = got[pl.ds((came - 1) * size, size), cols(h)].astype(F32)
                    total = term if total is None else total + term
                if total is not None:
                    acc[at] = (acc[at].astype(F32) + total).astype(BF)
                message(h, mask).start()

    def last(h):
        total = acc[block(0), cols(h)].astype(F32)
        for below in range(lowest(0, n)):
            message(h, 1 << below).wait_recv()
            total = total + got[pl.ds(((1 << below) - 1) * size, size), cols(h)].astype(F32)
        out[:, cols(h)] = total.astype(BF)

    def finish(h):
        for mask in range(1, n):
            message(h, mask).wait_send()

    return stage, last, finish


def dma(*shape):
    return pltpu.SemaphoreType.DMA(shape)


def gather_sems(A):
    g = GATHER_PARTS
    return dict(gzs=dma(A, g), gzr=dma(A, g), gxs=dma(A, g), gxr=dma(A, g))


def scatter_sems(A, parts):
    return dict(rxs=dma(parts, A), rxr=dma(parts, A), rzs=dma(parts, A), rzr=dma(parts, A))


HBM = pl.BlockSpec(memory_space=pltpu.HBM)
VM = pl.BlockSpec(memory_space=pltpu.VMEM)


def launch(kernel, cid, hbm_in, vmem_in, outs, scratch, small=None):
    small = small or {}
    everything = [*hbm_in, *vmem_in, *outs, *small, *scratch]

    def run(*refs):
        kernel(SimpleNamespace(**dict(zip(everything, refs))))

    results = pl.pallas_call(
        run,
        out_shape=[jax.ShapeDtypeStruct(*spec) for spec in (*outs.values(), *small.values())],
        in_specs=[HBM] * len(hbm_in) + [VM] * len(vmem_in),
        out_specs=[HBM] * len(outs) + [VM] * len(small),
        scratch_shapes=list(scratch.values()),
        compiler_params=pltpu.CompilerParams(
            collective_id=cid, has_side_effects=cid is not None, vmem_limit_bytes=VMEM_LIMIT
        ),
    )(*hbm_in.values(), *vmem_in.values())
    return dict(zip((*outs, *small), results))


def fetch_kernel(c, o):
    p = place(c.n)
    n, A, R, hb = c.n, c.n // 2, c.R, c.hb
    barrier = pltpu.get_barrier_semaphore()

    def signal(device):
        pl.semaphore_signal(barrier, inc=1, device_id=device, device_id_type=MESH)

    for k in range(1, n):
        signal((p.s, lax.rem(p.d + k, n), p.t))
    signal((p.s, p.d, 1 - p.t))
    signal((1 - p.s, p.d, p.t))
    pl.semaphore_wait(barrier, n + 1)

    @pl.when(p.s == 1)
    def _():
        pl.semaphore_wait(o.go, 1)

    side = (p.s, p.a * 2 + 1 - p.b, p.t)
    pair = (p.s, p.d, 1 - p.t)
    cuts = c.cuts
    bits = lowest(0, n)
    local = Local(o.lsem)
    waits = []

    def give(mask, bit, q):
        rows, cs = rows_of(flip(p.d, mask), R), pl.ds(*cuts[q])
        src = o.pk.at[rows, cs] if mask else o.pack_v.at[:, cs]
        far = mask | 1 << bit
        return rcopy(src, o.pk.at[rows, cs], o.gs.at[far, q], o.gr.at[far, q], (p.s, flip(p.d, 1 << bit), p.t))

    def taken(mask, q):
        at = (rows_of(flip(p.d, mask), R), pl.ds(*cuts[q]))
        return rcopy(o.pk.at[at], o.pk.at[at], o.gs.at[mask, q], o.gr.at[mask, q], side)

    def pass_on(mask, q):
        if mask:
            taken(mask, q).wait_recv()
        for bit in reversed(range(lowest(mask, n))):
            give(mask, bit, q).start()

    ffn = ((o.gate, o.gw), (o.up, o.uw), (o.down_t, o.dw))

    def block(m, source, half):
        return ffn[m][1].at[rows_of(source, R), rows_of(half, hb)]

    def trade(m, k):
        dest = lax.rem(p.d + k, n)
        return rcopy(
            ffn[m][0].at[:, rows_of(dest, hb)], block(m, p.d, p.t), o.ts.at[k, m], o.tr.at[k, m], (p.s, dest, p.t)
        )

    def came(m, k):
        source = lax.rem(p.d + n - k, n)
        return rcopy(
            ffn[m][0].at[:, rows_of(p.d, hb)], block(m, source, p.t), o.ts.at[k, m], o.tr.at[k, m], side
        )

    def share(m, k, half):
        source = lax.rem(p.d + n - k, n)
        src = ffn[m][0].at[:, rows_of(p.d, hb)] if k == 0 else block(m, source, half)
        return rcopy(src, block(m, source, half), o.ys.at[k, m], o.yr.at[k, m], pair)

    qkv, base, rank = c.qkv, c.qkv + c.heads, c.rank
    first = [
        local(o.query, o.pack_v.at[:, pl.ds(0, c.heads)]),
        local(o.key, o.pack_v.at[:, pl.ds(c.heads, HEAD)]),
        local(o.value, o.pack_v.at[:, pl.ds(c.heads + HEAD, HEAD)]),
    ]
    second = [local(o.out, o.out_v)]
    third = [local(o.lg, o.pack_v.at[:, pl.ds(base + 2 * LANES, c.per)]), local(o.lp, o.lp_v), local(o.lr, o.lr_v)]
    fourth = [local(o.down, o.down_v)]
    bounce = [local(ffn[m][0].at[:, rows_of(p.d, hb)], o.block_v.at[m]) for m in range(2)]

    def turned(x):
        return x.astype(F32).T.astype(BF)

    def prepare(q):
        if q == 0:
            for copy in first:
                copy.wait()
        elif q == 1:
            for copy in second:
                copy.wait()
            for i in range(0, c.heads, HEAD):
                o.pack_v[:, pl.ds(qkv + i, HEAD)] = turned(o.out_v[pl.ds(i, HEAD), :])
        else:
            for copy in third:
                copy.wait()
            o.rows_v[...] = jnp.zeros_like(o.rows_v)
            for i, gain in enumerate((o.g0, o.g1, o.g2, o.g3, o.g4, o.g5, o.g6, o.g7)):
                o.rows_v[rank + i : rank + i + 1, 0 : gain.shape[1]] = gain[...].astype(F32)
            left = o.rows_v[...].T
            o.pack_v[:, pl.ds(base, LANES)] = left.astype(BF)
            o.pack_v[:, pl.ds(base, rank)] = o.ll[...]
            o.rows_v[...] = jnp.zeros_like(o.rows_v)
            o.rows_v[0:rank, :] = o.lr_v[...].astype(F32)
            o.pack_v[:, pl.ds(base + LANES, LANES)] = o.rows_v[...].T.astype(BF)
            o.pack_v[:, pl.ds(base + 2 * LANES + c.per, c.per)] = turned(o.lp_v[...])

    def prepare_down():
        for copy in fourth:
            copy.wait()
        for k in range(n):
            o.down_t[:, pl.ds(k * hb, hb)] = turned(o.down_v[pl.ds(k * hb, hb), :])
        bounce.append(local(o.down_t.at[:, rows_of(p.d, hb)], o.block_v.at[2]))

    events = []
    inner = sorted((mask for mask in range(2, n, 2)), key=lambda mask: (-lowest(mask, n), mask))
    for q in range(len(cuts)):
        events.append((0.0 + 0.1 * q, lambda q=q: (prepare(q), pass_on(0, q))))
        for i, mask in enumerate(inner):
            events.append((c.ag[0] + c.ag[1] * q + c.ag[2] * i, lambda q=q, mask=mask: pass_on(mask, q)))
    events.append((c.tr[0] + c.tr[1] * (2 * n - 2), prepare_down))
    for k in range(n):
        for m in range(3):
            at = m * n + k
            if k:
                events.append((c.tr[0] + c.tr[1] * at, lambda m=m, k=k: trade(m, k).start()))
                events.append((c.tr[2] + c.tr[3] * at, lambda m=m, k=k: (came(m, k).wait_recv(), share(m, k, p.t).start())))
            else:
                events.append((c.tr[0] + c.tr[1] * at, lambda m=m: share(m, 0, p.t).start()))
    def release():
        pl.semaphore_signal(o.go, inc=1, device_id=(1 - p.s, p.d, p.t), device_id_type=MESH)

    events.append((c.go_at, lambda: pl.when(p.s == 0)(release)))
    for _, run in sorted(events, key=lambda e: e[0]):
        run()
    for copy in bounce:
        copy.wait()
    waits.append(local(o.pack_v, o.pk.at[rows_of(p.d, R)]))
    for m in range(3):
        waits.append(local(o.block_v.at[m], block(m, p.d, p.t)))

    for q in range(len(cuts)):
        for mask in range(1, n, 2):
            taken(mask, q).wait_recv()
    for k in range(n):
        for m in range(3):
            share(m, k, 1 - p.t).wait_recv()
    for q in range(len(cuts)):
        for mask in range(0, n, 2):
            for bit in range(lowest(mask, n)):
                give(mask, bit, q).wait_send()
    for k in range(n):
        for m in range(3):
            if k:
                trade(m, k).wait_send()
            share(m, k, p.t).wait_send()
    for copy in waits:
        copy.wait()
    last = local(o.pk.at[:, pl.ds(c.qkv + c.heads, LANES)], o.gcol)
    last.wait()
    o.grow_v[...] = o.gcol[...].astype(F32).T[c.rank : c.rank + 8]
    last = local(o.grow_v, o.grow)
    last.wait()


def load_weights(c, o, local):
    qn, on = c.qkv, c.heads
    got = [
        local(o.pk.at[:, pl.ds(qn + on, c.small)], o.sm_v),
        local(o.pk.at[:, pl.ds(0, qn)], o.qkv_v),
        local(o.pk.at[:, pl.ds(qn, on)], o.ot_v),
        local(o.gw, o.gw_v),
        local(o.uw, o.uw_v),
        local(o.dw, o.dw_v),
    ]
    return SimpleNamespace(sm=got[0], qkv=got[1], ot=got[2], gw=got[3], uw=got[4], dw=got[5])


def weight_scratch(c):
    return dict(
        sm_v=pltpu.VMEM((c.width, c.small), BF),
        qkv_v=pltpu.VMEM((c.width, c.qkv), BF),
        ot_v=pltpu.VMEM((c.width, c.heads), BF),
        gw_v=pltpu.VMEM((c.width, 2 * c.hb), BF),
        uw_v=pltpu.VMEM((c.width, 2 * c.hb), BF),
        dw_v=pltpu.VMEM((c.width, 2 * c.hb), BF),
    )


LL, LR, LG, LP = (0, 128), (128, 128), (256, 256), (512, 256)


def cols_of(cut):
    return (slice(None), pl.ds(*cut))


def enter(p, o, sender):
    barrier = pltpu.get_barrier_semaphore()

    def signal(device):
        pl.semaphore_signal(barrier, inc=1, device_id=device, device_id_type=MESH)

    partner = (1 - p.s, p.d, p.t)
    pl.when(p.s == sender)(lambda: signal(partner))
    line_greet(p, signal)
    line = p.A + 1
    pl.semaphore_wait(barrier, jnp.where(p.s == sender, line, line + 1))

    @pl.when(p.s == 1 - sender)
    def _():
        pl.semaphore_signal(o.ready, inc=1, device_id=partner, device_id_type=MESH)


def line_greet(p, signal):
    signal((p.s, p.d, 1 - p.t))
    signal((p.s, p.a * 2 + 1 - p.b, p.t))
    steps_of(p, lambda row: signal((p.s, row * 2 + p.b, p.t)))


def again(p):
    barrier = pltpu.get_barrier_semaphore()
    line_greet(p, lambda device: pl.semaphore_signal(barrier, inc=1, device_id=device, device_id_type=MESH))
    pl.semaphore_wait(barrier, p.A + 1)


def view(c, o, m, buffers, sems):
    slot = m if c.slots == 2 else 0
    names = {name: getattr(o, name + str(slot)) for name in buffers}
    names.update({name: getattr(o, name + str(m)) for name in sems})
    return SimpleNamespace(**names)


def twice(c, buffers, sems):
    out = {}
    for slot in range(c.slots):
        out.update({name + str(slot): spec for name, spec in buffers.items()})
    for m in range(2):
        out.update({name + str(m): spec for name, spec in sems.items()})
    return out


def run_stages(c, p, order, stages):
    if c.slots == 1:
        order = [item for m in range(2) for item in order if item[1] == m]
    for name, m in order:
        if c.slots == 1 and name == FIRST and m == 1:
            stages[0][LAST]()
            again(p)
        stages[m][name]()
    for m in range(2) if c.slots == 2 else (1,):
        stages[m][LAST]()


FIRST, GIVE, OWN, REST, SUMS, PASS, LAST = range(7)
BEGIN, PROJ, JOIN, TAIL_STAGE, MIDDLE, HEADS_STAGE, ENTRY = range(10, 17)


def line_stages(c, p, v, hidden_part, down_part, ready):
    start, carry, collect, finish = line_scatter(
        p, v.acc, v.other, v.got, v.step_got, c.r, c.halves, (v.rxs, v.rxr, v.rzs, v.rzr), v.down_v
    )
    link = SimpleNamespace()

    def begin():
        link.forward, link.arrive, link.gathered = line_gather(p, v.xbuf, c.r, (v.gzs, v.gzr, v.gxs, v.gxr))

    def own():
        ready(0)
        hidden_part(p.b)

    def rest():
        link.arrive()
        hidden_part(1 - p.b)
        ready(1)
        for h in range(HALVES):
            down_part(1 - p.b, v.other, h)
            start(h)
        for h in range(HALVES):
            down_part(p.b, v.acc, h)

    def sums():
        for h in range(HALVES):
            carry(h)

    def total():
        for h in range(HALVES):
            collect(h)

    def end():
        link.gathered()
        for h in range(HALVES):
            finish(h)

    return SimpleNamespace(begin=begin, give=lambda: link.forward(), own=own, rest=rest, sums=sums, total=total, end=end)


def once(*copies):
    state = [False]

    def run():
        if not state[0]:
            state[0] = True
            for copy in copies:
                copy.wait()

    return run


def forward_stages(c, p, o, v, m, w, local):
    r, width, hb2 = c.r, c.width, 2 * c.hb
    pair = (p.s, p.d, 1 - p.t)
    mine, theirs = rows_of(p.t, r), rows_of(1 - p.t, r)
    gain = lambda i: o.gains[i : i + 1, :]
    hand = rcopy(v.act_v, v.hid, v.hs.at[0], v.hr.at[0], (1 - p.s, p.d, p.t))
    first = pltpu.make_async_copy(o.hidden.at[m], v.hid, v.fsem.at[0])
    send = rcopy(v.nbuf.at[mine], v.nbuf.at[mine], v.ys.at[0], v.yr.at[0], pair)
    swap = rcopy(v.ysend, v.ygot, v.ys.at[1], v.yr.at[1], pair)
    keep = []

    def stash(*pairs):
        keep.extend(local(src, dst.at[m]) for src, dst in pairs)

    def normed_of():
        x = v.hid[...].astype(F32)
        return x, x * rms_of(x) * gain(0)

    def begin():
        lv = local(o.lin.at[m], v.lv)
        v.lv_wait = lv.wait

        @pl.when(p.s == 0)
        def _():
            first.start()
            first.wait()

        pl.when(p.s == 1)(hand.wait_recv)
        v.nbuf[mine, :] = normed_of()[1].astype(BF)
        send.start()
        w.sm()
        lane = lax.broadcasted_iota(jnp.int32, (r, LANES), 1)
        mid = jnp.where(lane < c.rank, nn(v.nbuf[mine, :], o.sm_v[cols_of(LL)]), 0.0)
        v.lmid_v[...] = mid.astype(BF)
        v.lraw_v[...] = nt(v.lmid_v[...], o.sm_v[cols_of(LR)])
        stash((v.hid, o.xlow), (v.lmid_v, o.lmid), (v.lraw_v, o.lraw))

    def proj():
        w.qkv()
        rcopy(v.nbuf.at[theirs], v.nbuf.at[theirs], v.ys.at[0], v.yr.at[0], pair).wait_recv()

        @tiles(c.qkv, 256)
        def _(at):
            v.qraw_v[:, at] = nn(v.nbuf[...], o.qkv_v[:, at])

        cos, sin = o.cos[...], o.sin[...]
        q_gain, k_gain = o.gains[6:7, 0:HEAD], o.gains[7:8, 0:HEAD]
        allowed = o.allowed[m] > 0.5
        kraw = v.qraw_v[:, pl.ds(c.heads, HEAD)]
        vraw = v.qraw_v[:, pl.ds(c.heads + HEAD, HEAD)]
        key = rotate(kraw * rms_of(kraw) * k_gain, cos, sin).astype(BF)
        value = (vraw * rms_of(vraw)).astype(BF)
        for h in range(c.heads // HEAD):
            at = pl.ds(h * HEAD, HEAD)
            raw = v.qraw_v[:, at]
            query = rotate(raw * rms_of(raw) * q_gain, cos, sin).astype(BF)
            scores = jnp.where(allowed, nt(query, key) * HEAD**-0.5, NEG)
            shifted = jnp.exp(scores - jnp.max(scores, axis=-1, keepdims=True))
            prob = shifted / jnp.sum(shifted, axis=-1, keepdims=True)
            v.heads_v[:, at] = nn(prob.astype(BF), value).astype(BF)
        w.ot()

        @tiles(width, 256)
        def _(at):
            v.acc[0 : 2 * r, at] = nt(v.heads_v[...], o.ot_v[at, :])

        v.ysend[...] = v.acc[theirs, :].astype(BF)
        swap.start()
        stash((v.nbuf, o.nfull), (v.qraw_v, o.qraw), (v.heads_v, o.heads))

    def join():
        x, normed = normed_of()
        swap.wait()
        att = v.acc[mine, :] + v.ygot[...].astype(F32)
        v.att_v[...] = att
        lraw = v.lraw_v[...]
        comb = (x + att * rms_of(att) * gain(1) + normed + lraw * rms_of(lraw) * gain(2)) * RH
        v.comb_v[...] = comb
        v.xbuf[p.b, rows_of(p.a, r), :] = (comb * rms_of(comb) * gain(3)).astype(BF)
        line.begin()
        stash((v.att_v, o.att), (v.comb_v, o.comb))

    def hidden_part(col):
        @tiles(hb2, min(256, hb2))
        def _(at):
            gate = nn(v.xbuf[col], o.gw_v[:, at])
            up = nn(v.xbuf[col], o.uw_v[:, at])
            v.gate_v[col, :, at] = gate.astype(BF)
            v.up_v[col, :, at] = up.astype(BF)
            v.geglu_v[col, :, at] = (gelu(gate) * up).astype(BF)

    def down_part(col, dest, h):
        start, size = c.halves[h]

        @tiles(size, 256)
        def _(at):
            at = pl.ds(pl.multiple_of(start + at.start, 256), 256)
            dest[:, at] = nt(v.geglu_v[col], o.dw_v[at, :]).astype(dest.dtype)

    def ready(i):
        if i == 0:
            w.gw()
            w.uw()
        else:
            w.dw()

    line = line_stages(c, p, v, hidden_part, down_part, ready)

    def rest():
        line.rest()
        stash((v.xbuf, o.pfull), (v.gate_v, o.gate), (v.up_v, o.up), (v.geglu_v, o.geglu))

    def tail():
        line.total()
        down = v.down_v[...]
        resid = v.comb_v[...] + down * rms_of(down) * gain(4)
        v.rf_v[...] = resid
        v.resid_v[...] = resid.astype(BF)
        graw = nn(v.resid_v[...], o.sm_v[cols_of(LG)])
        v.graw_v[...] = graw
        v.lv_wait()
        v.llow_v[...] = (gelu(graw) * v.lv[...].astype(F32)).astype(BF)
        proj = nt(v.llow_v[...], o.sm_v[cols_of(LP)])
        v.proj_v[...] = proj
        v.act_v[...] = (v.rf_v[...] + proj * rms_of(proj) * gain(5)).astype(BF)

        @pl.when(p.s == 0)
        def _():
            if m == 0:
                pl.semaphore_wait(o.ready, 1)
            hand.start()

        stash((v.down_v, o.down), (v.resid_v, o.resid), (v.graw_v, o.graw), (v.llow_v, o.llow), (v.proj_v, o.proj))
        stash((v.act_v, o.act))

    def end():
        send.wait_send()
        line.end()
        pl.when(p.s == 0)(hand.wait_send)
        for copy in keep:
            copy.wait()

    return {
        FIRST: begin, PROJ: proj, JOIN: join, GIVE: line.give, OWN: line.own, REST: rest, SUMS: line.sums,
        TAIL_STAGE: tail, LAST: end,
    }


FORWARD_ORDER = (
    (FIRST, 0), (PROJ, 0), (JOIN, 0), (FIRST, 1), (PROJ, 1), (GIVE, 0), (JOIN, 1), (OWN, 0), (GIVE, 1), (REST, 0),
    (OWN, 1), (SUMS, 0), (REST, 1), (TAIL_STAGE, 0), (SUMS, 1), (TAIL_STAGE, 1),
)


def waits_of(c, o, local):
    got = load_weights(c, o, local)
    return SimpleNamespace(**{name: once(copy) for name, copy in vars(got).items()})


def forward_kernel(c, o):
    p = place(c.n)
    local = Local(o.lsem)
    w = waits_of(c, o, local)
    enter(p, o, 0)
    views = [view(c, o, m, forward_buffers(c), stage_sems(c) | dict(hid=None)) for m in range(2)]
    stages = [forward_stages(c, p, o, views[m], m, w, local) for m in range(2)]
    run_stages(c, p, FORWARD_ORDER, stages)


def stash_shapes(c):
    m, r, w, q = 2, c.r, c.width, 2 * c.r
    ar, hb2 = c.n // 2 * c.r, 2 * c.hb
    return dict(
        act=((m, r, w), BF),
        xlow=((m, r, w), BF),
        nfull=((m, q, w), BF),
        qraw=((m, q, c.qkv), F32),
        heads=((m, q, c.heads), BF),
        att=((m, r, w), F32),
        lmid=((m, r, LANES), BF),
        lraw=((m, r, w), F32),
        comb=((m, r, w), F32),
        pfull=((m, 2, ar, w), BF),
        gate=((m, 2, ar, hb2), BF),
        up=((m, 2, ar, hb2), BF),
        geglu=((m, 2, ar, hb2), BF),
        down=((m, r, w), F32),
        resid=((m, r, w), BF),
        graw=((m, r, c.per), F32),
        llow=((m, r, c.per), BF),
        proj=((m, r, w), F32),
    )


TAIL = "_v"
GROW = "grow"


def scratch_of(shapes):
    return {name + TAIL: pltpu.VMEM(shape[1:], kind) for name, (shape, kind) in shapes.items()}


def line_buffers(c):
    ar = c.n // 2 * c.r
    return dict(
        xbuf=pltpu.VMEM((2, ar, c.width), BF),
        acc=pltpu.VMEM((ar, c.width), F32),
        other=pltpu.VMEM((ar, c.width), BF),
        got=pltpu.VMEM((ar, c.width), BF),
        step_got=pltpu.VMEM((ar, c.width), BF),
        ysend=pltpu.VMEM((c.r, c.width), BF),
        ygot=pltpu.VMEM((c.r, c.width), BF),
        lv=pltpu.VMEM((c.r, c.per), BF),
    )


def stage_sems(c):
    return dict(
        fsem=dma(1), hs=dma(1), hr=dma(1), ys=dma(2), yr=dma(2), **gather_sems(c.n // 2), **scatter_sems(c.n // 2, HALVES)
    )


def forward_buffers(c):
    shapes = stash_shapes(c)
    own = {name: shapes[name] for name in shapes if name not in ("xlow", "nfull", "pfull")}
    return dict(nbuf=pltpu.VMEM((2 * c.r, c.width), BF), rf_v=pltpu.VMEM((c.r, c.width), F32), **scratch_of(own), **line_buffers(c))


def shared_scratch(c):
    return dict(**weight_scratch(c), lsem=dma(80), ready=pltpu.SemaphoreType.REGULAR)


def forward_pass(c, weights, data, tables):
    scratch = dict(
        **twice(c, forward_buffers(c), stage_sems(c) | dict(hid=pltpu.VMEM((c.r, c.width), BF))), **shared_scratch(c)
    )
    return launch(
        lambda o: forward_kernel(c, o),
        0,
        dict(**weights, hidden=data.hidden, lin=data.lin),
        tables,
        stash_shapes(c),
        scratch,
    )


def backward_stages(c, p, o, v, m, w, local):
    r, width, hb2 = c.r, c.width, 2 * c.hb
    pair = (p.s, p.d, 1 - p.t)
    mine, theirs = rows_of(p.t, r), rows_of(1 - p.t, r)
    gain = lambda i: o.gains[i : i + 1, :]
    hand = rcopy(v.hid, v.hid, v.hs.at[0], v.hr.at[0], (1 - p.s, p.d, p.t))
    first = pltpu.make_async_copy(o.cot.at[m], v.hid, v.fsem.at[0])
    send = rcopy(v.abuf.at[mine], v.abuf.at[mine], v.ys.at[0], v.yr.at[0], pair)
    swap = rcopy(v.ysend, v.ygot, v.ys.at[1], v.yr.at[1], pair)
    keep, need = [], {}

    def stash(*pairs):
        keep.extend(local(src, dst.at[m]) for src, dst in pairs)

    def fetch():
        loads = (
            ((o.proj, v.proj_v), (o.graw, v.graw_v), (o.lin, v.lv)),
            ((o.down, v.down_v),),
            ((o.gate, v.gate_v), (o.up, v.up_v)),
            ((o.comb, v.comb_v), (o.att, v.att_v), (o.lraw, v.lraw_v)),
            ((o.xlow, v.xlow_v), (o.qraw, v.qraw_v)),
        )
        for i, group in enumerate(loads):
            need[i] = [local(src.at[m], dst) for src, dst in group]

    def have(i):
        for copy in need[i]:
            copy.wait()

    def begin():
        if c.slots == 1:
            fetch()

        @pl.when(p.s == 1)
        def _():
            first.start()
            first.wait()

        pl.when(p.s == 0)(hand.wait_recv)
        have(0)
        v.ggr_v[...] = jnp.zeros_like(v.ggr_v)
        dproj, v.ggr_v[5:6, :] = rms_back(v.proj_v[...], gain(5), v.hid[...].astype(F32))
        v.plow_v[...] = dproj.astype(BF)
        w.sm()
        dmid = nn(v.plow_v[...], o.sm_v[cols_of(LP)])
        value, slope = gelu_both(v.graw_v[...])
        v.lgrad_v[...] = value * dmid
        v.grlow_v[...] = (dmid * v.lv[...].astype(F32) * slope).astype(BF)
        dres = v.hid[...].astype(F32) + nt(v.grlow_v[...], o.sm_v[cols_of(LG)])
        v.igrad_v[...] = dres
        have(1)
        ddown, v.ggr_v[4:5, :] = rms_back(v.down_v[...], gain(4), dres)
        v.xbuf[p.b, rows_of(p.a, r), :] = ddown.astype(BF)
        line.begin()
        stash((v.lgrad_v, o.lgrad), (v.plow_v, o.plow), (v.grlow_v, o.grlow))

    def hidden_part(col):
        @tiles(hb2, min(256, hb2))
        def _(at):
            dgeglu = nn(v.xbuf[col], o.dw_v[:, at])
            value, slope = gelu_both(v.gate_v[col, :, at].astype(F32))
            up = v.up_v[col, :, at].astype(F32)
            v.up_v[col, :, at] = (dgeglu * value).astype(BF)
            v.gate_v[col, :, at] = (dgeglu * up * slope).astype(BF)

    def down_part(col, dest, h):
        start, size = c.halves[h]

        @tiles(size, 256)
        def _(at):
            at = pl.ds(pl.multiple_of(start + at.start, 256), 256)
            part = nt(v.gate_v[col], o.gw_v[at, :]) + nt(v.up_v[col], o.uw_v[at, :])
            dest[:, at] = part.astype(dest.dtype)

    def ready(i):
        if i == 0:
            w.dw()
            have(2)
        else:
            w.gw()
            w.uw()

    line = line_stages(c, p, v, hidden_part, down_part, ready)

    def rest():
        line.rest()
        stash((v.xbuf, o.dfull), (v.gate_v, o.dgl), (v.up_v, o.dul))

    def middle():
        line.total()
        have(3)
        dcomb, v.ggr_v[3:4, :] = rms_back(v.comb_v[...], gain(3), v.down_v[...])
        even = (v.igrad_v[...] + dcomb) * RH
        v.igrad_v[...] = even
        datt, v.ggr_v[1:2, :] = rms_back(v.att_v[...], gain(1), even)
        v.abuf[mine, :] = datt.astype(BF)
        send.start()
        dlraw, v.ggr_v[2:3, :] = rms_back(v.lraw_v[...], gain(2), v.igrad_v[...])
        v.lrlow_v[...] = dlraw.astype(BF)
        v.lmg_v[...] = nn(v.lrlow_v[...], o.sm_v[cols_of(LR)]).astype(BF)
        v.proj_v[...] = v.igrad_v[...] + nt(v.lmg_v[...], o.sm_v[cols_of(LL)])
        stash((v.lrlow_v, o.lrlow), (v.lmg_v, o.lmg))

    def heads():
        w.ot()
        rcopy(v.abuf.at[theirs], v.abuf.at[theirs], v.ys.at[0], v.yr.at[0], pair).wait_recv()

        @tiles(c.heads, 256)
        def _(at):
            v.hgrad_v[:, at] = nn(v.abuf[...], o.ot_v[:, at]).astype(BF)

        have(4)
        cos, sin = o.cos[...], o.sin[...]
        q_gain, k_gain = o.gains[6:7, 0:HEAD], o.gains[7:8, 0:HEAD]
        allowed = o.allowed[m] > 0.5
        k_at, v_at = pl.ds(c.heads, HEAD), pl.ds(c.heads + HEAD, HEAD)
        kraw, vraw = v.qraw_v[:, k_at], v.qraw_v[:, v_at]
        key = rotate(kraw * rms_of(kraw) * k_gain, cos, sin).astype(BF)
        value = (vraw * rms_of(vraw)).astype(BF)
        dkey = jnp.zeros(kraw.shape, F32)
        dvalue = jnp.zeros(vraw.shape, F32)
        dq_gain = jnp.zeros((1, HEAD), F32)
        for h in range(c.heads // HEAD):
            at = pl.ds(h * HEAD, HEAD)
            raw = v.qraw_v[:, at]
            query = rotate(raw * rms_of(raw) * q_gain, cos, sin).astype(BF)
            scores = jnp.where(allowed, nt(query, key) * HEAD**-0.5, NEG)
            shifted = jnp.exp(scores - jnp.max(scores, axis=-1, keepdims=True))
            prob = shifted / jnp.sum(shifted, axis=-1, keepdims=True)
            hgrad = v.hgrad_v[:, at]
            dprob = nt(hgrad, value)
            dvalue = dvalue + tn(prob.astype(BF), hgrad)
            inner = jnp.sum(prob * dprob, axis=-1, keepdims=True)
            dscore = (prob * (dprob - inner)).astype(BF)
            dquery = nn(dscore, key) * HEAD**-0.5
            dkey = dkey + tn(dscore, query) * HEAD**-0.5
            draw, dg = rms_back(raw, q_gain, rotate_back(dquery, cos, sin))
            dq_gain = dq_gain + dg
            v.dqkv_v[:, at] = draw.astype(BF)
        draw, dk_gain = rms_back(kraw, k_gain, rotate_back(dkey, cos, sin))
        v.dqkv_v[:, k_at] = draw.astype(BF)
        v.dqkv_v[:, v_at] = plain_back(vraw, dvalue).astype(BF)
        v.ggr_v[6:7, 0:HEAD] = dq_gain
        v.ggr_v[7:8, 0:HEAD] = dk_gain
        w.qkv()

        @tiles(width, 256)
        def _(at):
            v.acc[0 : 2 * r, at] = nt(v.dqkv_v[...], o.qkv_v[at, :])

        v.ysend[...] = v.acc[theirs, :].astype(BF)
        swap.start()
        stash((v.abuf, o.afull), (v.dqkv_v, o.dqkv))

    def entry():
        swap.wait()
        dnorm = v.proj_v[...] + v.acc[mine, :] + v.ygot[...].astype(F32)
        dx, v.ggr_v[0:1, :] = rms_back(v.xlow_v[...].astype(F32), gain(0), dnorm)
        dx = dx + v.igrad_v[...]
        v.igrad_v[...] = dx

        @pl.when(p.s == 1)
        def _():
            v.hid[...] = dx.astype(BF)
            if m == 0:
                pl.semaphore_wait(o.ready, 1)
            hand.start()

        stash((v.igrad_v, o.igrad), (v.ggr_v, o.ggr))

    def end():
        send.wait_send()
        line.end()
        pl.when(p.s == 1)(hand.wait_send)
        for copy in keep:
            copy.wait()

    return {
        FIRST: begin, GIVE: line.give, OWN: line.own, REST: rest, SUMS: line.sums, MIDDLE: middle, HEADS_STAGE: heads,
        ENTRY: entry, LAST: end, BEGIN: fetch,
    }


BACKWARD_ORDER = (
    (FIRST, 0), (GIVE, 0), (OWN, 0), (FIRST, 1), (REST, 0), (GIVE, 1), (OWN, 1), (SUMS, 0), (REST, 1), (MIDDLE, 0),
    (HEADS_STAGE, 0), (SUMS, 1), (ENTRY, 0), (MIDDLE, 1), (HEADS_STAGE, 1), (ENTRY, 1),
)


def backward_kernel(c, o):
    p = place(c.n)
    local = Local(o.lsem)
    views = [view(c, o, m, backward_buffers(c), stage_sems(c) | dict(hid=None)) for m in range(2)]
    late = {}
    w = SimpleNamespace(**{name: (lambda name=name: late[name]()) for name in ("sm", "qkv", "ot", "gw", "uw", "dw")})
    stages = [backward_stages(c, p, o, views[m], m, w, local) for m in range(2)]
    if c.slots == 2:
        stages[0][BEGIN]()
    late.update(vars(waits_of(c, o, local)))
    if c.slots == 2:
        stages[1][BEGIN]()
    enter(p, o, 1)
    run_stages(c, p, BACKWARD_ORDER, stages)


def grad_shapes(c):
    m, r, w, q = 2, c.r, c.width, 2 * c.r
    ar, hb2 = c.n // 2 * c.r, 2 * c.hb
    return dict(
        igrad=((m, r, w), F32),
        lgrad=((m, r, c.per), F32),
        plow=((m, r, w), BF),
        grlow=((m, r, c.per), BF),
        dfull=((m, 2, ar, w), BF),
        dgl=((m, 2, ar, hb2), BF),
        dul=((m, 2, ar, hb2), BF),
        lrlow=((m, r, w), BF),
        lmg=((m, r, LANES), BF),
        afull=((m, q, w), BF),
        dqkv=((m, q, c.qkv), BF),
        ggr=((m, 8, w), F32),
    )


READ = ("proj", "graw", "down", "gate", "up", "comb", "att", "lraw", "xlow", "qraw")


def backward_buffers(c):
    shapes, kept = grad_shapes(c), stash_shapes(c)
    own = {name: shapes[name] for name in shapes if name not in ("dfull", "afull", "dgl", "dul")}
    return dict(
        abuf=pltpu.VMEM((2 * c.r, c.width), BF),
        hgrad_v=pltpu.VMEM((2 * c.r, c.heads), BF),
        **scratch_of(own),
        **scratch_of({name: kept[name] for name in READ}),
        **line_buffers(c),
    )


def backward_pass(c, weights, data, tables, stash):
    scratch = dict(
        **twice(c, backward_buffers(c), stage_sems(c) | dict(hid=pltpu.VMEM((c.r, c.width), BF))), **shared_scratch(c)
    )
    return launch(
        lambda o: backward_kernel(c, o),
        3,
        dict(**weights, cot=data.cot, lin=data.lin, **{name: stash[name] for name in READ}),
        tables,
        grad_shapes(c),
        scratch,
    )


def return_kernel(c, o):
    p = place(c.n)
    n, A, R, hb = c.n, c.n // 2, c.R, c.hb
    pair = (p.s, p.d, 1 - p.t)
    side = (p.s, p.a * 2 + 1 - p.b, p.t)
    barrier = pltpu.get_barrier_semaphore()

    def signal(device):
        pl.semaphore_signal(barrier, inc=1, device_id=device, device_id_type=MESH)

    for k in range(1, n):
        signal((p.s, lax.rem(p.d + k, n), p.t))
    signal(pair)
    pl.semaphore_wait(barrier, n)
    local = Local(o.lsem)
    outs = ((o.pfull, o.dgl), (o.pfull, o.dul), (o.dfull, o.geglu))

    def swap(m, k):
        at = rows_of(lax.rem(p.d + k, n), R)
        return rcopy(o.fsend.at[m, at], o.fgot.at[m, at], o.ys.at[m, k], o.yr.at[m, k], pair)

    def ffn_out(m, source):
        return (o.gg, o.gu, o.gd)[m].at[:, rows_of(source, hb)]

    def trade(m, k):
        dest = lax.rem(p.d + k, n)
        return rcopy(
            o.fown.at[m, rows_of(dest, R)], ffn_out(m, p.d), o.ts.at[m, k], o.tr.at[m, k], (p.s, dest, p.t)
        )

    def came(m, k):
        source = lax.rem(p.d + n - k, n)
        return rcopy(o.fown.at[m, rows_of(p.d, R)], ffn_out(m, source), o.ts.at[m, k], o.tr.at[m, k], side)

    order = [*range(1, n), 0]
    inputs = {0: [local(outs[0][0], o.x_v), local(outs[0][1], o.y_v.at[0])], 1: [local(outs[1][1], o.y_v.at[1])]}

    def ffn_grad(m):
        for copy in inputs[m]:
            copy.wait()
        y = o.y_v.at[m % 2]
        tokens = 4 * y.shape[1]

        @tiles(c.width, 256)
        def _(rows):
            x = o.x_v[:, :, :, rows].reshape(-1, 256)
            mine = y[:, :, :, rows_of(p.t, hb)].reshape(-1, hb)
            o.fown[m, rows, :] = tn(x, mine).astype(BF)
            theirs = y[:, :, :, rows_of(1 - p.t, hb)].reshape(-1, hb)
            o.fsend[m, rows, :] = tn(x, theirs).astype(BF)

        for k in order:
            swap(m, k).start()
        if m == 0:
            inputs[2] = [local(outs[2][1], o.y_v.at[0])]
        if m == 1:
            inputs[2].append(local(outs[2][0], o.x_v))

    need = [
        local(getattr(o, name), getattr(o, name + TAIL))
        for name in ("nfull", "dqkv", "afull", "heads", "lrlow", "lmid", "resid", "grlow", "plow", "llow", "lmg", "gcol")
    ]
    stage, last, finish = cube_scatter(p, o.acc, o.got, R, c.parts, (o.rs, o.rr), o.gp_v)
    mine_copies = []

    def grad(x, y, at, block=512):
        tokens = 2 * x.shape[1]

        @tiles(c.width, block)
        def _(rows):
            left = x[:, :, rows].reshape(tokens, block)
            o.acc[rows, at] = tn(left, y[...].reshape(tokens, y.shape[2])).astype(BF)

    def ffn_block(m, k):
        rows = rows_of(lax.rem(p.d + k, n), R)
        swap(m, k).wait_recv()
        total = o.fown[m, rows, :].astype(F32) + o.fgot[m, rows, :].astype(F32)
        o.fown[m, rows, :] = total.astype(BF)
        if k:
            trade(m, k).start()
        else:
            mine_copies.append(local(o.fown.at[m, rows], ffn_out(m, p.d)))

    def part_grad(h):
        begin, size = c.parts[h]
        base = c.qkv + c.heads
        if begin < c.qkv:
            grad(o.nfull_v, o.dqkv_v.at[:, :, pl.ds(begin, size)], pl.ds(begin, size))
        elif begin < base:
            grad(o.afull_v, o.heads_v.at[:, :, pl.ds(begin - c.qkv, size)], pl.ds(begin, size))
        elif begin == base:
            mine = rows_of(p.t, c.r)
            lane = lax.broadcasted_iota(jnp.int32, (512, LANES), 1)

            @tiles(c.width, 512)
            def _(rows):
                left = tn(o.nfull_v[0, mine, rows], o.lmg_v[0]) + tn(o.nfull_v[1, mine, rows], o.lmg_v[1])
                gains = o.gcol_v[rows, :].astype(F32)
                o.acc[rows, pl.ds(begin, LANES)] = jnp.where(lane < c.rank, left, gains).astype(BF)

            grad(o.lrlow_v, o.lmid_v, pl.ds(begin + LANES, LANES))
            grad(o.resid_v, o.grlow_v, pl.ds(begin + 2 * LANES, c.per))
        else:
            grad(o.plow_v, o.llow_v, pl.ds(begin, c.per))

    def attn_ready():
        for copy in need:
            copy.wait()

    r0, per, lag, g1, g2 = c.kg
    top = lowest(0, n)
    events = [(-3.0, lambda: ffn_grad(0)), (-2.0, attn_ready), (g1, lambda: ffn_grad(1)), (g2, lambda: ffn_grad(2))]
    for m in range(3):
        for i, k in enumerate(order):
            events.append((r0 + (m * n + i) * 8 / (n * per), lambda m=m, k=k: ffn_block(m, k)))
    for h in range(len(c.parts)):
        events.append((h, lambda h=h: (part_grad(h), stage(h, 0))))
        for bit in range(1, top):
            events.append((h + lag[min(bit, len(lag)) - 1], lambda h=h, bit=bit: stage(h, bit)))
        events.append((h + lag[-1] + 0.01, lambda h=h: last(h)))
    for _, run in sorted(events, key=lambda e: e[0]):
        run()
    shared = pl.ds(c.qkv + c.heads, c.small)
    rest = rcopy(o.gp_v.at[:, shared], o.sgot, o.ss.at[0], o.sr.at[0], pair)
    rest.start()
    rest.wait()
    o.gp_v[:, shared] = (o.gp_v[:, shared].astype(F32) + o.sgot[...].astype(F32)).astype(BF)
    out = local(o.gp_v, o.gp)
    for m in range(3):
        for k in range(n):
            swap(m, k).wait_send()
            if k:
                came(m, k).wait_recv()
                trade(m, k).wait_send()
    for q in range(len(c.parts)):
        finish(q)
    for copy in [*mine_copies, out]:
        copy.wait()


def fetch_weights(c, arrays, gains):
    n, q = c.n, len(c.cuts)
    outs = dict(
        pk=((c.width, c.total), BF),
        gw=((c.width, 2 * c.hb), BF),
        uw=((c.width, 2 * c.hb), BF),
        dw=((c.width, 2 * c.hb), BF),
        grow=((8, c.width), F32),
    )
    scratch = dict(
        gcol=pltpu.VMEM((c.width, LANES), BF),
        grow_v=pltpu.VMEM((8, c.width), F32),
        pack_v=pltpu.VMEM((c.R, c.total), BF),
        out_v=pltpu.VMEM((c.heads, c.R), BF),
        lp_v=pltpu.VMEM((c.per, c.R), BF),
        lr_v=pltpu.VMEM((c.rank, c.R), BF),
        rows_v=pltpu.VMEM((LANES, c.R), F32),
        down_v=pltpu.VMEM((n * c.hb, c.R), BF),
        down_t=pltpu.VMEM((c.R, n * c.hb), BF),
        block_v=pltpu.VMEM((3, c.R, c.hb), BF),
        gs=dma(n, q), gr=dma(n, q), ts=dma(n, 3), tr=dma(n, 3), ys=dma(n, 3), yr=dma(n, 3), lsem=dma(24),
        go=pltpu.SemaphoreType.REGULAR,
    )
    return launch(lambda o: fetch_kernel(c, o), 6, arrays, gains, outs, scratch)


def return_grads(c, f, g, gcol):
    n = c.n
    R = c.R
    flat = ((R, n * c.hb), BF)
    outs = dict(gp=((R, c.total), BF), gg=flat, gu=flat, gd=flat)
    arrays = dict(
        nfull=f.nfull, dqkv=g.dqkv, afull=g.afull, heads=f.heads, lrlow=g.lrlow, lmid=f.lmid, resid=f.resid,
        grlow=g.grlow, plow=g.plow, llow=f.llow, lmg=g.lmg, gcol=gcol,
    )
    scratch = dict(
        acc=pltpu.VMEM((c.width, c.total), BF),
        got=pltpu.VMEM(((n - 1) * R, c.total), BF),
        gp_v=pltpu.VMEM((R, c.total), BF),
        fown=pltpu.VMEM((3, c.width, c.hb), BF),
        fgot=pltpu.VMEM((3, c.width, c.hb), BF),
        fsend=pltpu.VMEM((3, c.width, c.hb), BF),
        x_v=pltpu.VMEM(f.pfull.shape, BF),
        y_v=pltpu.VMEM((2, *g.dgl.shape), BF),
        sgot=pltpu.VMEM((R, c.small), BF),
        ys=dma(3, n), yr=dma(3, n), ts=dma(3, n), tr=dma(3, n), ss=dma(1), sr=dma(1), lsem=dma(24),
        rs=dma(len(c.parts), n), rr=dma(len(c.parts), n),
        **{name + TAIL: pltpu.VMEM(v.shape, v.dtype) for name, v in arrays.items()},
    )
    big = dict(pfull=f.pfull, dgl=g.dgl, dul=g.dul, dfull=g.dfull, geglu=f.geglu)
    return launch(lambda o: return_kernel(c, o), 7, dict(**arrays, **big), {}, outs, scratch)


def widen_kernel(c, o):
    local = Local(o.lsem)
    hb, R, rank = c.hb, c.R, c.rank
    loads = [local(o.gp, o.gp_v), local(o.gd, o.g_v.at[2]), local(o.gg, o.g_v.at[0]), local(o.gu, o.g_v.at[1])]
    base = c.qkv + c.heads
    loads[0].wait()
    o.f_v[...] = o.gp_v[:, pl.ds(0, c.qkv)].astype(F32)
    out = [
        local(o.f_v.at[:, pl.ds(0, c.heads)], o.q),
        local(o.f_v.at[:, pl.ds(c.heads, HEAD)], o.k),
        local(o.f_v.at[:, pl.ds(c.heads + HEAD, HEAD)], o.v),
    ]
    for i, (g, w) in enumerate(((0, o.wg), (1, o.wu))):
        loads[2 + i].wait()
        o.w_v[i] = o.g_v[g].astype(F32)
        out.append(local(o.w_v.at[i], w))
    loads[1].wait()
    for k in range(c.n):
        o.d_v[pl.ds(k * hb, hb), :] = o.g_v[2, :, pl.ds(k * hb, hb)].astype(F32).T
    out.append(local(o.d_v, o.wd))
    for i in range(0, c.heads, HEAD):
        o.t_v[pl.ds(i, HEAD), :] = o.gp_v[:, pl.ds(c.qkv + i, HEAD)].astype(F32).T
    out.append(local(o.t_v, o.out))
    left = o.gp_v[:, pl.ds(base, LANES)].astype(F32)
    o.ll[...] = left[:, :rank]
    rows = left.T
    for i, gain in enumerate((o.g0, o.g1, o.g2, o.g3, o.g4, o.g5, o.g6, o.g7)):
        gain[...] = rows[rank + i : rank + i + 1, 0 : gain.shape[1]]
    o.lr[...] = o.gp_v[:, pl.ds(base + LANES, LANES)].astype(F32).T[:rank]
    o.lg[...] = o.gp_v[:, pl.ds(base + 2 * LANES, c.per)].astype(F32)
    o.lp[...] = o.gp_v[:, pl.ds(base + 2 * LANES + c.per, c.per)].astype(F32).T
    for copy in out:
        copy.wait()


def widen(c, done):
    R, wide = c.R, c.n * c.hb
    outs = dict(
        q=((R, c.heads), F32), k=((R, HEAD), F32), v=((R, HEAD), F32),
        out=((c.heads, R), F32), wg=((R, wide), F32), wu=((R, wide), F32), wd=((wide, R), F32),
    )
    row, head = ((1, R), F32), ((1, HEAD // c.n), F32)
    small = dict(
        ll=((R, c.rank), F32), lr=((c.rank, R), F32), lg=((R, c.per), F32), lp=((c.per, R), F32),
        g0=row, g1=row, g2=row, g3=row, g4=row, g5=row, g6=head, g7=head,
    )
    scratch = dict(
        gp_v=pltpu.VMEM((R, c.total), BF), f_v=pltpu.VMEM((R, c.qkv), F32), t_v=pltpu.VMEM((c.heads, R), F32),
        g_v=pltpu.VMEM((3, R, wide), BF), w_v=pltpu.VMEM((2, R, wide), F32), d_v=pltpu.VMEM((wide, R), F32),
        lsem=dma(16),
    )
    return launch(lambda o: widen_kernel(c, o), None, done, {}, outs, scratch, small)


def body(
    hidden, layer_inputs, span_starts, cotangent, input_gain, query_weight, key_projection, value_projection,
    query_gain, key_norm_gain, output_weight, attention_gain, laurel_left, laurel_right, laurel_gain, prefeed_gain,
    gate_weight, up_weight, down_weight, postfeed_gain, layer_gate, layer_project, layer_gain,
):
    n, nt_ = lax.axis_size(D), lax.axis_size(T)
    t = lax.axis_index(T)
    rank = laurel_left.shape[2]
    width = hidden.shape[3]
    R = width // n
    heads = query_weight.shape[2]
    qkv = heads + 2 * HEAD
    per = layer_gate.shape[2]
    small = 2 * LANES + 2 * per
    base = qkv + heads
    c = SimpleNamespace(
        n=n, R=R, r=hidden.shape[2], width=width, heads=heads, qkv=qkv, per=per, small=small, rank=rank,
        total=qkv + heads + small, hb=gate_weight.shape[2] // n,
        cuts=((0, qkv), (qkv, heads), (qkv + heads, small)),
        parts=(*((i, 512) for i in range(0, qkv + heads, 512)), (base, small - per), (base + small - per, per)),
        slots=2 if n <= 8 else 1, ag=(12.0, 6.0, 12.0), tr=(1.0, 2.5, 30.0, 3.0), by_matrix=True, go_at=GO_AT, kg=KG,
        halves=tuple((h * width // HALVES, width // HALVES) for h in range(HALVES)),
    )
    weights = fetch_weights(
        c,
        dict(
            query=query_weight[0], key=key_projection[0], value=value_projection[0], out=output_weight[0],
            lr=laurel_right[0], lg=layer_gate[0], lp=layer_project[0],
            gate=gate_weight[0], up=up_weight[0], down=down_weight[0],
        ),
        dict(
            ll=laurel_left[0], g0=input_gain, g1=attention_gain, g2=laurel_gain, g3=prefeed_gain, g4=postfeed_gain,
            g5=layer_gain, g6=query_gain, g7=key_norm_gain,
        ),
    )
    columns = weights.pop(GROW)
    short = HEAD // n
    head_gains = columns[6:].reshape(2, n, R)[:, :, :short].reshape(2, HEAD)
    gain_rows = jnp.concatenate([columns[:6], jnp.pad(head_gains, ((0, 0), (0, width - HEAD)))], axis=0)

    span = c.r * nt_
    position = jnp.arange(span, dtype=jnp.int32)
    begin = span_starts[:, 0][:, None]
    inside = (position[None] >= begin) & (position[None] < begin + IMG)
    allowed = (position[None, :] <= position[:, None])[None] | (inside[:, :, None] & inside[:, None, :])
    half = HEAD // 2
    frequency = jnp.exp(jnp.arange(half, dtype=F32) * (-2.0 * math.log(10000.0) / HEAD))
    angles = jnp.arange(span, dtype=F32)[:, None] * frequency[None, :]
    tables = dict(gains=gain_rows, cos=jnp.cos(angles), sin=jnp.sin(angles), allowed=allowed.astype(F32))
    data = SimpleNamespace(hidden=hidden[:, 0], lin=layer_inputs[0, :, 0], cot=cotangent[:, 0])

    stash = forward_pass(c, weights, data, tables)
    grads = backward_pass(c, weights, data, tables, stash)
    f, g = SimpleNamespace(**stash), SimpleNamespace(**grads)

    sums = g.ggr[0] + g.ggr[1]
    head_sums = jnp.pad(sums[6:, :HEAD].reshape(2, n, short), ((0, 0), (0, 0), (0, R - short))).reshape(2, width)
    gain_cols = jnp.concatenate([sums[:6], head_sums], axis=0).T
    gcol = jnp.pad(gain_cols, ((0, 0), (rank, LANES - rank - 8))).astype(BF)
    w = SimpleNamespace(**widen(c, return_grads(c, f, g, gcol)))
    return (
        f.act[None, :, None],
        g.igrad[None, :, None],
        g.lgrad[None, :, None],
        w.g0,
        w.q[None],
        w.k[None],
        w.v[None],
        w.g6,
        w.g7,
        w.out[None],
        w.g1,
        w.ll[None],
        w.lr[None],
        w.g2,
        w.g3,
        w.wg[None],
        w.wu[None],
        w.wd[None],
        w.g4,
        w.lg[None],
        w.lp[None],
        w.g5,
    )


def solution(mesh):
    rows, cols = P(S, D, T), P(S, T, D)
    vec, tall, flat = P(S, D), P(S, D, None), P(S, None, D)
    seq, out = P(None, D, T, None), P(S, None, D, T, None)
    weights = (
        vec, rows, rows, rows, vec, vec, cols, vec, tall, flat, vec, vec, rows, rows, cols, vec, tall, flat, vec,
    )
    return jax.shard_map(
        body,
        mesh=mesh,
        in_specs=(seq, out, P(None, D), seq, *weights),
        out_specs=(out, out, out, *weights),
        check_vma=False,
    )
```

```python
import math
from types import SimpleNamespace

import jax
import jax.numpy as jnp
from jax import lax
from jax.experimental import pallas as pl
from jax.experimental.pallas import tpu as pltpu
from jax.sharding import PartitionSpec as P

S, D, T = "section", "dp", "tensor"
MESH = pl.DeviceIdType.MESH
BF, F32 = jnp.bfloat16, jnp.float32
HEAD = 256
IMG = 64
EPS = 1e-06
RH = 0.5**0.5
NEG = -1e30
LANES = 128
GELU_C = math.sqrt(2.0 / math.pi)
GELU_K = 0.044715
VMEM_LIMIT = 61 << 20
HALVES = 2
GATHER_PARTS = 2
GO_AT = 60.0
SHARED = 1
KG = (2.5, 3.0, (2.1, 3.2, 4.3), 0.6, 2.6)


def rms_of(v):
    return lax.rsqrt(jnp.mean(v * v, axis=-1, keepdims=True) + EPS)


def rms_back(v, gain, grad):
    r = rms_of(v)
    unit = v * r
    inner = grad * gain
    back = r * (inner - unit * jnp.mean(inner * unit, axis=-1, keepdims=True))
    return back, jnp.sum(grad * unit, axis=0, keepdims=True)


def plain_back(v, grad):
    r = rms_of(v)
    unit = v * r
    return r * (grad - unit * jnp.mean(grad * unit, axis=-1, keepdims=True))


def gelu(v):
    return 0.5 * v * (1.0 + jnp.tanh(GELU_C * (v + GELU_K * v * v * v)))


def gelu_both(v):
    square = v * v
    th = jnp.tanh(GELU_C * v * (1.0 + GELU_K * square))
    value = 0.5 * v * (1.0 + th)
    slope = 0.5 * (1.0 + th) + 0.5 * v * (1.0 - th * th) * GELU_C * (1.0 + 3.0 * GELU_K * square)
    return value, slope


def rotate(v, cos, sin):
    half = HEAD // 2
    front, back = v[:, :half], v[:, half:]
    return jnp.concatenate([front * cos - back * sin, back * cos + front * sin], axis=-1)


def rotate_back(g, cos, sin):
    half = HEAD // 2
    front, back = g[:, :half], g[:, half:]
    return jnp.concatenate([front * cos + back * sin, back * cos - front * sin], axis=-1)


def nn(x, w):
    return jnp.dot(x, w, preferred_element_type=F32)


def nt(x, w):
    return lax.dot_general(x, w, (((1,), (1,)), ((), ())), preferred_element_type=F32)


def tn(x, w):
    return lax.dot_general(x, w, (((0,), (0,)), ((), ())), preferred_element_type=F32)


def tiles(count, step):
    def wrap(fn):
        def one(j, carry):
            fn(pl.ds(pl.multiple_of(j * step, step), step))
            return carry

        lax.fori_loop(0, count // step, one, 0)

    return wrap


def place(n):
    s, d, t = lax.axis_index(S), lax.axis_index(D), lax.axis_index(T)
    return SimpleNamespace(s=s, d=d, t=t, a=lax.div(d, 2), b=lax.rem(d, 2), n=n, A=n // 2)


def rcopy(src, dst, send, recv, device):
    return pltpu.make_async_remote_copy(
        src_ref=src, dst_ref=dst, send_sem=send, recv_sem=recv, device_id=device, device_id_type=MESH
    )


def rows_of(index, size):
    return pl.ds(pl.multiple_of(index * size, size), size)


class Local:
    def __init__(self, sems):
        self.sems, self.used = sems, 0

    def __call__(self, src, dst):
        copy = pltpu.make_async_copy(src, dst, self.sems.at[self.used])
        self.used += 1
        copy.start()
        return copy


def steps_of(p, fn, far_first=False):
    for delta in range(p.A - 1, 0, -1) if far_first else range(1, p.A):
        pl.when(p.a - delta >= 0)(lambda: fn(p.a - delta))
        pl.when(p.a + delta < p.A)(lambda: fn(p.a + delta))


def line_gather(p, buf, size, sems):
    zs, zr, xs, xr = sems
    side = (p.s, p.a * 2 + 1 - p.b, p.t)
    part = size // GATHER_PARTS

    def at(col, row, g):
        return buf.at[col, pl.ds(pl.multiple_of(row * size + g * part, part), part)]

    def along(row, g):
        return rcopy(at(p.b, p.a, g), at(p.b, p.a, g), zs.at[row, g], zr.at[p.a, g], (p.s, row * 2 + p.b, p.t))

    def came(row, g):
        return rcopy(at(p.b, row, g), at(p.b, row, g), zs.at[row, g], zr.at[row, g], side)

    def across(col, row, g):
        return rcopy(at(col, row, g), at(col, row, g), xs.at[row, g], xr.at[row, g], side)

    def each(fn):
        def run(row):
            for g in range(GATHER_PARTS):
                fn(row, g)

        return run

    for g in range(GATHER_PARTS):
        steps_of(p, lambda row: along(row, g).start(), True)
        across(p.b, p.a, g).start()

    def forward(row, g):
        came(row, g).wait_recv()
        across(p.b, row, g).start()

    def arrive():
        for row in range(p.A):
            each(lambda row, g: across(1 - p.b, row, g).wait_recv())(row)

    def finish():
        steps_of(p, each(lambda row, g: along(row, g).wait_send()))
        for row in range(p.A):
            each(lambda row, g: across(p.b, row, g).wait_send())(row)

    return lambda: steps_of(p, each(forward)), arrive, finish


def line_scatter(p, acc, other, got, step_got, size, cuts, sems, out):
    xs, xr, zs, zr = sems
    side = (p.s, p.a * 2 + 1 - p.b, p.t)

    def part(row, h):
        return (rows_of(row, size), pl.ds(cuts[h][0], cuts[h][1]))

    def across(h, row):
        at = part(row, h)
        return rcopy(other.at[at], got.at[at], xs.at[h, row], xr.at[h, row], side)

    def along(h, row):
        return rcopy(
            other.at[part(row, h)], step_got.at[part(p.a, h)], zs.at[h, row], zr.at[h, p.a], (p.s, row * 2 + p.b, p.t)
        )

    def came(h, row):
        return rcopy(other.at[part(row, h)], step_got.at[part(row, h)], zs.at[h, row], zr.at[h, row], side)

    def start(h):
        steps_of(p, lambda row: across(h, row).start(), True)
        across(h, p.a).start()

    def carry(h):
        def pass_on(row):
            at = part(row, h)
            across(h, row).wait()
            other[at] = (acc[at] + got[at].astype(F32)).astype(BF)
            along(h, row).start()

        steps_of(p, pass_on, True)

    def collect(h):
        across(h, p.a).wait()
        at = part(p.a, h)
        cols = (slice(None), at[1])
        out[cols] = acc[at] + got[at].astype(F32)

        def add(row):
            came(h, row).wait_recv()
            out[cols] += step_got[part(row, h)].astype(F32)

        steps_of(p, add)

    def finish(h):
        steps_of(p, lambda row: along(h, row).wait_send())

    return start, carry, collect, finish


def lowest(mask, n):
    bit = 0
    while (1 << bit) < n and not mask >> bit & 1:
        bit += 1
    return bit


def flip(d, mask):
    bit = 0
    result = d
    while 1 << bit <= mask:
        if mask >> bit & 1:
            result = result + (1 - 2 * lax.rem(lax.div(d, 1 << bit), 2)) * (1 << bit)
        bit += 1
    return result


def cube_scatter(p, acc, got, size, cols, slots, sems, out):
    send, recv = sems
    n = p.n

    def block(mask):
        return rows_of(flip(p.d, mask), size)

    def message(h, mask):
        bit = lowest(mask, n)
        return rcopy(
            acc.at[block(mask), cols(h)],
            got.at[pl.ds((mask - 1) * size, size), slots(h)],
            send.at[h, mask],
            recv.at[h, mask],
            (p.s, flip(p.d, 1 << bit), p.t),
        )

    def stage(h, bit):
        for mask in range(1, n):
            if lowest(mask, n) == bit:
                at = (block(mask), cols(h))
                total = None
                for below in range(bit):
                    came = mask | 1 << below
                    message(h, came).wait_recv()
                    term = got[pl.ds((came - 1) * size, size), slots(h)].astype(F32)
                    total = term if total is None else total + term
                if total is not None:
                    acc[at] = (acc[at].astype(F32) + total).astype(BF)
                message(h, mask).start()

    def last(h):
        total = acc[block(0), cols(h)].astype(F32)
        for below in range(lowest(0, n)):
            message(h, 1 << below).wait_recv()
            total = total + got[pl.ds(((1 << below) - 1) * size, size), slots(h)].astype(F32)
        out[:, cols(h)] = total.astype(BF)

    def finish(h):
        for mask in range(1, n):
            message(h, mask).wait_send()

    return stage, last, finish


def dma(*shape):
    return pltpu.SemaphoreType.DMA(shape)


def gather_sems(A):
    g = GATHER_PARTS
    return dict(gzs=dma(A, g), gzr=dma(A, g), gxs=dma(A, g), gxr=dma(A, g))


def scatter_sems(A, parts):
    return dict(rxs=dma(parts, A), rxr=dma(parts, A), rzs=dma(parts, A), rzr=dma(parts, A))


HBM = pl.BlockSpec(memory_space=pltpu.HBM)
VM = pl.BlockSpec(memory_space=pltpu.VMEM)


def launch(kernel, cid, hbm_in, vmem_in, outs, scratch, small=None):
    small = small or {}
    everything = [*hbm_in, *vmem_in, *outs, *small, *scratch]

    def run(*refs):
        kernel(SimpleNamespace(**dict(zip(everything, refs))))

    results = pl.pallas_call(
        run,
        out_shape=[jax.ShapeDtypeStruct(*spec) for spec in (*outs.values(), *small.values())],
        in_specs=[HBM] * len(hbm_in) + [VM] * len(vmem_in),
        out_specs=[HBM] * len(outs) + [VM] * len(small),
        scratch_shapes=list(scratch.values()),
        compiler_params=pltpu.CompilerParams(
            collective_id=cid, has_side_effects=cid is not None, vmem_limit_bytes=VMEM_LIMIT
        ),
    )(*hbm_in.values(), *vmem_in.values())
    return dict(zip((*outs, *small), results))


def fetch_kernel(c, o):
    p = place(c.n)
    n, A, R, hb = c.n, c.n // 2, c.R, c.hb
    barrier = pltpu.get_barrier_semaphore()

    def signal(device):
        pl.semaphore_signal(barrier, inc=1, device_id=device, device_id_type=MESH)

    for k in range(1, n):
        signal((p.s, lax.rem(p.d + k, n), p.t))
    signal((p.s, p.d, 1 - p.t))
    signal((1 - p.s, p.d, p.t))
    pl.semaphore_wait(barrier, n + 1)

    @pl.when(p.s == 1)
    def _():
        pl.semaphore_wait(o.go, 1)

    side = (p.s, p.a * 2 + 1 - p.b, p.t)
    pair = (p.s, p.d, 1 - p.t)
    cuts = c.cuts
    bits = lowest(0, n)
    local = Local(o.lsem)
    waits = []

    def half(t):
        size = c.small // 2
        return pl.ds(pl.multiple_of(c.qkv + c.heads + t * size, LANES), size)

    def cols(q):
        return half(p.t) if q == SHARED else pl.ds(*cuts[q])

    def mirror(mask, t):
        at = (rows_of(flip(p.d, mask), R), half(t))
        return rcopy(o.pk.at[at], o.pk.at[at], o.ms.at[mask], o.mr.at[mask], pair)

    def give(mask, bit, q):
        rows, cs = rows_of(flip(p.d, mask), R), cols(q)
        src = o.pk.at[rows, cs] if mask else o.pack_v.at[:, cs]
        far = mask | 1 << bit
        return rcopy(src, o.pk.at[rows, cs], o.gs.at[far, q], o.gr.at[far, q], (p.s, flip(p.d, 1 << bit), p.t))

    def taken(mask, q):
        at = (rows_of(flip(p.d, mask), R), cols(q))
        return rcopy(o.pk.at[at], o.pk.at[at], o.gs.at[mask, q], o.gr.at[mask, q], side)

    def pass_on(mask, q):
        if mask:
            taken(mask, q).wait_recv()
        for bit in reversed(range(lowest(mask, n))):
            give(mask, bit, q).start()
        if mask and q == SHARED:
            mirror(mask, p.t).start()

    ffn = ((o.gate, o.gw), (o.up, o.uw), (o.down_t, o.dw))

    def block(m, source, half):
        return ffn[m][1].at[rows_of(source, R), rows_of(half, hb)]

    def trade(m, k):
        dest = lax.rem(p.d + k, n)
        return rcopy(
            ffn[m][0].at[:, rows_of(dest, hb)], block(m, p.d, p.t), o.ts.at[k, m], o.tr.at[k, m], (p.s, dest, p.t)
        )

    def came(m, k):
        source = lax.rem(p.d + n - k, n)
        return rcopy(
            ffn[m][0].at[:, rows_of(p.d, hb)], block(m, source, p.t), o.ts.at[k, m], o.tr.at[k, m], side
        )

    def share(m, k, half):
        source = lax.rem(p.d + n - k, n)
        src = ffn[m][0].at[:, rows_of(p.d, hb)] if k == 0 else block(m, source, half)
        return rcopy(src, block(m, source, half), o.ys.at[k, m], o.yr.at[k, m], pair)

    qkv, base, rank = c.qkv, c.qkv + c.heads, c.rank
    first = [
        local(o.query, o.pack_v.at[:, pl.ds(0, c.heads)]),
        local(o.key, o.pack_v.at[:, pl.ds(c.heads, HEAD)]),
        local(o.value, o.pack_v.at[:, pl.ds(c.heads + HEAD, HEAD)]),
    ]
    second = [local(o.out, o.out_v)]
    third = [local(o.lg, o.pack_v.at[:, pl.ds(base + 2 * LANES, c.per)]), local(o.lp, o.lp_v), local(o.lr, o.lr_v)]
    fourth = [local(o.down, o.down_v)]
    bounce = [local(ffn[m][0].at[:, rows_of(p.d, hb)], o.block_v.at[m]) for m in range(2)]

    def turned(x):
        return x.astype(F32).T.astype(BF)

    def prepare(q):
        if q == 0:
            for copy in first:
                copy.wait()
        elif q == 2:
            for copy in second:
                copy.wait()
            for i in range(0, c.heads, HEAD):
                o.pack_v[:, pl.ds(qkv + i, HEAD)] = turned(o.out_v[pl.ds(i, HEAD), :])
        else:
            for copy in third:
                copy.wait()
            o.rows_v[...] = jnp.zeros_like(o.rows_v)
            for i, gain in enumerate((o.g0, o.g1, o.g2, o.g3, o.g4, o.g5, o.g6, o.g7)):
                o.rows_v[rank + i : rank + i + 1, 0 : gain.shape[1]] = gain[...].astype(F32)
            left = o.rows_v[...].T
            o.pack_v[:, pl.ds(base, LANES)] = left.astype(BF)
            o.pack_v[:, pl.ds(base, rank)] = o.ll[...]
            o.rows_v[...] = jnp.zeros_like(o.rows_v)
            o.rows_v[0:rank, :] = o.lr_v[...].astype(F32)
            o.pack_v[:, pl.ds(base + LANES, LANES)] = o.rows_v[...].T.astype(BF)
            o.pack_v[:, pl.ds(base + 2 * LANES + c.per, c.per)] = turned(o.lp_v[...])

    def prepare_down():
        for copy in fourth:
            copy.wait()
        for k in range(n):
            o.down_t[:, pl.ds(k * hb, hb)] = turned(o.down_v[pl.ds(k * hb, hb), :])
        bounce.append(local(o.down_t.at[:, rows_of(p.d, hb)], o.block_v.at[2]))

    events = []
    inner = sorted((mask for mask in range(2, n, 2)), key=lambda mask: (-lowest(mask, n), mask))
    for q in range(len(cuts)):
        events.append((0.0 + 0.1 * q, lambda q=q: (prepare(q), pass_on(0, q))))
        for i, mask in enumerate(inner):
            events.append((c.ag[0] + c.ag[1] * q + c.ag[2] * i, lambda q=q, mask=mask: pass_on(mask, q)))
    events.append((c.tr[0] + c.tr[1] * (2 * n - 2), prepare_down))
    for k in range(n):
        for m in range(3):
            at = m * n + k
            if k:
                events.append((c.tr[0] + c.tr[1] * at, lambda m=m, k=k: trade(m, k).start()))
                events.append((c.tr[2] + c.tr[3] * at, lambda m=m, k=k: (came(m, k).wait_recv(), share(m, k, p.t).start())))
            else:
                events.append((c.tr[0] + c.tr[1] * at, lambda m=m: share(m, 0, p.t).start()))
    def release():
        pl.semaphore_signal(o.go, inc=1, device_id=(1 - p.s, p.d, p.t), device_id_type=MESH)

    events.append((c.go_at, lambda: pl.when(p.s == 0)(release)))
    for _, run in sorted(events, key=lambda e: e[0]):
        run()
    for copy in bounce:
        copy.wait()
    waits.append(local(o.pack_v, o.pk.at[rows_of(p.d, R)]))
    for m in range(3):
        waits.append(local(o.block_v.at[m], block(m, p.d, p.t)))

    for mask in range(1, n, 2):
        taken(mask, SHARED).wait_recv()
        mirror(mask, p.t).start()
    for q in range(len(cuts)):
        for mask in range(1, n, 2):
            if q != SHARED:
                taken(mask, q).wait_recv()
    for mask in range(1, n):
        mirror(mask, 1 - p.t).wait_recv()
        mirror(mask, p.t).wait_send()
    for k in range(n):
        for m in range(3):
            share(m, k, 1 - p.t).wait_recv()
    for q in range(len(cuts)):
        for mask in range(0, n, 2):
            for bit in range(lowest(mask, n)):
                give(mask, bit, q).wait_send()
    for k in range(n):
        for m in range(3):
            if k:
                trade(m, k).wait_send()
            share(m, k, p.t).wait_send()
    for copy in waits:
        copy.wait()
    last = local(o.pk.at[:, pl.ds(c.qkv + c.heads, LANES)], o.gcol)
    last.wait()
    o.grow_v[...] = o.gcol[...].astype(F32).T[c.rank : c.rank + 8]
    last = local(o.grow_v, o.grow)
    last.wait()


def load_weights(c, o, local):
    qn, on = c.qkv, c.heads
    got = [
        local(o.pk.at[:, pl.ds(qn + on, c.small)], o.sm_v),
        local(o.pk.at[:, pl.ds(0, qn)], o.qkv_v),
        local(o.pk.at[:, pl.ds(qn, on)], o.ot_v),
        local(o.gw, o.gw_v),
        local(o.uw, o.uw_v),
        local(o.dw, o.dw_v),
    ]
    return SimpleNamespace(sm=got[0], qkv=got[1], ot=got[2], gw=got[3], uw=got[4], dw=got[5])


def weight_scratch(c):
    return dict(
        sm_v=pltpu.VMEM((c.width, c.small), BF),
        qkv_v=pltpu.VMEM((c.width, c.qkv), BF),
        ot_v=pltpu.VMEM((c.width, c.heads), BF),
        gw_v=pltpu.VMEM((c.width, 2 * c.hb), BF),
        uw_v=pltpu.VMEM((c.width, 2 * c.hb), BF),
        dw_v=pltpu.VMEM((c.width, 2 * c.hb), BF),
    )


LL, LR, LG, LP = (0, 128), (128, 128), (256, 256), (512, 256)


def cols_of(cut):
    return (slice(None), pl.ds(*cut))


def enter(p, o, sender):
    barrier = pltpu.get_barrier_semaphore()

    def signal(device):
        pl.semaphore_signal(barrier, inc=1, device_id=device, device_id_type=MESH)

    partner = (1 - p.s, p.d, p.t)
    pl.when(p.s == sender)(lambda: signal(partner))
    line_greet(p, signal)
    line = p.A + 1
    pl.semaphore_wait(barrier, jnp.where(p.s == sender, line, line + 1))

    @pl.when(p.s == 1 - sender)
    def _():
        pl.semaphore_signal(o.ready, inc=1, device_id=partner, device_id_type=MESH)


def line_greet(p, signal):
    signal((p.s, p.d, 1 - p.t))
    signal((p.s, p.a * 2 + 1 - p.b, p.t))
    steps_of(p, lambda row: signal((p.s, row * 2 + p.b, p.t)))


def again(p):
    barrier = pltpu.get_barrier_semaphore()
    line_greet(p, lambda device: pl.semaphore_signal(barrier, inc=1, device_id=device, device_id_type=MESH))
    pl.semaphore_wait(barrier, p.A + 1)


def view(c, o, m, buffers, sems):
    slot = m if c.slots == 2 else 0
    names = {name: getattr(o, name + str(slot)) for name in buffers}
    names.update({name: getattr(o, name + str(m)) for name in sems})
    return SimpleNamespace(**names)


def twice(c, buffers, sems):
    out = {}
    for slot in range(c.slots):
        out.update({name + str(slot): spec for name, spec in buffers.items()})
    for m in range(2):
        out.update({name + str(m): spec for name, spec in sems.items()})
    return out


def run_stages(c, p, order, stages):
    if c.slots == 1:
        order = [item for m in range(2) for item in order if item[1] == m]
    for name, m in order:
        if c.slots == 1 and name == FIRST and m == 1:
            stages[0][LAST]()
            again(p)
        stages[m][name]()
    for m in range(2) if c.slots == 2 else (1,):
        stages[m][LAST]()


FIRST, GIVE, OWN, REST, SUMS, PASS, LAST = range(7)
BEGIN, PROJ, JOIN, TAIL_STAGE, MIDDLE, HEADS_STAGE, ENTRY = range(10, 17)


def line_stages(c, p, v, hidden_part, down_part, ready):
    start, carry, collect, finish = line_scatter(
        p, v.acc, v.other, v.got, v.step_got, c.r, c.halves, (v.rxs, v.rxr, v.rzs, v.rzr), v.down_v
    )
    link = SimpleNamespace()

    def begin():
        link.forward, link.arrive, link.gathered = line_gather(p, v.xbuf, c.r, (v.gzs, v.gzr, v.gxs, v.gxr))

    def own():
        ready(0)
        hidden_part(p.b)

    def rest():
        link.arrive()
        hidden_part(1 - p.b)
        ready(1)
        for h in range(HALVES):
            down_part(1 - p.b, v.other, h)
            start(h)
        for h in range(HALVES):
            down_part(p.b, v.acc, h)

    def sums():
        for h in range(HALVES):
            carry(h)

    def total():
        for h in range(HALVES):
            collect(h)

    def end():
        link.gathered()
        for h in range(HALVES):
            finish(h)

    return SimpleNamespace(begin=begin, give=lambda: link.forward(), own=own, rest=rest, sums=sums, total=total, end=end)


def once(*copies):
    state = [False]

    def run():
        if not state[0]:
            state[0] = True
            for copy in copies:
                copy.wait()

    return run


def forward_stages(c, p, o, v, m, w, local):
    r, width, hb2 = c.r, c.width, 2 * c.hb
    pair = (p.s, p.d, 1 - p.t)
    mine, theirs = rows_of(p.t, r), rows_of(1 - p.t, r)
    gain = lambda i: o.gains[i : i + 1, :]
    hand = rcopy(v.act_v, v.hid, v.hs.at[0], v.hr.at[0], (1 - p.s, p.d, p.t))
    first = pltpu.make_async_copy(o.hidden.at[m], v.hid, v.fsem.at[0])
    send = rcopy(v.nbuf.at[mine], v.nbuf.at[mine], v.ys.at[0], v.yr.at[0], pair)
    swap = rcopy(v.ysend, v.ygot, v.ys.at[1], v.yr.at[1], pair)
    keep = []

    def stash(*pairs):
        keep.extend(local(src, dst.at[m]) for src, dst in pairs)

    def normed_of():
        x = v.hid[...].astype(F32)
        return x, x * rms_of(x) * gain(0)

    def begin():
        lv = local(o.lin.at[m], v.lv)
        v.lv_wait = lv.wait

        @pl.when(p.s == 0)
        def _():
            first.start()
            first.wait()

        pl.when(p.s == 1)(hand.wait_recv)
        v.nbuf[mine, :] = normed_of()[1].astype(BF)
        send.start()
        w.sm()
        lane = lax.broadcasted_iota(jnp.int32, (r, LANES), 1)
        mid = jnp.where(lane < c.rank, nn(v.nbuf[mine, :], o.sm_v[cols_of(LL)]), 0.0)
        v.lmid_v[...] = mid.astype(BF)
        v.lraw_v[...] = nt(v.lmid_v[...], o.sm_v[cols_of(LR)])
        stash((v.hid, o.xlow), (v.lmid_v, o.lmid), (v.lraw_v, o.lraw))

    def proj():
        w.qkv()
        rcopy(v.nbuf.at[theirs], v.nbuf.at[theirs], v.ys.at[0], v.yr.at[0], pair).wait_recv()

        @tiles(c.qkv, 256)
        def _(at):
            v.qraw_v[:, at] = nn(v.nbuf[...], o.qkv_v[:, at])

        cos, sin = o.cos[...], o.sin[...]
        q_gain, k_gain = o.gains[6:7, 0:HEAD], o.gains[7:8, 0:HEAD]
        allowed = o.allowed[m] > 0.5
        kraw = v.qraw_v[:, pl.ds(c.heads, HEAD)]
        vraw = v.qraw_v[:, pl.ds(c.heads + HEAD, HEAD)]
        key = rotate(kraw * rms_of(kraw) * k_gain, cos, sin).astype(BF)
        value = (vraw * rms_of(vraw)).astype(BF)
        for h in range(c.heads // HEAD):
            at = pl.ds(h * HEAD, HEAD)
            raw = v.qraw_v[:, at]
            query = rotate(raw * rms_of(raw) * q_gain, cos, sin).astype(BF)
            scores = jnp.where(allowed, nt(query, key) * HEAD**-0.5, NEG)
            shifted = jnp.exp(scores - jnp.max(scores, axis=-1, keepdims=True))
            prob = shifted / jnp.sum(shifted, axis=-1, keepdims=True)
            v.heads_v[:, at] = nn(prob.astype(BF), value).astype(BF)
        w.ot()

        @tiles(width, 256)
        def _(at):
            v.acc[0 : 2 * r, at] = nt(v.heads_v[...], o.ot_v[at, :])

        v.ysend[...] = v.acc[theirs, :].astype(BF)
        swap.start()
        stash((v.nbuf, o.nfull), (v.qraw_v, o.qraw), (v.heads_v, o.heads))

    def join():
        x, normed = normed_of()
        swap.wait()
        att = v.acc[mine, :] + v.ygot[...].astype(F32)
        v.att_v[...] = att
        lraw = v.lraw_v[...]
        comb = (x + att * rms_of(att) * gain(1) + normed + lraw * rms_of(lraw) * gain(2)) * RH
        v.comb_v[...] = comb
        v.xbuf[p.b, rows_of(p.a, r), :] = (comb * rms_of(comb) * gain(3)).astype(BF)
        line.begin()
        stash((v.att_v, o.att), (v.comb_v, o.comb))

    def hidden_part(col):
        @tiles(hb2, min(256, hb2))
        def _(at):
            gate = nn(v.xbuf[col], o.gw_v[:, at])
            up = nn(v.xbuf[col], o.uw_v[:, at])
            v.gate_v[col, :, at] = gate.astype(BF)
            v.up_v[col, :, at] = up.astype(BF)
            v.geglu_v[col, :, at] = (gelu(gate) * up).astype(BF)

    def down_part(col, dest, h):
        start, size = c.halves[h]

        @tiles(size, 256)
        def _(at):
            at = pl.ds(pl.multiple_of(start + at.start, 256), 256)
            dest[:, at] = nt(v.geglu_v[col], o.dw_v[at, :]).astype(dest.dtype)

    def ready(i):
        if i == 0:
            w.gw()
            w.uw()
        else:
            w.dw()

    line = line_stages(c, p, v, hidden_part, down_part, ready)

    def rest():
        line.rest()
        stash((v.xbuf, o.pfull), (v.gate_v, o.gate), (v.up_v, o.up), (v.geglu_v, o.geglu))

    def tail():
        line.total()
        down = v.down_v[...]
        resid = v.comb_v[...] + down * rms_of(down) * gain(4)
        v.rf_v[...] = resid
        v.resid_v[...] = resid.astype(BF)
        graw = nn(v.resid_v[...], o.sm_v[cols_of(LG)])
        v.graw_v[...] = graw
        v.lv_wait()
        v.llow_v[...] = (gelu(graw) * v.lv[...].astype(F32)).astype(BF)
        proj = nt(v.llow_v[...], o.sm_v[cols_of(LP)])
        v.proj_v[...] = proj
        v.act_v[...] = (v.rf_v[...] + proj * rms_of(proj) * gain(5)).astype(BF)

        @pl.when(p.s == 0)
        def _():
            if m == 0:
                pl.semaphore_wait(o.ready, 1)
            hand.start()

        stash((v.down_v, o.down), (v.resid_v, o.resid), (v.graw_v, o.graw), (v.llow_v, o.llow), (v.proj_v, o.proj))
        stash((v.act_v, o.act))

    def end():
        send.wait_send()
        line.end()
        pl.when(p.s == 0)(hand.wait_send)
        for copy in keep:
            copy.wait()

    return {
        FIRST: begin, PROJ: proj, JOIN: join, GIVE: line.give, OWN: line.own, REST: rest, SUMS: line.sums,
        TAIL_STAGE: tail, LAST: end,
    }


FORWARD_ORDER = (
    (FIRST, 0), (PROJ, 0), (JOIN, 0), (FIRST, 1), (PROJ, 1), (GIVE, 0), (JOIN, 1), (OWN, 0), (GIVE, 1), (REST, 0),
    (OWN, 1), (SUMS, 0), (REST, 1), (TAIL_STAGE, 0), (SUMS, 1), (TAIL_STAGE, 1),
)


def waits_of(c, o, local):
    got = load_weights(c, o, local)
    return SimpleNamespace(**{name: once(copy) for name, copy in vars(got).items()})


def forward_kernel(c, o):
    p = place(c.n)
    local = Local(o.lsem)
    w = waits_of(c, o, local)
    enter(p, o, 0)
    views = [view(c, o, m, forward_buffers(c), stage_sems(c) | dict(hid=None)) for m in range(2)]
    stages = [forward_stages(c, p, o, views[m], m, w, local) for m in range(2)]
    run_stages(c, p, FORWARD_ORDER, stages)


def stash_shapes(c):
    m, r, w, q = 2, c.r, c.width, 2 * c.r
    ar, hb2 = c.n // 2 * c.r, 2 * c.hb
    return dict(
        act=((m, r, w), BF),
        xlow=((m, r, w), BF),
        nfull=((m, q, w), BF),
        qraw=((m, q, c.qkv), F32),
        heads=((m, q, c.heads), BF),
        att=((m, r, w), F32),
        lmid=((m, r, LANES), BF),
        lraw=((m, r, w), F32),
        comb=((m, r, w), F32),
        pfull=((m, 2, ar, w), BF),
        gate=((m, 2, ar, hb2), BF),
        up=((m, 2, ar, hb2), BF),
        geglu=((m, 2, ar, hb2), BF),
        down=((m, r, w), F32),
        resid=((m, r, w), BF),
        graw=((m, r, c.per), F32),
        llow=((m, r, c.per), BF),
        proj=((m, r, w), F32),
    )


TAIL = "_v"
GROW = "grow"


def scratch_of(shapes):
    return {name + TAIL: pltpu.VMEM(shape[1:], kind) for name, (shape, kind) in shapes.items()}


def line_buffers(c):
    ar = c.n // 2 * c.r
    return dict(
        xbuf=pltpu.VMEM((2, ar, c.width), BF),
        acc=pltpu.VMEM((ar, c.width), F32),
        other=pltpu.VMEM((ar, c.width), BF),
        got=pltpu.VMEM((ar, c.width), BF),
        step_got=pltpu.VMEM((ar, c.width), BF),
        ysend=pltpu.VMEM((c.r, c.width), BF),
        ygot=pltpu.VMEM((c.r, c.width), BF),
        lv=pltpu.VMEM((c.r, c.per), BF),
    )


def stage_sems(c):
    return dict(
        fsem=dma(1), hs=dma(1), hr=dma(1), ys=dma(2), yr=dma(2), **gather_sems(c.n // 2), **scatter_sems(c.n // 2, HALVES)
    )


def forward_buffers(c):
    shapes = stash_shapes(c)
    own = {name: shapes[name] for name in shapes if name not in ("xlow", "nfull", "pfull")}
    return dict(nbuf=pltpu.VMEM((2 * c.r, c.width), BF), rf_v=pltpu.VMEM((c.r, c.width), F32), **scratch_of(own), **line_buffers(c))


def shared_scratch(c):
    return dict(**weight_scratch(c), lsem=dma(80), ready=pltpu.SemaphoreType.REGULAR)


def forward_pass(c, weights, data, tables):
    scratch = dict(
        **twice(c, forward_buffers(c), stage_sems(c) | dict(hid=pltpu.VMEM((c.r, c.width), BF))), **shared_scratch(c)
    )
    return launch(
        lambda o: forward_kernel(c, o),
        0,
        dict(**weights, hidden=data.hidden, lin=data.lin),
        tables,
        stash_shapes(c),
        scratch,
    )


def backward_stages(c, p, o, v, m, w, local):
    r, width, hb2 = c.r, c.width, 2 * c.hb
    pair = (p.s, p.d, 1 - p.t)
    mine, theirs = rows_of(p.t, r), rows_of(1 - p.t, r)
    gain = lambda i: o.gains[i : i + 1, :]
    hand = rcopy(v.hid, v.hid, v.hs.at[0], v.hr.at[0], (1 - p.s, p.d, p.t))
    first = pltpu.make_async_copy(o.cot.at[m], v.hid, v.fsem.at[0])
    send = rcopy(v.abuf.at[mine], v.abuf.at[mine], v.ys.at[0], v.yr.at[0], pair)
    swap = rcopy(v.ysend, v.ygot, v.ys.at[1], v.yr.at[1], pair)
    keep, need = [], {}

    def stash(*pairs):
        keep.extend(local(src, dst.at[m]) for src, dst in pairs)

    def fetch():
        loads = (
            ((o.proj, v.proj_v), (o.graw, v.graw_v), (o.lin, v.lv)),
            ((o.down, v.down_v),),
            ((o.gate, v.gate_v), (o.up, v.up_v)),
            ((o.comb, v.comb_v), (o.att, v.att_v), (o.lraw, v.lraw_v)),
            ((o.xlow, v.xlow_v), (o.qraw, v.qraw_v)),
        )
        for i, group in enumerate(loads):
            need[i] = [local(src.at[m], dst) for src, dst in group]

    def have(i):
        for copy in need[i]:
            copy.wait()

    def begin():
        if c.slots == 1:
            fetch()

        @pl.when(p.s == 1)
        def _():
            first.start()
            first.wait()

        pl.when(p.s == 0)(hand.wait_recv)
        have(0)
        v.ggr_v[...] = jnp.zeros_like(v.ggr_v)
        dproj, v.ggr_v[5:6, :] = rms_back(v.proj_v[...], gain(5), v.hid[...].astype(F32))
        v.plow_v[...] = dproj.astype(BF)
        w.sm()
        dmid = nn(v.plow_v[...], o.sm_v[cols_of(LP)])
        value, slope = gelu_both(v.graw_v[...])
        v.lgrad_v[...] = value * dmid
        v.grlow_v[...] = (dmid * v.lv[...].astype(F32) * slope).astype(BF)
        dres = v.hid[...].astype(F32) + nt(v.grlow_v[...], o.sm_v[cols_of(LG)])
        v.igrad_v[...] = dres
        have(1)
        ddown, v.ggr_v[4:5, :] = rms_back(v.down_v[...], gain(4), dres)
        v.xbuf[p.b, rows_of(p.a, r), :] = ddown.astype(BF)
        line.begin()
        stash((v.lgrad_v, o.lgrad), (v.plow_v, o.plow), (v.grlow_v, o.grlow))

    def hidden_part(col):
        @tiles(hb2, min(256, hb2))
        def _(at):
            dgeglu = nn(v.xbuf[col], o.dw_v[:, at])
            value, slope = gelu_both(v.gate_v[col, :, at].astype(F32))
            up = v.up_v[col, :, at].astype(F32)
            v.up_v[col, :, at] = (dgeglu * value).astype(BF)
            v.gate_v[col, :, at] = (dgeglu * up * slope).astype(BF)

    def down_part(col, dest, h):
        start, size = c.halves[h]

        @tiles(size, 256)
        def _(at):
            at = pl.ds(pl.multiple_of(start + at.start, 256), 256)
            part = nt(v.gate_v[col], o.gw_v[at, :]) + nt(v.up_v[col], o.uw_v[at, :])
            dest[:, at] = part.astype(dest.dtype)

    def ready(i):
        if i == 0:
            w.dw()
            have(2)
        else:
            w.gw()
            w.uw()

    line = line_stages(c, p, v, hidden_part, down_part, ready)

    def rest():
        line.rest()
        stash((v.xbuf, o.dfull), (v.gate_v, o.dgl), (v.up_v, o.dul))

    def middle():
        line.total()
        have(3)
        dcomb, v.ggr_v[3:4, :] = rms_back(v.comb_v[...], gain(3), v.down_v[...])
        even = (v.igrad_v[...] + dcomb) * RH
        v.igrad_v[...] = even
        datt, v.ggr_v[1:2, :] = rms_back(v.att_v[...], gain(1), even)
        v.abuf[mine, :] = datt.astype(BF)
        send.start()
        dlraw, v.ggr_v[2:3, :] = rms_back(v.lraw_v[...], gain(2), v.igrad_v[...])
        v.lrlow_v[...] = dlraw.astype(BF)
        v.lmg_v[...] = nn(v.lrlow_v[...], o.sm_v[cols_of(LR)]).astype(BF)
        v.proj_v[...] = v.igrad_v[...] + nt(v.lmg_v[...], o.sm_v[cols_of(LL)])
        stash((v.lrlow_v, o.lrlow), (v.lmg_v, o.lmg))

    def heads():
        w.ot()
        rcopy(v.abuf.at[theirs], v.abuf.at[theirs], v.ys.at[0], v.yr.at[0], pair).wait_recv()

        @tiles(c.heads, 256)
        def _(at):
            v.hgrad_v[:, at] = nn(v.abuf[...], o.ot_v[:, at]).astype(BF)

        have(4)
        cos, sin = o.cos[...], o.sin[...]
        q_gain, k_gain = o.gains[6:7, 0:HEAD], o.gains[7:8, 0:HEAD]
        allowed = o.allowed[m] > 0.5
        k_at, v_at = pl.ds(c.heads, HEAD), pl.ds(c.heads + HEAD, HEAD)
        kraw, vraw = v.qraw_v[:, k_at], v.qraw_v[:, v_at]
        key = rotate(kraw * rms_of(kraw) * k_gain, cos, sin).astype(BF)
        value = (vraw * rms_of(vraw)).astype(BF)
        dkey = jnp.zeros(kraw.shape, F32)
        dvalue = jnp.zeros(vraw.shape, F32)
        dq_gain = jnp.zeros((1, HEAD), F32)
        for h in range(c.heads // HEAD):
            at = pl.ds(h * HEAD, HEAD)
            raw = v.qraw_v[:, at]
            query = rotate(raw * rms_of(raw) * q_gain, cos, sin).astype(BF)
            scores = jnp.where(allowed, nt(query, key) * HEAD**-0.5, NEG)
            shifted = jnp.exp(scores - jnp.max(scores, axis=-1, keepdims=True))
            prob = shifted / jnp.sum(shifted, axis=-1, keepdims=True)
            hgrad = v.hgrad_v[:, at]
            dprob = nt(hgrad, value)
            dvalue = dvalue + tn(prob.astype(BF), hgrad)
            inner = jnp.sum(prob * dprob, axis=-1, keepdims=True)
            dscore = (prob * (dprob - inner)).astype(BF)
            dquery = nn(dscore, key) * HEAD**-0.5
            dkey = dkey + tn(dscore, query) * HEAD**-0.5
            draw, dg = rms_back(raw, q_gain, rotate_back(dquery, cos, sin))
            dq_gain = dq_gain + dg
            v.dqkv_v[:, at] = draw.astype(BF)
        draw, dk_gain = rms_back(kraw, k_gain, rotate_back(dkey, cos, sin))
        v.dqkv_v[:, k_at] = draw.astype(BF)
        v.dqkv_v[:, v_at] = plain_back(vraw, dvalue).astype(BF)
        v.ggr_v[6:7, 0:HEAD] = dq_gain
        v.ggr_v[7:8, 0:HEAD] = dk_gain
        w.qkv()

        @tiles(width, 256)
        def _(at):
            v.acc[0 : 2 * r, at] = nt(v.dqkv_v[...], o.qkv_v[at, :])

        v.ysend[...] = v.acc[theirs, :].astype(BF)
        swap.start()
        stash((v.abuf, o.afull), (v.dqkv_v, o.dqkv))

    def entry():
        swap.wait()
        dnorm = v.proj_v[...] + v.acc[mine, :] + v.ygot[...].astype(F32)
        dx, v.ggr_v[0:1, :] = rms_back(v.xlow_v[...].astype(F32), gain(0), dnorm)
        dx = dx + v.igrad_v[...]
        v.igrad_v[...] = dx

        @pl.when(p.s == 1)
        def _():
            v.hid[...] = dx.astype(BF)
            if m == 0:
                pl.semaphore_wait(o.ready, 1)
            hand.start()

        stash((v.igrad_v, o.igrad), (v.ggr_v, o.ggr))

    def end():
        send.wait_send()
        line.end()
        pl.when(p.s == 1)(hand.wait_send)
        for copy in keep:
            copy.wait()

    return {
        FIRST: begin, GIVE: line.give, OWN: line.own, REST: rest, SUMS: line.sums, MIDDLE: middle, HEADS_STAGE: heads,
        ENTRY: entry, LAST: end, BEGIN: fetch,
    }


BACKWARD_ORDER = (
    (FIRST, 0), (GIVE, 0), (OWN, 0), (FIRST, 1), (REST, 0), (GIVE, 1), (OWN, 1), (SUMS, 0), (REST, 1), (MIDDLE, 0),
    (HEADS_STAGE, 0), (SUMS, 1), (ENTRY, 0), (MIDDLE, 1), (HEADS_STAGE, 1), (ENTRY, 1),
)


def backward_kernel(c, o):
    p = place(c.n)
    local = Local(o.lsem)
    views = [view(c, o, m, backward_buffers(c), stage_sems(c) | dict(hid=None)) for m in range(2)]
    late = {}
    w = SimpleNamespace(**{name: (lambda name=name: late[name]()) for name in ("sm", "qkv", "ot", "gw", "uw", "dw")})
    stages = [backward_stages(c, p, o, views[m], m, w, local) for m in range(2)]
    if c.slots == 2:
        stages[0][BEGIN]()
    late.update(vars(waits_of(c, o, local)))
    if c.slots == 2:
        stages[1][BEGIN]()
    enter(p, o, 1)
    run_stages(c, p, BACKWARD_ORDER, stages)


def grad_shapes(c):
    m, r, w, q = 2, c.r, c.width, 2 * c.r
    ar, hb2 = c.n // 2 * c.r, 2 * c.hb
    return dict(
        igrad=((m, r, w), F32),
        lgrad=((m, r, c.per), F32),
        plow=((m, r, w), BF),
        grlow=((m, r, c.per), BF),
        dfull=((m, 2, ar, w), BF),
        dgl=((m, 2, ar, hb2), BF),
        dul=((m, 2, ar, hb2), BF),
        lrlow=((m, r, w), BF),
        lmg=((m, r, LANES), BF),
        afull=((m, q, w), BF),
        dqkv=((m, q, c.qkv), BF),
        ggr=((m, 8, w), F32),
    )


READ = ("proj", "graw", "down", "gate", "up", "comb", "att", "lraw", "xlow", "qraw")


def backward_buffers(c):
    shapes, kept = grad_shapes(c), stash_shapes(c)
    own = {name: shapes[name] for name in shapes if name not in ("dfull", "afull", "dgl", "dul")}
    return dict(
        abuf=pltpu.VMEM((2 * c.r, c.width), BF),
        hgrad_v=pltpu.VMEM((2 * c.r, c.heads), BF),
        **scratch_of(own),
        **scratch_of({name: kept[name] for name in READ}),
        **line_buffers(c),
    )


def backward_pass(c, weights, data, tables, stash):
    scratch = dict(
        **twice(c, backward_buffers(c), stage_sems(c) | dict(hid=pltpu.VMEM((c.r, c.width), BF))), **shared_scratch(c)
    )
    return launch(
        lambda o: backward_kernel(c, o),
        3,
        dict(**weights, cot=data.cot, lin=data.lin, **{name: stash[name] for name in READ}),
        tables,
        grad_shapes(c),
        scratch,
    )


def return_kernel(c, o):
    p = place(c.n)
    n, A, R, hb = c.n, c.n // 2, c.R, c.hb
    pair = (p.s, p.d, 1 - p.t)
    side = (p.s, p.a * 2 + 1 - p.b, p.t)
    barrier = pltpu.get_barrier_semaphore()

    def signal(device):
        pl.semaphore_signal(barrier, inc=1, device_id=device, device_id_type=MESH)

    for k in range(1, n):
        signal((p.s, lax.rem(p.d + k, n), p.t))
    signal(pair)
    pl.semaphore_wait(barrier, n)
    local = Local(o.lsem)
    outs = ((o.pfull, o.dgl), (o.pfull, o.dul), (o.dfull, o.geglu))

    def swap(m, k):
        at = rows_of(lax.rem(p.d + k, n), R)
        return rcopy(o.fsend.at[m, at], o.fgot.at[m, at], o.ys.at[m, k], o.yr.at[m, k], pair)

    def ffn_out(m, source):
        return (o.gg, o.gu, o.gd)[m].at[:, rows_of(source, hb)]

    def trade(m, k):
        dest = lax.rem(p.d + k, n)
        return rcopy(
            o.fown.at[m, rows_of(dest, R)], ffn_out(m, p.d), o.ts.at[m, k], o.tr.at[m, k], (p.s, dest, p.t)
        )

    def came(m, k):
        source = lax.rem(p.d + n - k, n)
        return rcopy(o.fown.at[m, rows_of(p.d, R)], ffn_out(m, source), o.ts.at[m, k], o.tr.at[m, k], side)

    order = [*range(1, n), 0]
    inputs = {0: [local(outs[0][0], o.x_v), local(outs[0][1], o.y_v.at[0])], 1: [local(outs[1][1], o.y_v.at[1])]}

    def ffn_grad(m):
        for copy in inputs[m]:
            copy.wait()
        y = o.y_v.at[m % 2]
        tokens = 4 * y.shape[1]

        @tiles(c.width, 256)
        def _(rows):
            x = o.x_v[:, :, :, rows].reshape(-1, 256)
            mine = y[:, :, :, rows_of(p.t, hb)].reshape(-1, hb)
            o.fown[m, rows, :] = tn(x, mine).astype(BF)
            theirs = y[:, :, :, rows_of(1 - p.t, hb)].reshape(-1, hb)
            o.fsend[m, rows, :] = tn(x, theirs).astype(BF)

        for k in order:
            swap(m, k).start()
        if m == 0:
            inputs[2] = [local(outs[2][1], o.y_v.at[0])]
        if m == 1:
            inputs[2].append(local(outs[2][0], o.x_v))

    need = [
        local(getattr(o, name), getattr(o, name + TAIL))
        for name in ("nfull", "dqkv", "afull", "heads", "lrlow", "lmid", "resid", "grlow", "plow", "llow", "lmg", "gcol")
    ]
    base = c.qkv + c.heads

    def half(t):
        size = c.small // 2
        return pl.ds(pl.multiple_of(base + t * size, LANES), size)

    def slots(h):
        return pl.ds(*c.parts[h])

    def cols(h):
        return half(p.t) if c.parts[h][0] == base else slots(h)

    stage, last, finish = cube_scatter(p, o.acc, o.got, R, cols, slots, (o.rs, o.rr), o.gp_v)
    merge = rcopy(o.acc.at[:, half(1 - p.t)], o.sgot, o.ss.at[0], o.sr.at[0], pair)
    mine_copies = []

    def grad(x, y, at, block=512):
        tokens = 2 * x.shape[1]

        @tiles(c.width, block)
        def _(rows):
            left = x[:, :, rows].reshape(tokens, block)
            o.acc[rows, at] = tn(left, y[...].reshape(tokens, y.shape[2])).astype(BF)

    def ffn_block(m, k):
        rows = rows_of(lax.rem(p.d + k, n), R)
        swap(m, k).wait_recv()
        total = o.fown[m, rows, :].astype(F32) + o.fgot[m, rows, :].astype(F32)
        o.fown[m, rows, :] = total.astype(BF)
        if k:
            trade(m, k).start()
        else:
            mine_copies.append(local(o.fown.at[m, rows], ffn_out(m, p.d)))

    def part_grad(h):
        begin, size = c.parts[h]
        if begin < c.qkv:
            grad(o.nfull_v, o.dqkv_v.at[:, :, pl.ds(begin, size)], pl.ds(begin, size))
        elif begin < base:
            grad(o.afull_v, o.heads_v.at[:, :, pl.ds(begin - c.qkv, size)], pl.ds(begin, size))
        else:
            merge.wait()

            @tiles(c.width, 512)
            def _(rows):
                at = (rows, half(p.t))
                o.acc[at] = (o.acc[at].astype(F32) + o.sgot[rows, :].astype(F32)).astype(BF)

    def shared_grad():
        mine = rows_of(p.t, c.r)
        lane = lax.broadcasted_iota(jnp.int32, (512, LANES), 1)

        @tiles(c.width, 512)
        def _(rows):
            left = tn(o.nfull_v[0, mine, rows], o.lmg_v[0]) + tn(o.nfull_v[1, mine, rows], o.lmg_v[1])
            gains = o.gcol_v[rows, :].astype(F32)
            o.acc[rows, pl.ds(base, LANES)] = jnp.where(lane < c.rank, left, gains).astype(BF)

        grad(o.lrlow_v, o.lmid_v, pl.ds(base + LANES, LANES))
        grad(o.resid_v, o.grlow_v, pl.ds(base + 2 * LANES, c.per))
        grad(o.plow_v, o.llow_v, pl.ds(base + 2 * LANES + c.per, c.per))
        merge.start()

    def attn_ready():
        for copy in need:
            copy.wait()

    r0, per, lag, g1, g2 = c.kg
    top = lowest(0, n)
    events = [(-3.0, lambda: ffn_grad(0)), (-2.0, attn_ready), (1.3, shared_grad), (g1, lambda: ffn_grad(1)), (g2, lambda: ffn_grad(2))]
    for m in range(3):
        for i, k in enumerate(order):
            events.append((r0 + (m * n + i) * 8 / (n * per), lambda m=m, k=k: ffn_block(m, k)))
    for h in range(len(c.parts)):
        events.append((h, lambda h=h: (part_grad(h), stage(h, 0))))
        for bit in range(1, top):
            events.append((h + lag[min(bit, len(lag)) - 1], lambda h=h, bit=bit: stage(h, bit)))
        events.append((h + lag[-1] + 0.01, lambda h=h: last(h)))
    for _, run in sorted(events, key=lambda e: e[0]):
        run()
    rest = rcopy(o.gp_v.at[:, half(p.t)], o.gp_v.at[:, half(p.t)], o.ss.at[1], o.sr.at[1], pair)
    rest.start()
    rest.wait_send()
    theirs = o.gp_v.at[:, half(1 - p.t)]
    rcopy(theirs, theirs, o.ss.at[1], o.sr.at[1], pair).wait_recv()
    out = local(o.gp_v, o.gp)
    for m in range(3):
        for k in range(n):
            swap(m, k).wait_send()
            if k:
                came(m, k).wait_recv()
                trade(m, k).wait_send()
    for q in range(len(c.parts)):
        finish(q)
    for copy in [*mine_copies, out]:
        copy.wait()


def fetch_weights(c, arrays, gains):
    n, q = c.n, len(c.cuts)
    outs = dict(
        pk=((c.width, c.total), BF),
        gw=((c.width, 2 * c.hb), BF),
        uw=((c.width, 2 * c.hb), BF),
        dw=((c.width, 2 * c.hb), BF),
        grow=((8, c.width), F32),
    )
    scratch = dict(
        gcol=pltpu.VMEM((c.width, LANES), BF),
        grow_v=pltpu.VMEM((8, c.width), F32),
        pack_v=pltpu.VMEM((c.R, c.total), BF),
        out_v=pltpu.VMEM((c.heads, c.R), BF),
        lp_v=pltpu.VMEM((c.per, c.R), BF),
        lr_v=pltpu.VMEM((c.rank, c.R), BF),
        rows_v=pltpu.VMEM((LANES, c.R), F32),
        down_v=pltpu.VMEM((n * c.hb, c.R), BF),
        down_t=pltpu.VMEM((c.R, n * c.hb), BF),
        block_v=pltpu.VMEM((3, c.R, c.hb), BF),
        ms=dma(n), mr=dma(n), gs=dma(n, q), gr=dma(n, q), ts=dma(n, 3), tr=dma(n, 3), ys=dma(n, 3), yr=dma(n, 3), lsem=dma(24),
        go=pltpu.SemaphoreType.REGULAR,
    )
    return launch(lambda o: fetch_kernel(c, o), 6, arrays, gains, outs, scratch)


def return_grads(c, f, g, gcol):
    n = c.n
    R = c.R
    flat = ((R, n * c.hb), BF)
    outs = dict(gp=((R, c.total), BF), gg=flat, gu=flat, gd=flat)
    arrays = dict(
        nfull=f.nfull, dqkv=g.dqkv, afull=g.afull, heads=f.heads, lrlow=g.lrlow, lmid=f.lmid, resid=f.resid,
        grlow=g.grlow, plow=g.plow, llow=f.llow, lmg=g.lmg, gcol=gcol,
    )
    scratch = dict(
        acc=pltpu.VMEM((c.width, c.total), BF),
        got=pltpu.VMEM(((n - 1) * R, c.total - c.small // 2), BF),
        gp_v=pltpu.VMEM((R, c.total), BF),
        fown=pltpu.VMEM((3, c.width, c.hb), BF),
        fgot=pltpu.VMEM((3, c.width, c.hb), BF),
        fsend=pltpu.VMEM((3, c.width, c.hb), BF),
        x_v=pltpu.VMEM(f.pfull.shape, BF),
        y_v=pltpu.VMEM((2, *g.dgl.shape), BF),
        sgot=pltpu.VMEM((c.width, c.small // 2), BF),
        ys=dma(3, n), yr=dma(3, n), ts=dma(3, n), tr=dma(3, n), ss=dma(2), sr=dma(2), lsem=dma(24),
        rs=dma(len(c.parts), n), rr=dma(len(c.parts), n),
        **{name + TAIL: pltpu.VMEM(v.shape, v.dtype) for name, v in arrays.items()},
    )
    big = dict(pfull=f.pfull, dgl=g.dgl, dul=g.dul, dfull=g.dfull, geglu=f.geglu)
    return launch(lambda o: return_kernel(c, o), 7, dict(**arrays, **big), {}, outs, scratch)


def widen_kernel(c, o):
    local = Local(o.lsem)
    hb, R, rank = c.hb, c.R, c.rank
    loads = [local(o.gp, o.gp_v), local(o.gd, o.g_v.at[2]), local(o.gg, o.g_v.at[0]), local(o.gu, o.g_v.at[1])]
    base = c.qkv + c.heads
    loads[0].wait()
    o.f_v[...] = o.gp_v[:, pl.ds(0, c.qkv)].astype(F32)
    out = [
        local(o.f_v.at[:, pl.ds(0, c.heads)], o.q),
        local(o.f_v.at[:, pl.ds(c.heads, HEAD)], o.k),
        local(o.f_v.at[:, pl.ds(c.heads + HEAD, HEAD)], o.v),
    ]
    for i, (g, w) in enumerate(((0, o.wg), (1, o.wu))):
        loads[2 + i].wait()
        o.w_v[i] = o.g_v[g].astype(F32)
        out.append(local(o.w_v.at[i], w))
    loads[1].wait()
    for k in range(c.n):
        o.d_v[pl.ds(k * hb, hb), :] = o.g_v[2, :, pl.ds(k * hb, hb)].astype(F32).T
    out.append(local(o.d_v, o.wd))
    for i in range(0, c.heads, HEAD):
        o.t_v[pl.ds(i, HEAD), :] = o.gp_v[:, pl.ds(c.qkv + i, HEAD)].astype(F32).T
    out.append(local(o.t_v, o.out))
    left = o.gp_v[:, pl.ds(base, LANES)].astype(F32)
    o.ll[...] = left[:, :rank]
    rows = left.T
    for i, gain in enumerate((o.g0, o.g1, o.g2, o.g3, o.g4, o.g5, o.g6, o.g7)):
        gain[...] = rows[rank + i : rank + i + 1, 0 : gain.shape[1]]
    o.lr[...] = o.gp_v[:, pl.ds(base + LANES, LANES)].astype(F32).T[:rank]
    o.lg[...] = o.gp_v[:, pl.ds(base + 2 * LANES, c.per)].astype(F32)
    o.lp[...] = o.gp_v[:, pl.ds(base + 2 * LANES + c.per, c.per)].astype(F32).T
    for copy in out:
        copy.wait()


def widen(c, done):
    R, wide = c.R, c.n * c.hb
    outs = dict(
        q=((R, c.heads), F32), k=((R, HEAD), F32), v=((R, HEAD), F32),
        out=((c.heads, R), F32), wg=((R, wide), F32), wu=((R, wide), F32), wd=((wide, R), F32),
    )
    row, head = ((1, R), F32), ((1, HEAD // c.n), F32)
    small = dict(
        ll=((R, c.rank), F32), lr=((c.rank, R), F32), lg=((R, c.per), F32), lp=((c.per, R), F32),
        g0=row, g1=row, g2=row, g3=row, g4=row, g5=row, g6=head, g7=head,
    )
    scratch = dict(
        gp_v=pltpu.VMEM((R, c.total), BF), f_v=pltpu.VMEM((R, c.qkv), F32), t_v=pltpu.VMEM((c.heads, R), F32),
        g_v=pltpu.VMEM((3, R, wide), BF), w_v=pltpu.VMEM((2, R, wide), F32), d_v=pltpu.VMEM((wide, R), F32),
        lsem=dma(16),
    )
    return launch(lambda o: widen_kernel(c, o), None, done, {}, outs, scratch, small)


def body(
    hidden, layer_inputs, span_starts, cotangent, input_gain, query_weight, key_projection, value_projection,
    query_gain, key_norm_gain, output_weight, attention_gain, laurel_left, laurel_right, laurel_gain, prefeed_gain,
    gate_weight, up_weight, down_weight, postfeed_gain, layer_gate, layer_project, layer_gain,
):
    n, nt_ = lax.axis_size(D), lax.axis_size(T)
    t = lax.axis_index(T)
    rank = laurel_left.shape[2]
    width = hidden.shape[3]
    R = width // n
    heads = query_weight.shape[2]
    qkv = heads + 2 * HEAD
    per = layer_gate.shape[2]
    small = 2 * LANES + 2 * per
    base = qkv + heads
    c = SimpleNamespace(
        n=n, R=R, r=hidden.shape[2], width=width, heads=heads, qkv=qkv, per=per, small=small, rank=rank,
        total=qkv + heads + small, hb=gate_weight.shape[2] // n,
        cuts=((0, qkv), (base, small), (qkv, heads)),
        parts=(*((i, 512) for i in range(0, base, 512)), (base, small // 2)),
        slots=2 if n <= 8 else 1, ag=(12.0, 6.0, 12.0), tr=(1.0, 2.5, 30.0, 3.0), by_matrix=True, go_at=GO_AT, kg=KG,
        halves=tuple((h * width // HALVES, width // HALVES) for h in range(HALVES)),
    )
    weights = fetch_weights(
        c,
        dict(
            query=query_weight[0], key=key_projection[0], value=value_projection[0], out=output_weight[0],
            lr=laurel_right[0], lg=layer_gate[0], lp=layer_project[0],
            gate=gate_weight[0], up=up_weight[0], down=down_weight[0],
        ),
        dict(
            ll=laurel_left[0], g0=input_gain, g1=attention_gain, g2=laurel_gain, g3=prefeed_gain, g4=postfeed_gain,
            g5=layer_gain, g6=query_gain, g7=key_norm_gain,
        ),
    )
    columns = weights.pop(GROW)
    short = HEAD // n
    head_gains = columns[6:].reshape(2, n, R)[:, :, :short].reshape(2, HEAD)
    gain_rows = jnp.concatenate([columns[:6], jnp.pad(head_gains, ((0, 0), (0, width - HEAD)))], axis=0)

    span = c.r * nt_
    position = jnp.arange(span, dtype=jnp.int32)
    begin = span_starts[:, 0][:, None]
    inside = (position[None] >= begin) & (position[None] < begin + IMG)
    allowed = (position[None, :] <= position[:, None])[None] | (inside[:, :, None] & inside[:, None, :])
    half = HEAD // 2
    frequency = jnp.exp(jnp.arange(half, dtype=F32) * (-2.0 * math.log(10000.0) / HEAD))
    angles = jnp.arange(span, dtype=F32)[:, None] * frequency[None, :]
    tables = dict(gains=gain_rows, cos=jnp.cos(angles), sin=jnp.sin(angles), allowed=allowed.astype(F32))
    data = SimpleNamespace(hidden=hidden[:, 0], lin=layer_inputs[0, :, 0], cot=cotangent[:, 0])

    stash = forward_pass(c, weights, data, tables)
    grads = backward_pass(c, weights, data, tables, stash)
    f, g = SimpleNamespace(**stash), SimpleNamespace(**grads)

    sums = g.ggr[0] + g.ggr[1]
    head_sums = jnp.pad(sums[6:, :HEAD].reshape(2, n, short), ((0, 0), (0, 0), (0, R - short))).reshape(2, width)
    gain_cols = jnp.concatenate([sums[:6], head_sums], axis=0).T
    gcol = jnp.pad(gain_cols, ((0, 0), (rank, LANES - rank - 8))).astype(BF)
    w = SimpleNamespace(**widen(c, return_grads(c, f, g, gcol)))
    return (
        f.act[None, :, None],
        g.igrad[None, :, None],
        g.lgrad[None, :, None],
        w.g0,
        w.q[None],
        w.k[None],
        w.v[None],
        w.g6,
        w.g7,
        w.out[None],
        w.g1,
        w.ll[None],
        w.lr[None],
        w.g2,
        w.g3,
        w.wg[None],
        w.wu[None],
        w.wd[None],
        w.g4,
        w.lg[None],
        w.lp[None],
        w.g5,
    )


def solution(mesh):
    rows, cols = P(S, D, T), P(S, T, D)
    vec, tall, flat = P(S, D), P(S, D, None), P(S, None, D)
    seq, out = P(None, D, T, None), P(S, None, D, T, None)
    weights = (
        vec, rows, rows, rows, vec, vec, cols, vec, tall, flat, vec, vec, rows, rows, cols, vec, tall, flat, vec,
    )
    return jax.shard_map(
        body,
        mesh=mesh,
        in_specs=(seq, out, P(None, D), seq, *weights),
        out_specs=(out, out, out, *weights),
        check_vma=False,
    )
```

```python
import math
from types import SimpleNamespace

import jax
import jax.numpy as jnp
from jax import lax
from jax.experimental import pallas as pl
from jax.experimental.pallas import tpu as pltpu
from jax.sharding import PartitionSpec as P

S, D, T = "section", "dp", "tensor"
MESH = pl.DeviceIdType.MESH
BF, F32 = jnp.bfloat16, jnp.float32
HEAD = 256
IMG = 64
EPS = 1e-06
RH = 0.5**0.5
NEG = -1e30
LANES = 128
GELU_C = math.sqrt(2.0 / math.pi)
GELU_K = 0.044715
VMEM_LIMIT = 61 << 20
HALVES = 2
GATHER_PARTS = 2
GO_AT = 60.0
SHARED = 1
KG = (2.5, 3.0, (2.1, 3.2, 4.3), 0.6, 2.6)


def rms_of(v):
    return lax.rsqrt(jnp.mean(v * v, axis=-1, keepdims=True) + EPS)


def rms_back(v, gain, grad):
    r = rms_of(v)
    unit = v * r
    inner = grad * gain
    back = r * (inner - unit * jnp.mean(inner * unit, axis=-1, keepdims=True))
    return back, jnp.sum(grad * unit, axis=0, keepdims=True)


def plain_back(v, grad):
    r = rms_of(v)
    unit = v * r
    return r * (grad - unit * jnp.mean(grad * unit, axis=-1, keepdims=True))


def gelu(v):
    return 0.5 * v * (1.0 + jnp.tanh(GELU_C * (v + GELU_K * v * v * v)))


def gelu_both(v):
    square = v * v
    th = jnp.tanh(GELU_C * v * (1.0 + GELU_K * square))
    value = 0.5 * v * (1.0 + th)
    slope = 0.5 * (1.0 + th) + 0.5 * v * (1.0 - th * th) * GELU_C * (1.0 + 3.0 * GELU_K * square)
    return value, slope


def rotate(v, cos, sin):
    half = HEAD // 2
    front, back = v[:, :half], v[:, half:]
    return jnp.concatenate([front * cos - back * sin, back * cos + front * sin], axis=-1)


def rotate_back(g, cos, sin):
    half = HEAD // 2
    front, back = g[:, :half], g[:, half:]
    return jnp.concatenate([front * cos + back * sin, back * cos - front * sin], axis=-1)


def nn(x, w):
    return jnp.dot(x, w, preferred_element_type=F32)


def nt(x, w):
    return lax.dot_general(x, w, (((1,), (1,)), ((), ())), preferred_element_type=F32)


def tn(x, w):
    return lax.dot_general(x, w, (((0,), (0,)), ((), ())), preferred_element_type=F32)


def tiles(count, step):
    def wrap(fn):
        def one(j, carry):
            fn(pl.ds(pl.multiple_of(j * step, step), step))
            return carry

        lax.fori_loop(0, count // step, one, 0)

    return wrap


def place(n):
    s, d, t = lax.axis_index(S), lax.axis_index(D), lax.axis_index(T)
    return SimpleNamespace(s=s, d=d, t=t, a=lax.div(d, 2), b=lax.rem(d, 2), n=n, A=n // 2)


def rcopy(src, dst, send, recv, device):
    return pltpu.make_async_remote_copy(
        src_ref=src, dst_ref=dst, send_sem=send, recv_sem=recv, device_id=device, device_id_type=MESH
    )


def rows_of(index, size):
    return pl.ds(pl.multiple_of(index * size, size), size)


class Local:
    def __init__(self, sems):
        self.sems, self.used = sems, 0

    def __call__(self, src, dst):
        copy = pltpu.make_async_copy(src, dst, self.sems.at[self.used])
        self.used += 1
        copy.start()
        return copy


def steps_of(p, fn, far_first=False):
    for delta in range(p.A - 1, 0, -1) if far_first else range(1, p.A):
        pl.when(p.a - delta >= 0)(lambda: fn(p.a - delta))
        pl.when(p.a + delta < p.A)(lambda: fn(p.a + delta))


def line_gather(p, buf, size, sems):
    zs, zr, xs, xr = sems
    side = (p.s, p.a * 2 + 1 - p.b, p.t)
    part = size // GATHER_PARTS

    def at(col, row, g):
        return buf.at[col, pl.ds(pl.multiple_of(row * size + g * part, part), part)]

    def along(row, g):
        return rcopy(at(p.b, p.a, g), at(p.b, p.a, g), zs.at[row, g], zr.at[p.a, g], (p.s, row * 2 + p.b, p.t))

    def came(row, g):
        return rcopy(at(p.b, row, g), at(p.b, row, g), zs.at[row, g], zr.at[row, g], side)

    def across(col, row, g):
        return rcopy(at(col, row, g), at(col, row, g), xs.at[row, g], xr.at[row, g], side)

    def each(fn):
        def run(row):
            for g in range(GATHER_PARTS):
                fn(row, g)

        return run

    for g in range(GATHER_PARTS):
        steps_of(p, lambda row: along(row, g).start(), True)
        across(p.b, p.a, g).start()

    def forward(row, g):
        came(row, g).wait_recv()
        across(p.b, row, g).start()

    def arrive():
        for row in range(p.A):
            each(lambda row, g: across(1 - p.b, row, g).wait_recv())(row)

    def finish():
        steps_of(p, each(lambda row, g: along(row, g).wait_send()))
        for row in range(p.A):
            each(lambda row, g: across(p.b, row, g).wait_send())(row)

    return lambda: steps_of(p, each(forward)), arrive, finish


def line_scatter(p, acc, other, got, step_got, size, cuts, sems, out):
    xs, xr, zs, zr = sems
    side = (p.s, p.a * 2 + 1 - p.b, p.t)

    def part(row, h):
        return (rows_of(row, size), pl.ds(cuts[h][0], cuts[h][1]))

    def across(h, row):
        at = part(row, h)
        return rcopy(other.at[at], got.at[at], xs.at[h, row], xr.at[h, row], side)

    def along(h, row):
        return rcopy(
            other.at[part(row, h)], step_got.at[part(p.a, h)], zs.at[h, row], zr.at[h, p.a], (p.s, row * 2 + p.b, p.t)
        )

    def came(h, row):
        return rcopy(other.at[part(row, h)], step_got.at[part(row, h)], zs.at[h, row], zr.at[h, row], side)

    def start(h):
        steps_of(p, lambda row: across(h, row).start(), True)
        across(h, p.a).start()

    def carry(h):
        def pass_on(row):
            at = part(row, h)
            across(h, row).wait()
            other[at] = (acc[at] + got[at].astype(F32)).astype(BF)
            along(h, row).start()

        steps_of(p, pass_on, True)

    def collect(h):
        across(h, p.a).wait()
        at = part(p.a, h)
        cols = (slice(None), at[1])
        out[cols] = acc[at] + got[at].astype(F32)

        def add(row):
            came(h, row).wait_recv()
            out[cols] += step_got[part(row, h)].astype(F32)

        steps_of(p, add)

    def finish(h):
        steps_of(p, lambda row: along(h, row).wait_send())

    return start, carry, collect, finish


def lowest(mask, n):
    bit = 0
    while (1 << bit) < n and not mask >> bit & 1:
        bit += 1
    return bit


def flip(d, mask):
    bit = 0
    result = d
    while 1 << bit <= mask:
        if mask >> bit & 1:
            result = result + (1 - 2 * lax.rem(lax.div(d, 1 << bit), 2)) * (1 << bit)
        bit += 1
    return result


def cube_scatter(p, acc, got, size, cols, slots, sems, out):
    send, recv = sems
    n = p.n

    def block(mask):
        return rows_of(flip(p.d, mask), size)

    def message(h, mask):
        bit = lowest(mask, n)
        return rcopy(
            acc.at[block(mask), cols(h)],
            got.at[pl.ds((mask - 1) * size, size), slots(h)],
            send.at[h, mask],
            recv.at[h, mask],
            (p.s, flip(p.d, 1 << bit), p.t),
        )

    def stage(h, bit):
        for mask in range(1, n):
            if lowest(mask, n) == bit:
                at = (block(mask), cols(h))
                total = None
                for below in range(bit):
                    came = mask | 1 << below
                    message(h, came).wait_recv()
                    term = got[pl.ds((came - 1) * size, size), slots(h)].astype(F32)
                    total = term if total is None else total + term
                if total is not None:
                    acc[at] = (acc[at].astype(F32) + total).astype(BF)
                message(h, mask).start()

    def last(h):
        total = acc[block(0), cols(h)].astype(F32)
        for below in range(lowest(0, n)):
            message(h, 1 << below).wait_recv()
            total = total + got[pl.ds(((1 << below) - 1) * size, size), slots(h)].astype(F32)
        out[:, cols(h)] = total.astype(BF)

    def finish(h):
        for mask in range(1, n):
            message(h, mask).wait_send()

    return stage, last, finish


def dma(*shape):
    return pltpu.SemaphoreType.DMA(shape)


def gather_sems(A):
    g = GATHER_PARTS
    return dict(gzs=dma(A, g), gzr=dma(A, g), gxs=dma(A, g), gxr=dma(A, g))


def scatter_sems(A, parts):
    return dict(rxs=dma(parts, A), rxr=dma(parts, A), rzs=dma(parts, A), rzr=dma(parts, A))


HBM = pl.BlockSpec(memory_space=pltpu.HBM)
VM = pl.BlockSpec(memory_space=pltpu.VMEM)


def launch(kernel, cid, hbm_in, vmem_in, outs, scratch, small=None):
    small = small or {}
    everything = [*hbm_in, *vmem_in, *outs, *small, *scratch]

    def run(*refs):
        kernel(SimpleNamespace(**dict(zip(everything, refs))))

    results = pl.pallas_call(
        run,
        out_shape=[jax.ShapeDtypeStruct(*spec) for spec in (*outs.values(), *small.values())],
        in_specs=[HBM] * len(hbm_in) + [VM] * len(vmem_in),
        out_specs=[HBM] * len(outs) + [VM] * len(small),
        scratch_shapes=list(scratch.values()),
        compiler_params=pltpu.CompilerParams(
            collective_id=cid, has_side_effects=cid is not None, vmem_limit_bytes=VMEM_LIMIT
        ),
    )(*hbm_in.values(), *vmem_in.values())
    return dict(zip((*outs, *small), results))


def fetch_kernel(c, o):
    p = place(c.n)
    n, A, R, hb = c.n, c.n // 2, c.R, c.hb
    barrier = pltpu.get_barrier_semaphore()

    def signal(device):
        pl.semaphore_signal(barrier, inc=1, device_id=device, device_id_type=MESH)

    for k in range(1, n):
        signal((p.s, lax.rem(p.d + k, n), p.t))
    signal((p.s, p.d, 1 - p.t))
    signal((1 - p.s, p.d, p.t))
    pl.semaphore_wait(barrier, n + 1)

    @pl.when(p.s == 1)
    def _():
        pl.semaphore_wait(o.go, 1)

    side = (p.s, p.a * 2 + 1 - p.b, p.t)
    pair = (p.s, p.d, 1 - p.t)
    cuts = c.cuts
    bits = lowest(0, n)
    local = Local(o.lsem)
    waits = []

    def half(t):
        size = c.small // 2
        return pl.ds(pl.multiple_of(c.qkv + c.heads + t * size, LANES), size)

    def cols(q):
        return half(p.t) if q == SHARED else pl.ds(*cuts[q])

    def mirror(mask, t):
        at = (rows_of(flip(p.d, mask), R), half(t))
        return rcopy(o.pk.at[at], o.pk.at[at], o.ms.at[mask], o.mr.at[mask], pair)

    def give(mask, bit, q):
        rows, cs = rows_of(flip(p.d, mask), R), cols(q)
        src = o.pk.at[rows, cs] if mask else o.pack_v.at[:, cs]
        far = mask | 1 << bit
        return rcopy(src, o.pk.at[rows, cs], o.gs.at[far, q], o.gr.at[far, q], (p.s, flip(p.d, 1 << bit), p.t))

    def taken(mask, q):
        at = (rows_of(flip(p.d, mask), R), cols(q))
        return rcopy(o.pk.at[at], o.pk.at[at], o.gs.at[mask, q], o.gr.at[mask, q], side)

    def pass_on(mask, q):
        if mask:
            taken(mask, q).wait_recv()
        for bit in reversed(range(lowest(mask, n))):
            give(mask, bit, q).start()
        if mask and q == SHARED:
            mirror(mask, p.t).start()

    ffn = ((o.gate, o.gw), (o.up, o.uw), (o.down_t, o.dw))

    def block(m, source, half):
        return ffn[m][1].at[rows_of(source, R), rows_of(half, hb)]

    def trade(m, k):
        dest = lax.rem(p.d + k, n)
        return rcopy(
            ffn[m][0].at[:, rows_of(dest, hb)], block(m, p.d, p.t), o.ts.at[k, m], o.tr.at[k, m], (p.s, dest, p.t)
        )

    def came(m, k):
        source = lax.rem(p.d + n - k, n)
        return rcopy(
            ffn[m][0].at[:, rows_of(p.d, hb)], block(m, source, p.t), o.ts.at[k, m], o.tr.at[k, m], side
        )

    def share(m, k, half):
        source = lax.rem(p.d + n - k, n)
        src = ffn[m][0].at[:, rows_of(p.d, hb)] if k == 0 else block(m, source, half)
        return rcopy(src, block(m, source, half), o.ys.at[k, m], o.yr.at[k, m], pair)

    qkv, base, rank = c.qkv, c.qkv + c.heads, c.rank
    first = [
        local(o.query, o.pack_v.at[:, pl.ds(0, c.heads)]),
        local(o.key, o.pack_v.at[:, pl.ds(c.heads, HEAD)]),
        local(o.value, o.pack_v.at[:, pl.ds(c.heads + HEAD, HEAD)]),
    ]
    second = [local(o.out, o.out_v)]
    third = [local(o.lg, o.pack_v.at[:, pl.ds(base + 2 * LANES, c.per)]), local(o.lp, o.lp_v), local(o.lr, o.lr_v)]
    fourth = [local(o.down, o.down_v)]
    bounce = [local(ffn[m][0].at[:, rows_of(p.d, hb)], o.block_v.at[m]) for m in range(2)]

    def turned(x):
        return x.astype(F32).T.astype(BF)

    def prepare(q):
        if q == 0:
            for copy in first:
                copy.wait()
        elif q == 2:
            for copy in second:
                copy.wait()
            for i in range(0, c.heads, HEAD):
                o.pack_v[:, pl.ds(qkv + i, HEAD)] = turned(o.out_v[pl.ds(i, HEAD), :])
        else:
            for copy in third:
                copy.wait()
            o.rows_v[...] = jnp.zeros_like(o.rows_v)
            for i, gain in enumerate((o.g0, o.g1, o.g2, o.g3, o.g4, o.g5, o.g6, o.g7)):
                o.rows_v[rank + i : rank + i + 1, 0 : gain.shape[1]] = gain[...].astype(F32)
            left = o.rows_v[...].T
            o.pack_v[:, pl.ds(base, LANES)] = left.astype(BF)
            o.pack_v[:, pl.ds(base, rank)] = o.ll[...]
            o.rows_v[...] = jnp.zeros_like(o.rows_v)
            o.rows_v[0:rank, :] = o.lr_v[...].astype(F32)
            o.pack_v[:, pl.ds(base + LANES, LANES)] = o.rows_v[...].T.astype(BF)
            o.pack_v[:, pl.ds(base + 2 * LANES + c.per, c.per)] = turned(o.lp_v[...])

    def prepare_down():
        for copy in fourth:
            copy.wait()
        for k in range(n):
            o.down_t[:, pl.ds(k * hb, hb)] = turned(o.down_v[pl.ds(k * hb, hb), :])
        bounce.append(local(o.down_t.at[:, rows_of(p.d, hb)], o.block_v.at[2]))

    events = []
    inner = sorted((mask for mask in range(2, n, 2)), key=lambda mask: (-lowest(mask, n), mask))
    for q in range(len(cuts)):
        events.append((0.0 + 0.1 * q, lambda q=q: (prepare(q), pass_on(0, q))))
        for i, mask in enumerate(inner):
            events.append((c.ag[0] + c.ag[1] * q + c.ag[2] * i, lambda q=q, mask=mask: pass_on(mask, q)))
    events.append((c.tr[0] + c.tr[1] * (2 * n - 2), prepare_down))
    for k in range(n):
        for m in range(3):
            at = m * n + k
            if k:
                events.append((c.tr[0] + c.tr[1] * at, lambda m=m, k=k: trade(m, k).start()))
                events.append((c.tr[2] + c.tr[3] * at, lambda m=m, k=k: (came(m, k).wait_recv(), share(m, k, p.t).start())))
            else:
                events.append((c.tr[0] + c.tr[1] * at, lambda m=m: share(m, 0, p.t).start()))
    def release():
        pl.semaphore_signal(o.go, inc=1, device_id=(1 - p.s, p.d, p.t), device_id_type=MESH)

    events.append((c.go_at, lambda: pl.when(p.s == 0)(release)))
    for _, run in sorted(events, key=lambda e: e[0]):
        run()
    for copy in bounce:
        copy.wait()
    waits.append(local(o.pack_v, o.pk.at[rows_of(p.d, R)]))
    for m in range(3):
        waits.append(local(o.block_v.at[m], block(m, p.d, p.t)))

    for mask in range(1, n, 2):
        taken(mask, SHARED).wait_recv()
        mirror(mask, p.t).start()
    for q in range(len(cuts)):
        for mask in range(1, n, 2):
            if q != SHARED:
                taken(mask, q).wait_recv()
    for mask in range(1, n):
        mirror(mask, 1 - p.t).wait_recv()
        mirror(mask, p.t).wait_send()
    for k in range(n):
        for m in range(3):
            share(m, k, 1 - p.t).wait_recv()
    for q in range(len(cuts)):
        for mask in range(0, n, 2):
            for bit in range(lowest(mask, n)):
                give(mask, bit, q).wait_send()
    for k in range(n):
        for m in range(3):
            if k:
                trade(m, k).wait_send()
            share(m, k, p.t).wait_send()
    for copy in waits:
        copy.wait()
    last = local(o.pk.at[:, pl.ds(c.qkv + c.heads, LANES)], o.gcol)
    last.wait()
    o.grow_v[...] = o.gcol[...].astype(F32).T[c.rank : c.rank + 8]
    last = local(o.grow_v, o.grow)
    last.wait()


def load_weights(c, o, local):
    qn, on = c.qkv, c.heads
    got = [
        local(o.pk.at[:, pl.ds(qn + on, c.small)], o.sm_v),
        local(o.pk.at[:, pl.ds(0, qn)], o.qkv_v),
        local(o.pk.at[:, pl.ds(qn, on)], o.ot_v),
        local(o.gw, o.gw_v),
        local(o.uw, o.uw_v),
        local(o.dw, o.dw_v),
    ]
    return SimpleNamespace(sm=got[0], qkv=got[1], ot=got[2], gw=got[3], uw=got[4], dw=got[5])


def weight_scratch(c):
    return dict(
        sm_v=pltpu.VMEM((c.width, c.small), BF),
        qkv_v=pltpu.VMEM((c.width, c.qkv), BF),
        ot_v=pltpu.VMEM((c.width, c.heads), BF),
        gw_v=pltpu.VMEM((c.width, 2 * c.hb), BF),
        uw_v=pltpu.VMEM((c.width, 2 * c.hb), BF),
        dw_v=pltpu.VMEM((c.width, 2 * c.hb), BF),
    )


LL, LR, LG, LP = (0, 128), (128, 128), (256, 256), (512, 256)


def cols_of(cut):
    return (slice(None), pl.ds(*cut))


def enter(p, o, sender):
    barrier = pltpu.get_barrier_semaphore()

    def signal(device):
        pl.semaphore_signal(barrier, inc=1, device_id=device, device_id_type=MESH)

    partner = (1 - p.s, p.d, p.t)
    pl.when(p.s == sender)(lambda: signal(partner))
    line_greet(p, signal)
    line = p.A + 1
    pl.semaphore_wait(barrier, jnp.where(p.s == sender, line, line + 1))

    @pl.when(p.s == 1 - sender)
    def _():
        pl.semaphore_signal(o.ready, inc=1, device_id=partner, device_id_type=MESH)


def line_greet(p, signal):
    signal((p.s, p.d, 1 - p.t))
    signal((p.s, p.a * 2 + 1 - p.b, p.t))
    steps_of(p, lambda row: signal((p.s, row * 2 + p.b, p.t)))


def again(p):
    barrier = pltpu.get_barrier_semaphore()
    line_greet(p, lambda device: pl.semaphore_signal(barrier, inc=1, device_id=device, device_id_type=MESH))
    pl.semaphore_wait(barrier, p.A + 1)


def view(c, o, m, buffers, sems):
    slot = m if c.slots == 2 else 0
    names = {name: getattr(o, name + str(slot)) for name in buffers}
    names.update({name: getattr(o, name + str(m)) for name in sems})
    return SimpleNamespace(**names)


def twice(c, buffers, sems):
    out = {}
    for slot in range(c.slots):
        out.update({name + str(slot): spec for name, spec in buffers.items()})
    for m in range(2):
        out.update({name + str(m): spec for name, spec in sems.items()})
    return out


def run_stages(c, p, order, stages):
    if c.slots == 1:
        order = [item for m in range(2) for item in order if item[1] == m]
    for name, m in order:
        if c.slots == 1 and name == FIRST and m == 1:
            stages[0][LAST]()
            again(p)
        stages[m][name]()
    for m in range(2) if c.slots == 2 else (1,):
        stages[m][LAST]()


FIRST, GIVE, OWN, REST, SUMS, PASS, LAST = range(7)
BEGIN, PROJ, JOIN, TAIL_STAGE, MIDDLE, HEADS_STAGE, ENTRY = range(10, 17)


def line_stages(c, p, v, hidden_part, down_part, ready):
    start, carry, collect, finish = line_scatter(
        p, v.acc, v.other, v.got, v.step_got, c.r, c.halves, (v.rxs, v.rxr, v.rzs, v.rzr), v.down_v
    )
    link = SimpleNamespace()

    def begin():
        link.forward, link.arrive, link.gathered = line_gather(p, v.xbuf, c.r, (v.gzs, v.gzr, v.gxs, v.gxr))

    def own():
        ready(0)
        hidden_part(p.b)

    def rest():
        link.arrive()
        hidden_part(1 - p.b)
        ready(1)
        for h in range(HALVES):
            down_part(1 - p.b, v.other, h)
            start(h)
        for h in range(HALVES):
            down_part(p.b, v.acc, h)

    def sums():
        for h in range(HALVES):
            carry(h)

    def total():
        for h in range(HALVES):
            collect(h)

    def end():
        link.gathered()
        for h in range(HALVES):
            finish(h)

    return SimpleNamespace(begin=begin, give=lambda: link.forward(), own=own, rest=rest, sums=sums, total=total, end=end)


def once(*copies):
    state = [False]

    def run():
        if not state[0]:
            state[0] = True
            for copy in copies:
                copy.wait()

    return run


def forward_stages(c, p, o, v, m, w, local):
    r, width, hb2 = c.r, c.width, 2 * c.hb
    pair = (p.s, p.d, 1 - p.t)
    mine, theirs = rows_of(p.t, r), rows_of(1 - p.t, r)
    gain = lambda i: o.gains[i : i + 1, :]
    hand = rcopy(v.act_v, v.hid, v.hs.at[0], v.hr.at[0], (1 - p.s, p.d, p.t))
    first = pltpu.make_async_copy(o.hidden.at[m], v.hid, v.fsem.at[0])
    send = rcopy(v.nbuf.at[mine], v.nbuf.at[mine], v.ys.at[0], v.yr.at[0], pair)
    swap = rcopy(v.ysend, v.ygot, v.ys.at[1], v.yr.at[1], pair)
    keep = []

    def stash(*pairs):
        keep.extend(local(src, dst.at[m]) for src, dst in pairs)

    def normed_of():
        x = v.hid[...].astype(F32)
        return x, x * rms_of(x) * gain(0)

    def begin():
        lv = local(o.lin.at[m], v.lv)
        v.lv_wait = lv.wait

        @pl.when(p.s == 0)
        def _():
            first.start()
            first.wait()

        pl.when(p.s == 1)(hand.wait_recv)
        v.nbuf[mine, :] = normed_of()[1].astype(BF)
        send.start()
        w.sm()
        lane = lax.broadcasted_iota(jnp.int32, (r, LANES), 1)
        mid = jnp.where(lane < c.rank, nn(v.nbuf[mine, :], o.sm_v[cols_of(LL)]), 0.0)
        v.lmid_v[...] = mid.astype(BF)
        v.lraw_v[...] = nt(v.lmid_v[...], o.sm_v[cols_of(LR)])
        stash((v.hid, o.xlow), (v.lmid_v, o.lmid), (v.lraw_v, o.lraw))

    def proj():
        w.qkv()
        rcopy(v.nbuf.at[theirs], v.nbuf.at[theirs], v.ys.at[0], v.yr.at[0], pair).wait_recv()

        @tiles(c.qkv, 256)
        def _(at):
            v.qraw_v[:, at] = nn(v.nbuf[...], o.qkv_v[:, at])

        cos, sin = o.cos[...], o.sin[...]
        q_gain, k_gain = o.gains[6:7, 0:HEAD], o.gains[7:8, 0:HEAD]
        allowed = o.allowed[m] > 0.5
        kraw = v.qraw_v[:, pl.ds(c.heads, HEAD)]
        vraw = v.qraw_v[:, pl.ds(c.heads + HEAD, HEAD)]
        key = rotate(kraw * rms_of(kraw) * k_gain, cos, sin).astype(BF)
        value = (vraw * rms_of(vraw)).astype(BF)
        for h in range(c.heads // HEAD):
            at = pl.ds(h * HEAD, HEAD)
            raw = v.qraw_v[:, at]
            query = rotate(raw * rms_of(raw) * q_gain, cos, sin).astype(BF)
            scores = jnp.where(allowed, nt(query, key) * HEAD**-0.5, NEG)
            shifted = jnp.exp(scores - jnp.max(scores, axis=-1, keepdims=True))
            prob = shifted / jnp.sum(shifted, axis=-1, keepdims=True)
            v.heads_v[:, at] = nn(prob.astype(BF), value).astype(BF)
        w.ot()

        @tiles(width, 256)
        def _(at):
            v.acc[0 : 2 * r, at] = nt(v.heads_v[...], o.ot_v[at, :])

        v.ysend[...] = v.acc[theirs, :].astype(BF)
        swap.start()
        stash((v.nbuf, o.nfull), (v.qraw_v, o.qraw), (v.heads_v, o.heads))

    def join():
        x, normed = normed_of()
        swap.wait()
        att = v.acc[mine, :] + v.ygot[...].astype(F32)
        v.att_v[...] = att
        lraw = v.lraw_v[...]
        comb = (x + att * rms_of(att) * gain(1) + normed + lraw * rms_of(lraw) * gain(2)) * RH
        v.comb_v[...] = comb
        v.xbuf[p.b, rows_of(p.a, r), :] = (comb * rms_of(comb) * gain(3)).astype(BF)
        line.begin()
        stash((v.att_v, o.att), (v.comb_v, o.comb))

    def hidden_part(col):
        @tiles(hb2, min(256, hb2))
        def _(at):
            gate = nn(v.xbuf[col], o.gw_v[:, at])
            up = nn(v.xbuf[col], o.uw_v[:, at])
            v.gate_v[col, :, at] = gate.astype(BF)
            v.up_v[col, :, at] = up.astype(BF)
            v.geglu_v[col, :, at] = (gelu(gate) * up).astype(BF)

    def down_part(col, dest, h):
        start, size = c.halves[h]

        @tiles(size, 256)
        def _(at):
            at = pl.ds(pl.multiple_of(start + at.start, 256), 256)
            dest[:, at] = nt(v.geglu_v[col], o.dw_v[at, :]).astype(dest.dtype)

    def ready(i):
        if i == 0:
            w.gw()
            w.uw()
        else:
            w.dw()

    line = line_stages(c, p, v, hidden_part, down_part, ready)

    def rest():
        line.rest()
        stash((v.xbuf, o.pfull), (v.gate_v, o.gate), (v.up_v, o.up), (v.geglu_v, o.geglu))

    def tail():
        line.total()
        down = v.down_v[...]
        resid = v.comb_v[...] + down * rms_of(down) * gain(4)
        v.rf_v[...] = resid
        v.resid_v[...] = resid.astype(BF)
        graw = nn(v.resid_v[...], o.sm_v[cols_of(LG)])
        v.graw_v[...] = graw
        v.lv_wait()
        v.llow_v[...] = (gelu(graw) * v.lv[...].astype(F32)).astype(BF)
        proj = nt(v.llow_v[...], o.sm_v[cols_of(LP)])
        v.proj_v[...] = proj
        v.act_v[...] = (v.rf_v[...] + proj * rms_of(proj) * gain(5)).astype(BF)

        @pl.when(p.s == 0)
        def _():
            if m == 0:
                pl.semaphore_wait(o.ready, 1)
            hand.start()

        stash((v.down_v, o.down), (v.resid_v, o.resid), (v.graw_v, o.graw), (v.llow_v, o.llow), (v.proj_v, o.proj))
        stash((v.act_v, o.act))

    def end():
        send.wait_send()
        line.end()
        pl.when(p.s == 0)(hand.wait_send)
        for copy in keep:
            copy.wait()

    return {
        FIRST: begin, PROJ: proj, JOIN: join, GIVE: line.give, OWN: line.own, REST: rest, SUMS: line.sums,
        TAIL_STAGE: tail, LAST: end,
    }


FORWARD_ORDER = (
    (FIRST, 0), (PROJ, 0), (JOIN, 0), (FIRST, 1), (PROJ, 1), (GIVE, 0), (JOIN, 1), (OWN, 0), (GIVE, 1), (REST, 0),
    (OWN, 1), (SUMS, 0), (REST, 1), (TAIL_STAGE, 0), (SUMS, 1), (TAIL_STAGE, 1),
)


def waits_of(c, o, local):
    got = load_weights(c, o, local)
    return SimpleNamespace(**{name: once(copy) for name, copy in vars(got).items()})


def forward_kernel(c, o):
    p = place(c.n)
    local = Local(o.lsem)
    w = waits_of(c, o, local)
    enter(p, o, 0)
    views = [view(c, o, m, forward_buffers(c), stage_sems(c) | dict(hid=None)) for m in range(2)]
    stages = [forward_stages(c, p, o, views[m], m, w, local) for m in range(2)]
    run_stages(c, p, FORWARD_ORDER, stages)


def stash_shapes(c):
    m, r, w, q = 2, c.r, c.width, 2 * c.r
    ar, hb2 = c.n // 2 * c.r, 2 * c.hb
    return dict(
        act=((m, r, w), BF),
        xlow=((m, r, w), BF),
        nfull=((m, q, w), BF),
        qraw=((m, q, c.qkv), F32),
        heads=((m, q, c.heads), BF),
        att=((m, r, w), F32),
        lmid=((m, r, LANES), BF),
        lraw=((m, r, w), F32),
        comb=((m, r, w), F32),
        pfull=((m, 2, ar, w), BF),
        gate=((m, 2, ar, hb2), BF),
        up=((m, 2, ar, hb2), BF),
        geglu=((m, 2, ar, hb2), BF),
        down=((m, r, w), F32),
        resid=((m, r, w), BF),
        graw=((m, r, c.per), F32),
        llow=((m, r, c.per), BF),
        proj=((m, r, w), F32),
    )


TAIL = "_v"
GROW = "grow"


def scratch_of(shapes):
    return {name + TAIL: pltpu.VMEM(shape[1:], kind) for name, (shape, kind) in shapes.items()}


def line_buffers(c):
    ar = c.n // 2 * c.r
    return dict(
        xbuf=pltpu.VMEM((2, ar, c.width), BF),
        acc=pltpu.VMEM((ar, c.width), F32),
        other=pltpu.VMEM((ar, c.width), BF),
        got=pltpu.VMEM((ar, c.width), BF),
        step_got=pltpu.VMEM((ar, c.width), BF),
        ysend=pltpu.VMEM((c.r, c.width), BF),
        ygot=pltpu.VMEM((c.r, c.width), BF),
        lv=pltpu.VMEM((c.r, c.per), BF),
    )


def stage_sems(c):
    return dict(
        fsem=dma(1), hs=dma(1), hr=dma(1), ys=dma(2), yr=dma(2), **gather_sems(c.n // 2), **scatter_sems(c.n // 2, HALVES)
    )


def forward_buffers(c):
    shapes = stash_shapes(c)
    own = {name: shapes[name] for name in shapes if name not in ("xlow", "nfull", "pfull")}
    return dict(nbuf=pltpu.VMEM((2 * c.r, c.width), BF), rf_v=pltpu.VMEM((c.r, c.width), F32), **scratch_of(own), **line_buffers(c))


def shared_scratch(c):
    return dict(**weight_scratch(c), lsem=dma(80), ready=pltpu.SemaphoreType.REGULAR)


def forward_pass(c, weights, data, tables):
    scratch = dict(
        **twice(c, forward_buffers(c), stage_sems(c) | dict(hid=pltpu.VMEM((c.r, c.width), BF))), **shared_scratch(c)
    )
    return launch(
        lambda o: forward_kernel(c, o),
        0,
        dict(**weights, hidden=data.hidden, lin=data.lin),
        tables,
        stash_shapes(c),
        scratch,
    )


def backward_stages(c, p, o, v, m, w, local):
    r, width, hb2 = c.r, c.width, 2 * c.hb
    pair = (p.s, p.d, 1 - p.t)
    mine, theirs = rows_of(p.t, r), rows_of(1 - p.t, r)
    gain = lambda i: o.gains[i : i + 1, :]
    hand = rcopy(v.hid, v.hid, v.hs.at[0], v.hr.at[0], (1 - p.s, p.d, p.t))
    first = pltpu.make_async_copy(o.cot.at[m], v.hid, v.fsem.at[0])
    send = rcopy(v.abuf.at[mine], v.abuf.at[mine], v.ys.at[0], v.yr.at[0], pair)
    swap = rcopy(v.ysend, v.ygot, v.ys.at[1], v.yr.at[1], pair)
    keep, need = [], {}

    def stash(*pairs):
        keep.extend(local(src, dst.at[m]) for src, dst in pairs)

    def fetch():
        loads = (
            ((o.proj, v.proj_v), (o.graw, v.graw_v), (o.lin, v.lv)),
            ((o.down, v.down_v),),
            ((o.gate, v.gate_v), (o.up, v.up_v)),
            ((o.comb, v.comb_v), (o.att, v.att_v), (o.lraw, v.lraw_v)),
            ((o.xlow, v.xlow_v), (o.qraw, v.qraw_v)),
        )
        for i, group in enumerate(loads):
            need[i] = [local(src.at[m], dst) for src, dst in group]

    def have(i):
        for copy in need[i]:
            copy.wait()

    def begin():
        if c.slots == 1:
            fetch()

        @pl.when(p.s == 1)
        def _():
            first.start()
            first.wait()

        pl.when(p.s == 0)(hand.wait_recv)
        have(0)
        v.ggr_v[...] = jnp.zeros_like(v.ggr_v)
        dproj, v.ggr_v[5:6, :] = rms_back(v.proj_v[...], gain(5), v.hid[...].astype(F32))
        v.plow_v[...] = dproj.astype(BF)
        w.sm()
        dmid = nn(v.plow_v[...], o.sm_v[cols_of(LP)])
        value, slope = gelu_both(v.graw_v[...])
        v.lgrad_v[...] = value * dmid
        v.grlow_v[...] = (dmid * v.lv[...].astype(F32) * slope).astype(BF)
        dres = v.hid[...].astype(F32) + nt(v.grlow_v[...], o.sm_v[cols_of(LG)])
        v.igrad_v[...] = dres
        have(1)
        ddown, v.ggr_v[4:5, :] = rms_back(v.down_v[...], gain(4), dres)
        v.xbuf[p.b, rows_of(p.a, r), :] = ddown.astype(BF)
        line.begin()
        stash((v.lgrad_v, o.lgrad), (v.plow_v, o.plow), (v.grlow_v, o.grlow))

    def hidden_part(col):
        @tiles(hb2, min(256, hb2))
        def _(at):
            dgeglu = nn(v.xbuf[col], o.dw_v[:, at])
            value, slope = gelu_both(v.gate_v[col, :, at].astype(F32))
            up = v.up_v[col, :, at].astype(F32)
            v.up_v[col, :, at] = (dgeglu * value).astype(BF)
            v.gate_v[col, :, at] = (dgeglu * up * slope).astype(BF)

    def down_part(col, dest, h):
        start, size = c.halves[h]

        @tiles(size, 256)
        def _(at):
            at = pl.ds(pl.multiple_of(start + at.start, 256), 256)
            part = nt(v.gate_v[col], o.gw_v[at, :]) + nt(v.up_v[col], o.uw_v[at, :])
            dest[:, at] = part.astype(dest.dtype)

    def ready(i):
        if i == 0:
            w.dw()
            have(2)
        else:
            w.gw()
            w.uw()

    line = line_stages(c, p, v, hidden_part, down_part, ready)

    def rest():
        line.rest()
        stash((v.xbuf, o.dfull), (v.gate_v, o.dgl), (v.up_v, o.dul))

    def middle():
        line.total()
        have(3)
        dcomb, v.ggr_v[3:4, :] = rms_back(v.comb_v[...], gain(3), v.down_v[...])
        even = (v.igrad_v[...] + dcomb) * RH
        v.igrad_v[...] = even
        datt, v.ggr_v[1:2, :] = rms_back(v.att_v[...], gain(1), even)
        v.abuf[mine, :] = datt.astype(BF)
        send.start()
        dlraw, v.ggr_v[2:3, :] = rms_back(v.lraw_v[...], gain(2), v.igrad_v[...])
        v.lrlow_v[...] = dlraw.astype(BF)
        v.lmg_v[...] = nn(v.lrlow_v[...], o.sm_v[cols_of(LR)]).astype(BF)
        v.proj_v[...] = v.igrad_v[...] + nt(v.lmg_v[...], o.sm_v[cols_of(LL)])
        stash((v.lrlow_v, o.lrlow), (v.lmg_v, o.lmg))

    def heads():
        w.ot()
        rcopy(v.abuf.at[theirs], v.abuf.at[theirs], v.ys.at[0], v.yr.at[0], pair).wait_recv()

        @tiles(c.heads, 256)
        def _(at):
            v.hgrad_v[:, at] = nn(v.abuf[...], o.ot_v[:, at]).astype(BF)

        have(4)
        cos, sin = o.cos[...], o.sin[...]
        q_gain, k_gain = o.gains[6:7, 0:HEAD], o.gains[7:8, 0:HEAD]
        allowed = o.allowed[m] > 0.5
        k_at, v_at = pl.ds(c.heads, HEAD), pl.ds(c.heads + HEAD, HEAD)
        kraw, vraw = v.qraw_v[:, k_at], v.qraw_v[:, v_at]
        key = rotate(kraw * rms_of(kraw) * k_gain, cos, sin).astype(BF)
        value = (vraw * rms_of(vraw)).astype(BF)
        dkey = jnp.zeros(kraw.shape, F32)
        dvalue = jnp.zeros(vraw.shape, F32)
        dq_gain = jnp.zeros((1, HEAD), F32)
        for h in range(c.heads // HEAD):
            at = pl.ds(h * HEAD, HEAD)
            raw = v.qraw_v[:, at]
            query = rotate(raw * rms_of(raw) * q_gain, cos, sin).astype(BF)
            scores = jnp.where(allowed, nt(query, key) * HEAD**-0.5, NEG)
            shifted = jnp.exp(scores - jnp.max(scores, axis=-1, keepdims=True))
            prob = shifted / jnp.sum(shifted, axis=-1, keepdims=True)
            hgrad = v.hgrad_v[:, at]
            dprob = nt(hgrad, value)
            dvalue = dvalue + tn(prob.astype(BF), hgrad)
            inner = jnp.sum(prob * dprob, axis=-1, keepdims=True)
            dscore = (prob * (dprob - inner)).astype(BF)
            dquery = nn(dscore, key) * HEAD**-0.5
            dkey = dkey + tn(dscore, query) * HEAD**-0.5
            draw, dg = rms_back(raw, q_gain, rotate_back(dquery, cos, sin))
            dq_gain = dq_gain + dg
            v.dqkv_v[:, at] = draw.astype(BF)
        draw, dk_gain = rms_back(kraw, k_gain, rotate_back(dkey, cos, sin))
        v.dqkv_v[:, k_at] = draw.astype(BF)
        v.dqkv_v[:, v_at] = plain_back(vraw, dvalue).astype(BF)
        v.ggr_v[6:7, 0:HEAD] = dq_gain
        v.ggr_v[7:8, 0:HEAD] = dk_gain
        w.qkv()

        @tiles(width, 256)
        def _(at):
            v.acc[0 : 2 * r, at] = nt(v.dqkv_v[...], o.qkv_v[at, :])

        v.ysend[...] = v.acc[theirs, :].astype(BF)
        swap.start()
        stash((v.abuf, o.afull), (v.dqkv_v, o.dqkv))

    def entry():
        swap.wait()
        dnorm = v.proj_v[...] + v.acc[mine, :] + v.ygot[...].astype(F32)
        dx, v.ggr_v[0:1, :] = rms_back(v.xlow_v[...].astype(F32), gain(0), dnorm)
        dx = dx + v.igrad_v[...]
        v.igrad_v[...] = dx

        @pl.when(p.s == 1)
        def _():
            v.hid[...] = dx.astype(BF)
            if m == 0:
                pl.semaphore_wait(o.ready, 1)
            hand.start()

        stash((v.igrad_v, o.igrad), (v.ggr_v, o.ggr))

    def end():
        send.wait_send()
        line.end()
        pl.when(p.s == 1)(hand.wait_send)
        for copy in keep:
            copy.wait()

    return {
        FIRST: begin, GIVE: line.give, OWN: line.own, REST: rest, SUMS: line.sums, MIDDLE: middle, HEADS_STAGE: heads,
        ENTRY: entry, LAST: end, BEGIN: fetch,
    }


BACKWARD_ORDER = (
    (FIRST, 0), (GIVE, 0), (OWN, 0), (FIRST, 1), (REST, 0), (GIVE, 1), (OWN, 1), (SUMS, 0), (REST, 1), (MIDDLE, 0),
    (SUMS, 1), (HEADS_STAGE, 0), (ENTRY, 0), (MIDDLE, 1), (HEADS_STAGE, 1), (ENTRY, 1),
)


def backward_kernel(c, o):
    p = place(c.n)
    local = Local(o.lsem)
    views = [view(c, o, m, backward_buffers(c), stage_sems(c) | dict(hid=None)) for m in range(2)]
    late = {}
    w = SimpleNamespace(**{name: (lambda name=name: late[name]()) for name in ("sm", "qkv", "ot", "gw", "uw", "dw")})
    stages = [backward_stages(c, p, o, views[m], m, w, local) for m in range(2)]
    if c.slots == 2:
        stages[0][BEGIN]()
    late.update(vars(waits_of(c, o, local)))
    if c.slots == 2:
        stages[1][BEGIN]()
    enter(p, o, 1)
    run_stages(c, p, BACKWARD_ORDER, stages)


def grad_shapes(c):
    m, r, w, q = 2, c.r, c.width, 2 * c.r
    ar, hb2 = c.n // 2 * c.r, 2 * c.hb
    return dict(
        igrad=((m, r, w), F32),
        lgrad=((m, r, c.per), F32),
        plow=((m, r, w), BF),
        grlow=((m, r, c.per), BF),
        dfull=((m, 2, ar, w), BF),
        dgl=((m, 2, ar, hb2), BF),
        dul=((m, 2, ar, hb2), BF),
        lrlow=((m, r, w), BF),
        lmg=((m, r, LANES), BF),
        afull=((m, q, w), BF),
        dqkv=((m, q, c.qkv), BF),
        ggr=((m, 8, w), F32),
    )


READ = ("proj", "graw", "down", "gate", "up", "comb", "att", "lraw", "xlow", "qraw")


def backward_buffers(c):
    shapes, kept = grad_shapes(c), stash_shapes(c)
    own = {name: shapes[name] for name in shapes if name not in ("dfull", "afull", "dgl", "dul")}
    return dict(
        abuf=pltpu.VMEM((2 * c.r, c.width), BF),
        hgrad_v=pltpu.VMEM((2 * c.r, c.heads), BF),
        **scratch_of(own),
        **scratch_of({name: kept[name] for name in READ}),
        **line_buffers(c),
    )


def backward_pass(c, weights, data, tables, stash):
    scratch = dict(
        **twice(c, backward_buffers(c), stage_sems(c) | dict(hid=pltpu.VMEM((c.r, c.width), BF))), **shared_scratch(c)
    )
    return launch(
        lambda o: backward_kernel(c, o),
        3,
        dict(**weights, cot=data.cot, lin=data.lin, **{name: stash[name] for name in READ}),
        tables,
        grad_shapes(c),
        scratch,
    )


def return_kernel(c, o):
    p = place(c.n)
    n, A, R, hb = c.n, c.n // 2, c.R, c.hb
    pair = (p.s, p.d, 1 - p.t)
    side = (p.s, p.a * 2 + 1 - p.b, p.t)
    barrier = pltpu.get_barrier_semaphore()

    def signal(device):
        pl.semaphore_signal(barrier, inc=1, device_id=device, device_id_type=MESH)

    for k in range(1, n):
        signal((p.s, lax.rem(p.d + k, n), p.t))
    signal(pair)
    pl.semaphore_wait(barrier, n)
    local = Local(o.lsem)
    outs = ((o.pfull, o.dgl), (o.pfull, o.dul), (o.dfull, o.geglu))

    def swap(m, k):
        at = rows_of(lax.rem(p.d + k, n), R)
        return rcopy(o.fsend.at[m, at], o.fgot.at[m, at], o.ys.at[m, k], o.yr.at[m, k], pair)

    def ffn_out(m, source):
        return (o.gg, o.gu, o.gd)[m].at[:, rows_of(source, hb)]

    def trade(m, k):
        dest = lax.rem(p.d + k, n)
        return rcopy(
            o.fown.at[m, rows_of(dest, R)], ffn_out(m, p.d), o.ts.at[m, k], o.tr.at[m, k], (p.s, dest, p.t)
        )

    def came(m, k):
        source = lax.rem(p.d + n - k, n)
        return rcopy(o.fown.at[m, rows_of(p.d, R)], ffn_out(m, source), o.ts.at[m, k], o.tr.at[m, k], side)

    order = [*range(1, n), 0]
    inputs = {0: [local(outs[0][0], o.x_v), local(outs[0][1], o.y_v.at[0])], 1: [local(outs[1][1], o.y_v.at[1])]}

    def ffn_grad(m):
        for copy in inputs[m]:
            copy.wait()
        y = o.y_v.at[m % 2]
        tokens = 4 * y.shape[1]

        @tiles(c.width, 256)
        def _(rows):
            x = o.x_v[:, :, :, rows].reshape(-1, 256)
            mine = y[:, :, :, rows_of(p.t, hb)].reshape(-1, hb)
            o.fown[m, rows, :] = tn(x, mine).astype(BF)
            theirs = y[:, :, :, rows_of(1 - p.t, hb)].reshape(-1, hb)
            o.fsend[m, rows, :] = tn(x, theirs).astype(BF)

        for k in order:
            swap(m, k).start()
        if m == 0:
            inputs[2] = [local(outs[2][1], o.y_v.at[0])]
        if m == 1:
            inputs[2].append(local(outs[2][0], o.x_v))

    need = [
        local(getattr(o, name), getattr(o, name + TAIL))
        for name in ("nfull", "dqkv", "afull", "heads", "lrlow", "lmid", "resid", "grlow", "plow", "llow", "lmg", "gcol")
    ]
    base = c.qkv + c.heads

    def half(t):
        size = c.small // 2
        return pl.ds(pl.multiple_of(base + t * size, LANES), size)

    def slots(h):
        return pl.ds(*c.parts[h])

    def cols(h):
        return half(p.t) if c.parts[h][0] == base else slots(h)

    stage, last, finish = cube_scatter(p, o.acc, o.got, R, cols, slots, (o.rs, o.rr), o.gp_v)
    merge = rcopy(o.acc.at[:, half(1 - p.t)], o.sgot, o.ss.at[0], o.sr.at[0], pair)
    mine_copies = []

    def grad(x, y, at, block=512):
        tokens = 2 * x.shape[1]

        @tiles(c.width, block)
        def _(rows):
            left = x[:, :, rows].reshape(tokens, block)
            o.acc[rows, at] = tn(left, y[...].reshape(tokens, y.shape[2])).astype(BF)

    def ffn_block(m, k):
        rows = rows_of(lax.rem(p.d + k, n), R)
        swap(m, k).wait_recv()
        total = o.fown[m, rows, :].astype(F32) + o.fgot[m, rows, :].astype(F32)
        o.fown[m, rows, :] = total.astype(BF)
        if k:
            trade(m, k).start()
        else:
            mine_copies.append(local(o.fown.at[m, rows], ffn_out(m, p.d)))

    def part_grad(h):
        begin, size = c.parts[h]
        if begin < c.qkv:
            grad(o.nfull_v, o.dqkv_v.at[:, :, pl.ds(begin, size)], pl.ds(begin, size))
        elif begin < base:
            grad(o.afull_v, o.heads_v.at[:, :, pl.ds(begin - c.qkv, size)], pl.ds(begin, size))
        else:
            merge.wait()

            @tiles(c.width, 512)
            def _(rows):
                at = (rows, half(p.t))
                o.acc[at] = (o.acc[at].astype(F32) + o.sgot[rows, :].astype(F32)).astype(BF)

    def shared_grad():
        mine = rows_of(p.t, c.r)
        lane = lax.broadcasted_iota(jnp.int32, (512, LANES), 1)

        @tiles(c.width, 512)
        def _(rows):
            left = tn(o.nfull_v[0, mine, rows], o.lmg_v[0]) + tn(o.nfull_v[1, mine, rows], o.lmg_v[1])
            gains = o.gcol_v[rows, :].astype(F32)
            o.acc[rows, pl.ds(base, LANES)] = jnp.where(lane < c.rank, left, gains).astype(BF)

        grad(o.lrlow_v, o.lmid_v, pl.ds(base + LANES, LANES))
        grad(o.resid_v, o.grlow_v, pl.ds(base + 2 * LANES, c.per))
        grad(o.plow_v, o.llow_v, pl.ds(base + 2 * LANES + c.per, c.per))
        merge.start()

    def attn_ready():
        for copy in need:
            copy.wait()

    r0, per, lag, g1, g2 = c.kg
    top = lowest(0, n)
    events = [(-3.0, lambda: ffn_grad(0)), (-2.0, attn_ready), (1.3, shared_grad), (g1, lambda: ffn_grad(1)), (g2, lambda: ffn_grad(2))]
    for m in range(3):
        for i, k in enumerate(order):
            events.append((r0 + (m * n + i) * 8 / (n * per), lambda m=m, k=k: ffn_block(m, k)))
    for h in range(len(c.parts)):
        events.append((h, lambda h=h: (part_grad(h), stage(h, 0))))
        for bit in range(1, top):
            events.append((h + lag[min(bit, len(lag)) - 1], lambda h=h, bit=bit: stage(h, bit)))
        events.append((h + lag[-1] + 0.01, lambda h=h: last(h)))
    for _, run in sorted(events, key=lambda e: e[0]):
        run()
    rest = rcopy(o.gp_v.at[:, half(p.t)], o.gp_v.at[:, half(p.t)], o.ss.at[1], o.sr.at[1], pair)
    rest.start()
    rest.wait_send()
    theirs = o.gp_v.at[:, half(1 - p.t)]
    rcopy(theirs, theirs, o.ss.at[1], o.sr.at[1], pair).wait_recv()
    out = local(o.gp_v, o.gp)
    for m in range(3):
        for k in range(n):
            swap(m, k).wait_send()
            if k:
                came(m, k).wait_recv()
                trade(m, k).wait_send()
    for q in range(len(c.parts)):
        finish(q)
    for copy in [*mine_copies, out]:
        copy.wait()


def fetch_weights(c, arrays, gains):
    n, q = c.n, len(c.cuts)
    outs = dict(
        pk=((c.width, c.total), BF),
        gw=((c.width, 2 * c.hb), BF),
        uw=((c.width, 2 * c.hb), BF),
        dw=((c.width, 2 * c.hb), BF),
        grow=((8, c.width), F32),
    )
    scratch = dict(
        gcol=pltpu.VMEM((c.width, LANES), BF),
        grow_v=pltpu.VMEM((8, c.width), F32),
        pack_v=pltpu.VMEM((c.R, c.total), BF),
        out_v=pltpu.VMEM((c.heads, c.R), BF),
        lp_v=pltpu.VMEM((c.per, c.R), BF),
        lr_v=pltpu.VMEM((c.rank, c.R), BF),
        rows_v=pltpu.VMEM((LANES, c.R), F32),
        down_v=pltpu.VMEM((n * c.hb, c.R), BF),
        down_t=pltpu.VMEM((c.R, n * c.hb), BF),
        block_v=pltpu.VMEM((3, c.R, c.hb), BF),
        ms=dma(n), mr=dma(n), gs=dma(n, q), gr=dma(n, q), ts=dma(n, 3), tr=dma(n, 3), ys=dma(n, 3), yr=dma(n, 3), lsem=dma(24),
        go=pltpu.SemaphoreType.REGULAR,
    )
    return launch(lambda o: fetch_kernel(c, o), 6, arrays, gains, outs, scratch)


def return_grads(c, f, g, gcol):
    n = c.n
    R = c.R
    flat = ((R, n * c.hb), BF)
    outs = dict(gp=((R, c.total), BF), gg=flat, gu=flat, gd=flat)
    arrays = dict(
        nfull=f.nfull, dqkv=g.dqkv, afull=g.afull, heads=f.heads, lrlow=g.lrlow, lmid=f.lmid, resid=f.resid,
        grlow=g.grlow, plow=g.plow, llow=f.llow, lmg=g.lmg, gcol=gcol,
    )
    scratch = dict(
        acc=pltpu.VMEM((c.width, c.total), BF),
        got=pltpu.VMEM(((n - 1) * R, c.total - c.small // 2), BF),
        gp_v=pltpu.VMEM((R, c.total), BF),
        fown=pltpu.VMEM((3, c.width, c.hb), BF),
        fgot=pltpu.VMEM((3, c.width, c.hb), BF),
        fsend=pltpu.VMEM((3, c.width, c.hb), BF),
        x_v=pltpu.VMEM(f.pfull.shape, BF),
        y_v=pltpu.VMEM((2, *g.dgl.shape), BF),
        sgot=pltpu.VMEM((c.width, c.small // 2), BF),
        ys=dma(3, n), yr=dma(3, n), ts=dma(3, n), tr=dma(3, n), ss=dma(2), sr=dma(2), lsem=dma(24),
        rs=dma(len(c.parts), n), rr=dma(len(c.parts), n),
        **{name + TAIL: pltpu.VMEM(v.shape, v.dtype) for name, v in arrays.items()},
    )
    big = dict(pfull=f.pfull, dgl=g.dgl, dul=g.dul, dfull=g.dfull, geglu=f.geglu)
    return launch(lambda o: return_kernel(c, o), 7, dict(**arrays, **big), {}, outs, scratch)


def widen_kernel(c, o):
    local = Local(o.lsem)
    hb, R, rank = c.hb, c.R, c.rank
    loads = [local(o.gp, o.gp_v), local(o.gd, o.g_v.at[2]), local(o.gg, o.g_v.at[0]), local(o.gu, o.g_v.at[1])]
    base = c.qkv + c.heads
    loads[0].wait()
    o.f_v[...] = o.gp_v[:, pl.ds(0, c.qkv)].astype(F32)
    out = [
        local(o.f_v.at[:, pl.ds(0, c.heads)], o.q),
        local(o.f_v.at[:, pl.ds(c.heads, HEAD)], o.k),
        local(o.f_v.at[:, pl.ds(c.heads + HEAD, HEAD)], o.v),
    ]
    for i, (g, w) in enumerate(((0, o.wg), (1, o.wu))):
        loads[2 + i].wait()
        o.w_v[i] = o.g_v[g].astype(F32)
        out.append(local(o.w_v.at[i], w))
    loads[1].wait()
    for k in range(c.n):
        o.d_v[pl.ds(k * hb, hb), :] = o.g_v[2, :, pl.ds(k * hb, hb)].astype(F32).T
    out.append(local(o.d_v, o.wd))
    for i in range(0, c.heads, HEAD):
        o.t_v[pl.ds(i, HEAD), :] = o.gp_v[:, pl.ds(c.qkv + i, HEAD)].astype(F32).T
    out.append(local(o.t_v, o.out))
    left = o.gp_v[:, pl.ds(base, LANES)].astype(F32)
    o.ll[...] = left[:, :rank]
    rows = left.T
    for i, gain in enumerate((o.g0, o.g1, o.g2, o.g3, o.g4, o.g5, o.g6, o.g7)):
        gain[...] = rows[rank + i : rank + i + 1, 0 : gain.shape[1]]
    o.lr[...] = o.gp_v[:, pl.ds(base + LANES, LANES)].astype(F32).T[:rank]
    o.lg[...] = o.gp_v[:, pl.ds(base + 2 * LANES, c.per)].astype(F32)
    o.lp[...] = o.gp_v[:, pl.ds(base + 2 * LANES + c.per, c.per)].astype(F32).T
    for copy in out:
        copy.wait()


def widen(c, done):
    R, wide = c.R, c.n * c.hb
    outs = dict(
        q=((R, c.heads), F32), k=((R, HEAD), F32), v=((R, HEAD), F32),
        out=((c.heads, R), F32), wg=((R, wide), F32), wu=((R, wide), F32), wd=((wide, R), F32),
    )
    row, head = ((1, R), F32), ((1, HEAD // c.n), F32)
    small = dict(
        ll=((R, c.rank), F32), lr=((c.rank, R), F32), lg=((R, c.per), F32), lp=((c.per, R), F32),
        g0=row, g1=row, g2=row, g3=row, g4=row, g5=row, g6=head, g7=head,
    )
    scratch = dict(
        gp_v=pltpu.VMEM((R, c.total), BF), f_v=pltpu.VMEM((R, c.qkv), F32), t_v=pltpu.VMEM((c.heads, R), F32),
        g_v=pltpu.VMEM((3, R, wide), BF), w_v=pltpu.VMEM((2, R, wide), F32), d_v=pltpu.VMEM((wide, R), F32),
        lsem=dma(16),
    )
    return launch(lambda o: widen_kernel(c, o), None, done, {}, outs, scratch, small)


def body(
    hidden, layer_inputs, span_starts, cotangent, input_gain, query_weight, key_projection, value_projection,
    query_gain, key_norm_gain, output_weight, attention_gain, laurel_left, laurel_right, laurel_gain, prefeed_gain,
    gate_weight, up_weight, down_weight, postfeed_gain, layer_gate, layer_project, layer_gain,
):
    n, nt_ = lax.axis_size(D), lax.axis_size(T)
    t = lax.axis_index(T)
    rank = laurel_left.shape[2]
    width = hidden.shape[3]
    R = width // n
    heads = query_weight.shape[2]
    qkv = heads + 2 * HEAD
    per = layer_gate.shape[2]
    small = 2 * LANES + 2 * per
    base = qkv + heads
    c = SimpleNamespace(
        n=n, R=R, r=hidden.shape[2], width=width, heads=heads, qkv=qkv, per=per, small=small, rank=rank,
        total=qkv + heads + small, hb=gate_weight.shape[2] // n,
        cuts=((0, qkv), (base, small), (qkv, heads)),
        parts=(*((i, 512) for i in range(0, base, 512)), (base, small // 2)),
        slots=2 if n <= 8 else 1, ag=(12.0, 6.0, 12.0), tr=(1.0, 2.5, 30.0, 3.0), by_matrix=True, go_at=GO_AT, kg=KG,
        halves=tuple((h * width // HALVES, width // HALVES) for h in range(HALVES)),
    )
    weights = fetch_weights(
        c,
        dict(
            query=query_weight[0], key=key_projection[0], value=value_projection[0], out=output_weight[0],
            lr=laurel_right[0], lg=layer_gate[0], lp=layer_project[0],
            gate=gate_weight[0], up=up_weight[0], down=down_weight[0],
        ),
        dict(
            ll=laurel_left[0], g0=input_gain, g1=attention_gain, g2=laurel_gain, g3=prefeed_gain, g4=postfeed_gain,
            g5=layer_gain, g6=query_gain, g7=key_norm_gain,
        ),
    )
    columns = weights.pop(GROW)
    short = HEAD // n
    head_gains = columns[6:].reshape(2, n, R)[:, :, :short].reshape(2, HEAD)
    gain_rows = jnp.concatenate([columns[:6], jnp.pad(head_gains, ((0, 0), (0, width - HEAD)))], axis=0)

    span = c.r * nt_
    position = jnp.arange(span, dtype=jnp.int32)
    begin = span_starts[:, 0][:, None]
    inside = (position[None] >= begin) & (position[None] < begin + IMG)
    allowed = (position[None, :] <= position[:, None])[None] | (inside[:, :, None] & inside[:, None, :])
    half = HEAD // 2
    frequency = jnp.exp(jnp.arange(half, dtype=F32) * (-2.0 * math.log(10000.0) / HEAD))
    angles = jnp.arange(span, dtype=F32)[:, None] * frequency[None, :]
    tables = dict(gains=gain_rows, cos=jnp.cos(angles), sin=jnp.sin(angles), allowed=allowed.astype(F32))
    data = SimpleNamespace(hidden=hidden[:, 0], lin=layer_inputs[0, :, 0], cot=cotangent[:, 0])

    stash = forward_pass(c, weights, data, tables)
    grads = backward_pass(c, weights, data, tables, stash)
    f, g = SimpleNamespace(**stash), SimpleNamespace(**grads)

    sums = g.ggr[0] + g.ggr[1]
    head_sums = jnp.pad(sums[6:, :HEAD].reshape(2, n, short), ((0, 0), (0, 0), (0, R - short))).reshape(2, width)
    gain_cols = jnp.concatenate([sums[:6], head_sums], axis=0).T
    gcol = jnp.pad(gain_cols, ((0, 0), (rank, LANES - rank - 8))).astype(BF)
    w = SimpleNamespace(**widen(c, return_grads(c, f, g, gcol)))
    return (
        f.act[None, :, None],
        g.igrad[None, :, None],
        g.lgrad[None, :, None],
        w.g0,
        w.q[None],
        w.k[None],
        w.v[None],
        w.g6,
        w.g7,
        w.out[None],
        w.g1,
        w.ll[None],
        w.lr[None],
        w.g2,
        w.g3,
        w.wg[None],
        w.wu[None],
        w.wd[None],
        w.g4,
        w.lg[None],
        w.lp[None],
        w.g5,
    )


def solution(mesh):
    rows, cols = P(S, D, T), P(S, T, D)
    vec, tall, flat = P(S, D), P(S, D, None), P(S, None, D)
    seq, out = P(None, D, T, None), P(S, None, D, T, None)
    weights = (
        vec, rows, rows, rows, vec, vec, cols, vec, tall, flat, vec, vec, rows, rows, cols, vec, tall, flat, vec,
    )
    return jax.shard_map(
        body,
        mesh=mesh,
        in_specs=(seq, out, P(None, D), seq, *weights),
        out_specs=(out, out, out, *weights),
        check_vma=False,
    )
```
